512 devices in a mesh: group: 16 (over y, core), mp: 32 (over z, x).
Axes of the slice: x: 4, y: 8, z: 8, core: 2. Of those that a mesh axis runs over, the one named last changes fastest.
Arguments:
- resident_state: float32 [256, 16, 16384], P('group', None, 'mp'), may hold values from -4 to 4
- resident_conv: bfloat16 [256, 3, 16384], P('group', None, 'mp'), may hold values from -6 to 6
- migrate_from: int32 [256], P('group'), may hold values from 0 to 255, as said below
- decode_inputs: bfloat16 [256, 4, 16384], P('group', None, 'mp'), may hold values from -6 to 6
- decode_gates: bfloat16 [256, 4, 16384], P('group', None, 'mp'), may hold values from -6 to 6
- prompt_inputs: bfloat16 [128, 16, 16384], P('group', None, 'mp'), may hold values from -6 to 6
- prompt_gates: bfloat16 [128, 16, 16384], P('group', None, 'mp'), may hold values from -6 to 6
- prompt_length: int32 [128], P('group'), may hold values from 1 to 16, as said below
- prompt_dest: int32 [128, 1], P('group'), may hold values from 0 to 15; in each aligned block of 8 rows (0 to 7, 8 to 15, ...) at most 2 rows name the same one
- conv_weight: float32 [4, 16384], P(None, 'mp'), may hold values from -3 to 3
- conv_bias: float32 [16384], P('mp'), may hold values from -3 to 3
- rank_weight: bfloat16 [16384, 512], P('mp'), may hold values from -0.046875 to 0.046875
- select_weight: bfloat16 [16384, 32], P('mp'), may hold values from -0.09375 to 0.09375
- step_weight: bfloat16 [512, 16384], P(None, 'mp'), may hold values from -0.25 to 0.25
- step_bias: float32 [16384], P('mp'), may hold values from -4 to -1
- decay_log: float32 [16, 16384], P(None, 'mp'), may hold values from 0 to 3
- skip_gain: float32 [16384], P('mp'), may hold values from 0.5 to 1.5
Outputs:
- decode_out: bfloat16 [256, 4, 16384], P('group', None, 'mp')
- final_state: float32 [256, 16, 16384], P('group', None, 'mp')
- final_conv: bfloat16 [256, 3, 16384], P('group', None, 'mp')
- prefill_out: bfloat16 [128, 16, 16384], P('group', None, 'mp')
- prompt_state: float32 [512, 16, 16384], P('group', None, 'mp')
- prompt_conv: bfloat16 [512, 3, 16384], P('group', None, 'mp')
The draws below stay inside these ranges and needn't reach their ends.
Inputs may be any that keep to these rules, and one draw needn't show every extreme that they name: `migrate_from`: A permutation of the 256 requests over the 256 slots; slot s of group q is entry q * 16 + s. In every group exactly 4 slots hold a request other than their own, and exactly 4 of its requests leave their slots. `prompt_length`: every group holds a prompt of length 16. `prompt_dest`: of the 8 prompts of one group, at most 2 go to one destination.
All inputs are finite; a program needn't handle non-finite values.
Results may differ from the reference program's by a relative error of at most 0.0085.
Values may be sent and summed in bfloat16 or wider, within the bound.
No kernel may reach another device: no remote copies, remote signals or barrier semaphores. Data moves between devices by JAX's collectives and lax.ppermute only.
A program may use at most 64 MiB of HBM per device.

```python
import math
import jax
import jax.numpy as jnp
import numpy as np
from jax import lax

INNER = 16384
STATE = 16
CONV = 4
DT_RANK = 512
REQ_DEV = 16
PR_DEV = 8
MIG = 4
PAIR = 2
P_SIZE = 16
DEC = 4
REQS = 256
PROMPTS = 128
SLOTS = 512
N_GROUP = 16


def draw_migrate_from(key, part):
    key = jax.random.fold_in(key, 11)
    first_key, second_key = jax.random.split(key)
    group_keys = jax.random.split(first_key, N_GROUP)
    orders = jax.vmap(lambda one_key: jax.random.permutation(one_key, REQ_DEV))(group_keys)
    leaving = (orders[:, :MIG] + jnp.arange(N_GROUP, dtype=jnp.int32)[:, None] * REQ_DEV).reshape(-1).astype(jnp.int32)
    cycle = jax.random.permutation(second_key, N_GROUP * MIG)
    targets = leaving[cycle]
    sources = leaving[jnp.roll(cycle, -1)]
    return jnp.arange(REQS, dtype=jnp.int32).at[targets].set(sources)


def draw_prompt_length(key, part):
    key = jax.random.fold_in(key, 23)
    first_key, second_key = jax.random.split(key)
    lengths = jax.random.randint(first_key, (PROMPTS,), 1, P_SIZE + 1).astype(jnp.int32)
    chosen = jax.random.randint(second_key, (N_GROUP,), 0, PR_DEV).astype(jnp.int32)
    positions = jnp.arange(PROMPTS, dtype=jnp.int32)
    full_rows = positions % PR_DEV == chosen[positions // PR_DEV]
    return jnp.where(full_rows, P_SIZE, lengths).astype(jnp.int32)


def levels(stream_key, extent, cuts, least, largest):
    def one(axis_at, parts):
        draws = jax.random.uniform(jax.random.fold_in(jax.random.fold_in(stream_key, 6), axis_at), (parts,), jnp.float32, least / len(cuts), largest / len(cuts))
        return jnp.repeat(jnp.exp(draws), extent[axis_at] // parts).reshape((-1,) + (1,) * (len(extent) - axis_at - 1))

    loudness = one(*cuts[0])
    for cut in cuts[1:]:
        loudness = loudness * one(*cut)
    return loudness


def routed_block(rng, own, number, rows, amount, top, most, lean):
    sequence = jax.random.permutation(rng, amount)
    crowded, usual = load_shares(amount, rows * top, most, lean, True), load_shares(amount, rows * top, most, lean, False)
    places = jnp.arange(amount)

    def named(sizes, rotation):
        used = int((sizes > 0).sum())
        fixed = max(1, used // 4)
        shifted = fixed + (places - fixed + rotation * (used - fixed)) % max(1, amount - fixed)
        return jnp.zeros((amount,), jnp.int32).at[sequence[jnp.where(places < fixed, places, shifted)]].set(jnp.asarray(sizes, jnp.int32))

    sizes = jnp.where(number % 4 == 0, named(crowded, number // 4), named(usual, number - number // 4 - 1))
    mixed = jax.random.permutation(jax.random.fold_in(own, 3), amount)
    giver, sink = mixed[0:amount // 2 * 2:2], mixed[1:amount // 2 * 2:2]
    margin = jnp.minimum(sizes[giver] - 1, most - sizes[sink]) // 2
    margin = jnp.where((giver == sequence[0]) | (sink == sequence[0]) | (sizes[sink] == 0), 0, jnp.maximum(margin, 0))
    shifted = jax.random.randint(jax.random.fold_in(own, 4), (amount // 2,), 0, 1 << 20) % (margin + 1)
    sizes = sizes.at[giver].add(-shifted).at[sink].add(shifted)
    members = jnp.searchsorted(jnp.cumsum(sizes), jnp.arange(rows * top), side="right").astype(jnp.int32)
    table = members.reshape(top, rows).T
    table = table[jax.random.permutation(jax.random.fold_in(own, 1), rows)]
    rotation = jax.random.randint(jax.random.fold_in(own, 2), (rows, 1), 0, top)
    return jnp.take_along_axis(table, (jnp.arange(top)[None, :] + rotation) % top, axis=1)


def load_shares(amount, total, most, lean, full):
    weights = [(1 << 20) // math.isqrt(rank ** lean) + 1 for rank in range(1, amount + 1)]
    largest = most if full else min(most, max(-(-total // amount), total * weights[0] // sum(weights)))
    least = 1 if total - largest >= amount - 1 else 0
    given, rest = [largest] + [least] * (amount - 1), total - largest - least * (amount - 1)
    while rest > 0:
        candidates = [i for i in range(1, amount) if given[i] < largest] or [i for i in range(1, amount) if given[i] < most]
        mass, budget = sum([weights[i] for i in candidates]), rest
        for i in candidates:
            extra = min(most - given[i], max(1, budget * weights[i] // mass), rest)
            given[i] = given[i] + extra
            rest = rest - extra
    return np.array(given)


def normal_values(stream_key, dims, scale, most, cuts=(), kind=jnp.bfloat16):
    values = scale * jax.random.normal(stream_key, dims, jnp.float32)
    if cuts:
        values = values * levels(stream_key, dims, cuts, -0.22, 0.18)
    return jnp.clip(values, -most, most).astype(kind)


def setup_inputs(seed: int = 0) -> dict:
    key_list = jax.random.split(jax.random.key(seed), 18)
    resident_state = normal_values(key_list[0], (REQS, STATE, INNER), 0.5, 4.0, ((0, 16), (2, 32)), jnp.float32)
    resident_conv = normal_values(key_list[1], (REQS, CONV - 1, INNER), 1.0, 6.0, ((0, 16), (2, 32)))
    migrate_from = draw_migrate_from(jax.random.fold_in(key_list[17], 71), 0)
    decode_inputs = normal_values(key_list[3], (REQS, DEC, INNER), 1.0, 6.0, ((0, 16), (2, 32)))
    decode_gates = normal_values(key_list[4], (REQS, DEC, INNER), 1.0, 6.0, ((0, 16), (2, 32)))
    prompt_inputs = normal_values(key_list[5], (PROMPTS, P_SIZE, INNER), 1.0, 6.0, ((0, 16), (2, 32)))
    prompt_gates = normal_values(key_list[6], (PROMPTS, P_SIZE, INNER), 1.0, 6.0, ((0, 16), (2, 32)))
    prompt_length = draw_prompt_length(jax.random.fold_in(key_list[17], 71), 0)
    prompt_dest_keys = jax.random.split(jax.random.fold_in(key_list[8], 1), PROMPTS // PR_DEV)
    prompt_dest_turns = jax.random.permutation(jax.random.fold_in(key_list[8], 3), PROMPTS // PR_DEV)
    prompt_dest = jax.vmap(lambda own, number: routed_block(jax.random.fold_in(key_list[8], 2), own, number, PR_DEV, N_GROUP, 1, PAIR, 2))(prompt_dest_keys, prompt_dest_turns).reshape((PROMPTS, 1))
    conv_weight = normal_values(key_list[9], (CONV, INNER), CONV ** -0.5, 3.0, ((1, 32),), jnp.float32)
    conv_bias = normal_values(key_list[10], (INNER,), 0.5, 3.0, ((0, 32),), jnp.float32)
    rank_weight = normal_values(key_list[11], (INNER, DT_RANK), INNER ** -0.5, 0.046875, ((0, 32),))
    select_weight = normal_values(key_list[12], (INNER, 2 * STATE), (INNER // 4) ** -0.5, 0.09375, ((0, 32),))
    step_weight = normal_values(key_list[13], (DT_RANK, INNER), DT_RANK ** -0.5, 0.25, ((1, 32),))
    step_bias = jnp.clip(-4.0 + 3.0 * jax.random.uniform(key_list[14], (INNER,), jnp.float32) ** levels(key_list[14], (INNER,), ((0, 32),), -0.2, 0.2), -4.0, -1.0)
    decay_log = jnp.clip(3.0 * jax.random.uniform(key_list[15], (STATE, INNER), jnp.float32) ** levels(key_list[15], (STATE, INNER), ((1, 32),), -0.2, 0.2), 0.0, 3.0)
    skip_gain = jnp.clip(0.5 + 1.0 * jax.random.uniform(key_list[16], (INNER,), jnp.float32) ** levels(key_list[16], (INNER,), ((0, 32),), -0.2, 0.2), 0.5, 1.5)
    return {"resident_state": resident_state, "resident_conv": resident_conv, "migrate_from": migrate_from, "decode_inputs": decode_inputs, "decode_gates": decode_gates, "prompt_inputs": prompt_inputs, "prompt_gates": prompt_gates, "prompt_length": prompt_length, "prompt_dest": prompt_dest, "conv_weight": conv_weight, "conv_bias": conv_bias, "rank_weight": rank_weight, "select_weight": select_weight, "step_weight": step_weight, "step_bias": step_bias, "decay_log": decay_log, "skip_gain": skip_gain}


EPS = 1e-06

def local_features(inputs, history, conv_weight, conv_bias, rank_weight, select_weight):
    steps_count = inputs.shape[1]
    history_len = history.shape[1]
    padded = jnp.concatenate([history.astype(jnp.float32), inputs.astype(jnp.float32)], axis=1)
    conv_sum = conv_bias
    for offset in range(history_len + 1):
        conv_sum = conv_sum + conv_weight[offset] * padded[:, offset:offset + steps_count]
    conved = jax.nn.silu(conv_sum).astype(jnp.bfloat16)
    flat_rows = conved.reshape(-1, conved.shape[2])
    low_rank = jnp.dot(flat_rows, rank_weight, preferred_element_type=jnp.float32)
    selects = jnp.dot(flat_rows, select_weight, preferred_element_type=jnp.float32)
    return (padded, conved, low_rank, selects)

def step_sizes(low_rank, step_weight, step_bias, lengths, shape):
    normed = (low_rank * lax.rsqrt(lax.optimization_barrier(jnp.mean(low_rank * low_rank, axis=-1, keepdims=True)) + EPS)).astype(jnp.bfloat16)
    step_size = jax.nn.softplus(jnp.dot(normed, step_weight, preferred_element_type=jnp.float32) + step_bias)
    step_size = step_size.reshape(shape)
    live_rows = jnp.arange(shape[1], dtype=jnp.int32)[None, :] < lengths[:, None]
    step_size = jnp.where(live_rows[:, :, None], step_size, 0.0)
    return (step_size, live_rows)

def mixer(inputs, gate_rows, history, start_state, lengths, params):
    conv_weight, conv_bias, rank_weight, select_weight, step_weight, step_bias, decay_log, skip_gain = params
    padded, conved, low_rank, selects = local_features(inputs, history, conv_weight, conv_bias, rank_weight, select_weight)
    item_count, steps_count, channels = conved.shape
    step_size, live_rows = step_sizes(low_rank, step_weight, step_bias, lengths, conved.shape)
    states = selects.shape[1] // 2
    b_rows = selects[:, :states].reshape(item_count, steps_count, states)
    c_rows = selects[:, states:].reshape(item_count, steps_count, states)
    decay_rate = -jnp.exp(decay_log)

    def one_request(block_items):
        first_state, step_item, conv_item, b_item, c_item, gate_item, live_item = block_items

        def advance(carried, position):
            step_t, conv_t, b_t, c_t, gate_t, live_t = position
            conv_f = conv_t.astype(jnp.float32)
            carried = jnp.exp(step_t[None, :] * decay_rate) * carried + (step_t * conv_f)[None, :] * b_t[:, None]
            values_out = lax.optimization_barrier(jnp.sum(c_t[:, None] * carried, axis=0)) + skip_gain * conv_f
            result = jnp.where(live_t, values_out * jax.nn.silu(gate_t.astype(jnp.float32)), 0.0).astype(jnp.bfloat16)
            return (carried, result)
        last_state, outputs = lax.scan(advance, first_state, (step_item, conv_item, b_item, c_item, gate_item, live_item))
        return (outputs, last_state)
    outputs, finals = lax.map(one_request, (start_state, step_size, conved, b_rows, c_rows, gate_rows, live_rows))
    history_len = history.shape[1]
    tail_rows = jax.vmap(lambda row, count: lax.dynamic_slice_in_dim(row, count.astype(jnp.int32), history_len, 0))(padded, lengths)
    return (outputs, finals, tail_rows.astype(jnp.bfloat16))

def reference(resident_state, resident_conv, migrate_from, decode_inputs, decode_gates, prompt_inputs, prompt_gates, prompt_length, prompt_dest, conv_weight, conv_bias, rank_weight, select_weight, step_weight, step_bias, decay_log, skip_gain):
    params = (conv_weight, conv_bias, rank_weight, select_weight, step_weight, step_bias, decay_log, skip_gain)
    moved_state = resident_state[migrate_from]
    moved_conv = resident_conv[migrate_from]
    decode_lengths = jnp.full((REQS,), DEC, jnp.int32)
    decode_out, final_state, final_conv = mixer(decode_inputs, decode_gates, moved_conv, moved_state, decode_lengths, params)
    empty_conv = jnp.zeros((PROMPTS, CONV - 1, INNER), jnp.bfloat16)
    empty_state = jnp.zeros((PROMPTS, STATE, INNER), jnp.float32)
    prefill_out, prompt_final, prompt_tail = mixer(prompt_inputs, prompt_gates, empty_conv, empty_state, prompt_length, params)
    destination = prompt_dest[:, 0]
    dest_hot = (destination[:, None] == jnp.arange(N_GROUP, dtype=jnp.int32)[None, :]).astype(jnp.int32)
    dest_hot = dest_hot.reshape(N_GROUP, PR_DEV, N_GROUP)
    earlier = jnp.cumsum(dest_hot, axis=1) - dest_hot
    rank_in = lax.optimization_barrier(jnp.sum(earlier * dest_hot, axis=2)).reshape(-1)
    anchor = jnp.arange(PROMPTS, dtype=jnp.int32) // PR_DEV
    slot = destination * (N_GROUP * PAIR) + anchor * PAIR + rank_in
    prompt_state = jnp.zeros((SLOTS, STATE, INNER), jnp.float32).at[slot].set(prompt_final)
    prompt_conv = jnp.zeros((SLOTS, CONV - 1, INNER), jnp.bfloat16).at[slot].set(prompt_tail)
    return (decode_out, final_state, final_conv, prefill_out, prompt_state, prompt_conv)
```

```python
import jax
import jax.numpy as jnp
from jax import lax
from jax.experimental import pallas as pl
from jax.experimental.pallas import tpu as pltpu
from jax.sharding import PartitionSpec as P

MIG = 4
PAIR = 2
EPS = 1e-06
LANES = 128
ROWS0 = 24
LOG2E = 1.4426950408889634

F32 = jnp.float32
BF16 = jnp.bfloat16
VMEM = pl.BlockSpec(memory_space=pltpu.VMEM)
SMEM = pl.BlockSpec(memory_space=pltpu.SMEM)
PARAMS = pltpu.CompilerParams(vmem_limit_bytes=40 * 1024 * 1024)


def silu(x):
    return x / (1.0 + jnp.exp(-x))


def softplus(x):
    return jnp.maximum(x, 0.0) + jnp.log1p(jnp.exp(-jnp.abs(x)))


def iota(shape, dim):
    return lax.broadcasted_iota(jnp.int32, shape, dim)


def from_scalars(ref, count, shape):
    rows = iota(shape, 0)
    out = jnp.zeros(shape, jnp.int32)
    for i in range(count):
        out = jnp.where(rows == i, ref[i], out)
    return out


def slots_of(dest_ref, count):
    dests = [dest_ref[i, 0] for i in range(count)]
    ranks = []
    for i in range(count):
        rank = jnp.int32(0)
        for j in range(i):
            rank = rank + (dests[j] == dests[i]).astype(jnp.int32)
        ranks.append(rank)
    return dests, ranks


def pack_kernel(mig_ref, dest_ref, len_ref, conv_ref, state_ref, u_ref, pay_ref, state_out_ref, scr):
    groups = pay_ref.shape[0]
    reqs = conv_ref.shape[0]
    prompts, steps, channels = u_ref.shape
    own = lax.axis_index("group")
    count = jnp.int32(0)
    picks = [jnp.int32(0) for _ in range(MIG)]
    for r in range(reqs):
        moved = mig_ref[r] != own * reqs + r
        for k in range(MIG):
            picks[k] = jnp.where(moved & (count == k), r, picks[k])
        count = count + moved.astype(jnp.int32)
    base = scr.at[groups]
    base[...] = jnp.zeros(base.shape, F32)
    lane = iota((1, channels), 1) - own * ROWS0
    ids = jnp.zeros((1, channels), jnp.int32)
    code = jnp.zeros((1, channels), jnp.int32)
    for k in range(MIG):
        state_out_ref[k] = state_ref[picks[k]].astype(BF16)
        hist = conv_ref[picks[k]].astype(F32)
        for j in range(3):
            base[4 * j + k : 4 * j + k + 1, :] = hist[j : j + 1, :]
            here = lane == 4 * j + k
            ids = jnp.where(here, own * reqs + picks[k], ids)
            code = jnp.where(here, j + 1, code)
    base[12:13, :] = ids.astype(F32)
    base[13:14, :] = code.astype(F32)
    for d in range(groups):
        scr[d] = base[...]
    dests, ranks = slots_of(dest_ref, prompts)
    rows = iota((steps, channels), 0)
    for i in range(prompts):
        u = u_ref[i].astype(F32)
        tails = [
            jnp.sum(jnp.where(rows == len_ref[i] - 3 + j, u, 0.0), axis=0, keepdims=True)
            for j in range(3)
        ]
        for q in range(PAIR):

            @pl.when(ranks[i] == q)
            def _():
                for j in range(3):
                    at = 16 + 3 * q + j
                    scr[dests[i], at : at + 1, :] = tails[j]

    for d in range(groups):
        pay_ref[d] = scr[d].astype(BF16)


def put_lanes(ref, start, value):
    for l in range(ref.shape[0]):
        ref[l, start : start + value.shape[0], :] = value[:, l * LANES : (l + 1) * LANES]


def project(x, rank_ref, select_ref):
    low = jnp.dot(x, rank_ref[...], preferred_element_type=F32)
    sel = jnp.dot(x, select_ref[...], preferred_element_type=F32)
    return low, sel


def put_partials(pay_ref, first, low, sel):
    rank = low.shape[1]
    wide = jnp.concatenate(
        [sel, jnp.zeros((sel.shape[0], pay_ref.shape[2] - rank - sel.shape[1]), F32)], axis=1
    )
    for j in range(low.shape[0] // 8):
        pay_ref[first + j, :, :rank] = low[8 * j : 8 * j + 8].astype(BF16)
        pay_ref[first + j, :, rank:] = wide[8 * j : 8 * j + 8].astype(BF16)


def prompt_kernel(u_ref, cw_ref, cb_ref, rank_ref, select_ref, pay_ref, x_ref, scr, x_scr):
    prompts, steps, channels = u_ref.shape
    for i in range(prompts):
        put_lanes(scr, i * steps, u_ref[i].astype(F32))
    for l in range(channels // LANES):
        cols = slice(l * LANES, (l + 1) * LANES)
        taps = [cw_ref[k : k + 1, cols] for k in range(4)]
        bias = cb_ref[:, cols]
        window = [jnp.zeros((prompts, LANES), F32) for _ in range(3)]
        for t in range(steps):
            window.append(scr[l, pl.ds(t, prompts, stride=steps), :])
            acc = bias
            for k in range(4):
                acc = acc + taps[k] * window[t + k]
            x_scr[t * prompts : (t + 1) * prompts, cols] = silu(acc)
    x = x_scr[...].astype(BF16)
    x_ref[...] = x
    low, sel = project(x, rank_ref, select_ref)
    put_partials(pay_ref, 0, low, sel)


def decode_kernel(
    mig_ref, got_ref, conv_ref, u_ref, cw_ref, cb_ref, rank_ref, select_ref, prompt_pay_ref,
    pay_ref, x_ref, pos_ref, final_conv_ref, prompt_conv_ref, cand, scr, x_scr,
):
    groups = got_ref.shape[0]
    reqs, steps, channels = u_ref.shape
    own = lax.axis_index("group")
    ids = jnp.zeros((8, channels), F32)
    for s in range(groups):
        block = got_ref[s].astype(F32)
        cand[s * ROWS0 : (s + 1) * ROWS0, :] = block
        ids = ids + block[8:16]
        for q in range(PAIR):
            prompt_conv_ref[s * PAIR + q] = block[16 + 3 * q : 19 + 3 * q].astype(BF16)
    table = groups * ROWS0
    cand[table:, :] = jnp.zeros((channels - table, channels), F32)
    for r in range(reqs):
        cand[table + 8 * r : table + 8 * r + 3, :] = conv_ref[r].astype(F32)
        u = u_ref[r].astype(F32)
        put_lanes(scr, 8 * r, u)
        final_conv_ref[r] = u[1:4].astype(BF16)
    shape = (reqs, channels)
    lane = iota(shape, 1)
    row = iota(shape, 0)
    wanted = from_scalars(mig_ref, reqs, shape)
    moved = wanted != own * reqs + row
    codes = jnp.broadcast_to(ids[5:6], shape)
    found = moved & (jnp.broadcast_to(ids[4:5], shape) == wanted.astype(F32))
    pool = cand[...].astype(BF16)
    hist = []
    for j in range(3):
        hit = (found & (codes == j + 1.0)) | ((~moved) & (lane == table + 8 * row + j))
        hist.append(jnp.dot(hit.astype(BF16), pool, preferred_element_type=F32))
    first = jnp.where(found & (codes == 1.0), lane, 0)
    at = jnp.sum(first.astype(F32), axis=1, keepdims=True).astype(jnp.int32)
    pos_ref[...] = jnp.broadcast_to(jnp.where(moved[:, :1], at, -1), pos_ref.shape)
    for l in range(channels // LANES):
        cols = slice(l * LANES, (l + 1) * LANES)
        taps = [cw_ref[k : k + 1, cols] for k in range(4)]
        bias = cb_ref[:, cols]
        window = [hist[j][:, cols] for j in range(3)]
        for t in range(steps):
            window.append(scr[l, pl.ds(t, reqs, stride=8), :])
            acc = bias
            for k in range(4):
                acc = acc + taps[k] * window[t + k]
            x_scr[t * reqs : (t + 1) * reqs, cols] = silu(acc)
    x = x_scr[...].astype(BF16)
    x_ref[...] = x
    low, sel = project(x, rank_ref, select_ref)
    first_block = prompt_pay_ref.shape[0]
    pay_ref[:first_block] = prompt_pay_ref[...]
    put_partials(pay_ref, first_block, low, sel)
    used = first_block + x.shape[0] // 8
    pay_ref[used:] = jnp.zeros((pay_ref.shape[0] - used,) + pay_ref.shape[1:], BF16)


def norm_kernel(part_ref, out_ref):
    blocks, rows, width = part_ref.shape
    total = part_ref[0].astype(F32)
    for j in range(1, blocks):
        total = total + part_ref[j].astype(F32)
    rank = (width // LANES - 1) * LANES
    low = total[:, :rank]
    normed = low * lax.rsqrt(jnp.mean(low * low, axis=-1, keepdims=True) + EPS)
    for j in range(blocks):
        out_ref[j, :, :rank] = normed.astype(BF16)
        out_ref[j, :, rank:] = total[:, rank:].astype(BF16)


def steps_of(rows_ref, step_w_ref, step_b_ref, low_scr, step_scr):
    for j in range(low_scr.shape[0] // 8):
        low_scr[8 * j : 8 * j + 8, :] = rows_ref[j].astype(F32)
    rank = step_w_ref.shape[0]
    normed = low_scr[:, :rank].astype(BF16)
    step_scr[...] = softplus(
        jnp.dot(normed, step_w_ref[...], preferred_element_type=F32) + step_b_ref[...]
    )
    return rank


def scan(
    t, items, live, x, gate_scr, gate_stride, low_scr, step_scr, rank, decay_scr, skip_ref, h_scr,
    y_scr, y_stride,
):
    states = decay_scr.shape[1] // 8
    start = pl.multiple_of(t * items, 8)
    for g in range(items // 8):
        rows = pl.ds(start + 8 * g, 8)
        alive = None if live is None else live[8 * g : 8 * g + 8]
        sel = low_scr[rows, rank:]
        lanes = range(h_scr.shape[0])
        step, drive, conved, y = [], [], [], []
        for l in lanes:
            cols = slice(l * LANES, (l + 1) * LANES)
            step_l = step_scr[rows, cols]
            if alive is not None:
                step_l = jnp.where(alive, step_l, 0.0)
            conved_l = x[rows, cols]
            step.append(step_l)
            conved.append(conved_l)
            drive.append(step_l * conved_l)
            y.append(skip_ref[:, cols] * conved_l)
        for n in range(states):
            b = jnp.broadcast_to(sel[:, n : n + 1], (8, LANES))
            c = jnp.broadcast_to(sel[:, states + n : states + n + 1], (8, LANES))
            at = slice(n * items + 8 * g, n * items + 8 * g + 8)
            for l in lanes:
                keep = jnp.exp2(step[l] * decay_scr[l, 8 * n : 8 * n + 8, :])
                h = keep * h_scr[l, at, :] + drive[l] * b
                h_scr[l, at, :] = h
                y[l] = y[l] + c * h
        for l in lanes:
            gate = gate_scr[l, pl.ds(8 * g * gate_stride + t, 8, stride=gate_stride), :]
            out = y[l] * silu(gate)
            if alive is not None:
                out = jnp.where(alive, out, 0.0)
            y_scr[l, pl.ds(8 * g * y_stride + t, 8, stride=y_stride), :] = out


def put_decay(decay_ref, decay_scr):
    decay = jnp.exp(decay_ref[...]) * -LOG2E
    for n in range(decay.shape[0]):
        put_lanes(decay_scr, 8 * n, jnp.broadcast_to(decay[n : n + 1], (8, decay.shape[1])))


def prefill_kernel(
    len_ref, dest_ref, rows_ref, x_ref, gate_ref, step_w_ref, step_b_ref, decay_ref, skip_ref,
    out_ref, pay_ref, low_scr, step_scr, x_scr, gate_scr, decay_scr, h_scr, y_scr,
):
    prompts, steps, channels = gate_ref.shape
    states = decay_ref.shape[0]
    rank = steps_of(rows_ref, step_w_ref, step_b_ref, low_scr, step_scr)
    x_scr[...] = x_ref[...].astype(F32)
    for i in range(prompts):
        put_lanes(gate_scr, i * steps, gate_ref[i].astype(F32))
    put_decay(decay_ref, decay_scr)
    h_scr[...] = jnp.zeros(h_scr.shape, F32)
    lengths = from_scalars(len_ref, prompts, (prompts, LANES))

    @pl.loop(0, steps)
    def _(t):
        scan(
            t, prompts, t < lengths, x_scr, gate_scr, steps, low_scr, step_scr, rank, decay_scr,
            skip_ref, h_scr, y_scr, steps,
        )

    dests, ranks = slots_of(dest_ref, prompts)
    pay_ref[...] = jnp.zeros(pay_ref.shape, BF16)
    for i in range(prompts):
        for l in range(channels // LANES):
            cols = slice(l * LANES, (l + 1) * LANES)
            out_ref[i, :, cols] = y_scr[l, i * steps : (i + 1) * steps, :].astype(BF16)
            final = h_scr[l, pl.ds(i, states, stride=prompts), :]
            pay_ref[dests[i] * PAIR + ranks[i], :, cols] = final.astype(BF16)


def decode_scan_kernel(
    pos_ref, rows_ref, x_ref, gate_ref, state_ref, moved_ref, step_w_ref, step_b_ref, decay_ref,
    skip_ref, out_ref, final_ref, low_scr, step_scr, x_scr, gate_scr, decay_scr, h_scr, y_scr,
):
    reqs, steps, channels = gate_ref.shape
    states = decay_ref.shape[0]
    rank = steps_of(rows_ref, step_w_ref, step_b_ref, low_scr, step_scr)
    x_scr[...] = x_ref[...].astype(F32)
    put_decay(decay_ref, decay_scr)
    for r in range(reqs):
        put_lanes(gate_scr, 8 * r, gate_ref[r].astype(F32))
        code = pos_ref[r, 0]
        for l in range(channels // LANES):
            cols = slice(l * LANES, (l + 1) * LANES)

            @pl.when(code < 0)
            def _():
                h_scr[l, pl.ds(r, states, stride=reqs), :] = state_ref[r, :, cols]

            @pl.when(code >= 0)
            def _():
                source = lax.div(code, ROWS0)
                at = source * MIG + (code - source * ROWS0)
                h_scr[l, pl.ds(r, states, stride=reqs), :] = moved_ref[at, :, cols].astype(F32)

    @pl.loop(0, steps)
    def _(t):
        scan(
            t, reqs, None, x_scr, gate_scr, 8, low_scr, step_scr, rank, decay_scr, skip_ref,
            h_scr, y_scr, 8,
        )

    for r in range(reqs):
        for l in range(channels // LANES):
            cols = slice(l * LANES, (l + 1) * LANES)
            out_ref[r, :, cols] = y_scr[l, 8 * r : 8 * r + steps, :].astype(BF16)
            final_ref[r, :, cols] = h_scr[l, pl.ds(r, states, stride=reqs), :]


def exchange(value, axis):
    return lax.all_to_all(value, axis, split_axis=0, concat_axis=0, tiled=True)


def on_device(
    resident_state,
    resident_conv,
    migrate_from,
    decode_inputs,
    decode_gates,
    prompt_inputs,
    prompt_gates,
    prompt_length,
    prompt_dest,
    conv_weight,
    conv_bias,
    rank_weight,
    select_weight,
    step_weight,
    step_bias,
    decay_log,
    skip_gain,
):
    groups = lax.axis_size("group")
    peers = lax.axis_size("mp")
    reqs, states, channels = resident_state.shape
    prompts, steps, _ = prompt_inputs.shape
    decode_steps = decode_inputs.shape[1]
    tiles = channels // LANES
    rank = rank_weight.shape[1]
    width = rank + LANES
    prompt_rows = prompts * steps
    decode_rows = reqs * decode_steps
    bias_row = conv_bias.reshape(1, channels)
    step_bias_row = step_bias.reshape(1, channels)
    skip_row = skip_gain.reshape(1, channels)

    def struct(shape, dtype):
        return jax.ShapeDtypeStruct(shape, dtype)

    def scratch(shape):
        return pltpu.VMEM(shape, F32)

    send_conv, send_state = pl.pallas_call(
        pack_kernel,
        out_shape=(
            struct((groups, ROWS0, channels), BF16),
            struct((MIG, states, channels), BF16),
        ),
        in_specs=[SMEM] * 3 + [VMEM] * 3,
        out_specs=(VMEM, VMEM),
        scratch_shapes=[scratch((groups + 1, ROWS0, channels))],
        compiler_params=PARAMS,
        name="pack",
    )(migrate_from, prompt_dest, prompt_length, resident_conv, resident_state, prompt_inputs)
    got_conv = exchange(send_conv, "group")
    got_state = lax.all_gather(send_state, "group", axis=0, tiled=True)

    prompt_pay, prompt_x = pl.pallas_call(
        prompt_kernel,
        out_shape=(
            struct((prompt_rows // 8, 8, width), BF16),
            struct((prompt_rows, channels), BF16),
        ),
        in_specs=[VMEM] * 5,
        out_specs=(VMEM, VMEM),
        scratch_shapes=[scratch((tiles, prompt_rows, LANES)), scratch((prompt_rows, channels))],
        compiler_params=PARAMS,
        name="prompt_features",
    )(prompt_inputs, conv_weight, bias_row, rank_weight, select_weight)

    pay, decode_x, position, final_conv, prompt_conv = pl.pallas_call(
        decode_kernel,
        out_shape=(
            struct((peers, 8, width), BF16),
            struct((decode_rows, channels), BF16),
            struct((reqs, LANES), jnp.int32),
            struct(resident_conv.shape, BF16),
            struct((groups * PAIR, 3, channels), BF16),
        ),
        in_specs=[SMEM] + [VMEM] * 8,
        out_specs=(VMEM,) * 5,
        scratch_shapes=[
            scratch((channels, channels)),
            scratch((tiles, reqs * 8, LANES)),
            scratch((decode_rows, channels)),
        ],
        compiler_params=PARAMS,
        name="decode_features",
    )(
        migrate_from, got_conv, resident_conv, decode_inputs, conv_weight, bias_row, rank_weight,
        select_weight, prompt_pay,
    )

    parts = exchange(pay, "mp")
    shares = pl.pallas_call(
        norm_kernel,
        out_shape=struct((peers, 8, width), BF16),
        in_specs=[VMEM],
        out_specs=VMEM,
        compiler_params=PARAMS,
        name="sum_norm",
    )(parts)
    rows = exchange(shares, "mp")

    prompt_blocks = prompt_rows // 8
    decode_blocks = decode_rows // 8
    prefill_out, send_final = pl.pallas_call(
        prefill_kernel,
        out_shape=(
            struct(prompt_inputs.shape, BF16),
            struct((groups * PAIR, states, channels), BF16),
        ),
        grid=(1,),
        in_specs=[SMEM] * 2
        + [pl.BlockSpec((prompt_blocks, 8, width), lambda i: (0, 0, 0))]
        + [VMEM] * 6,
        out_specs=(VMEM, VMEM),
        scratch_shapes=[
            scratch((prompt_rows, width)),
            scratch((prompt_rows, channels)),
            scratch((prompt_rows, channels)),
            scratch((tiles, prompt_rows, LANES)),
            scratch((tiles, 8 * states, LANES)),
            scratch((tiles, prompts * states, LANES)),
            scratch((tiles, prompt_rows, LANES)),
        ],
        compiler_params=PARAMS,
        name="prefill_scan",
    )(
        prompt_length, prompt_dest, rows, prompt_x, prompt_gates, step_weight, step_bias_row,
        decay_log, skip_row,
    )
    got_final = exchange(send_final.reshape(groups, PAIR, states, channels), "group")

    first = prompt_blocks // decode_blocks
    decode_out, final_state = pl.pallas_call(
        decode_scan_kernel,
        out_shape=(struct(decode_inputs.shape, BF16), struct(resident_state.shape, F32)),
        grid=(1,),
        in_specs=[SMEM]
        + [pl.BlockSpec((decode_blocks, 8, width), lambda i: (first, 0, 0))]
        + [VMEM] * 8,
        out_specs=(VMEM, VMEM),
        scratch_shapes=[
            scratch((decode_rows, width)),
            scratch((decode_rows, channels)),
            scratch((decode_rows, channels)),
            scratch((tiles, reqs * 8, LANES)),
            scratch((tiles, 8 * states, LANES)),
            scratch((tiles, reqs * states, LANES)),
            scratch((tiles, reqs * 8, LANES)),
        ],
        compiler_params=PARAMS,
        name="decode_scan",
    )(
        position, rows, decode_x, decode_gates, resident_state, got_state, step_weight,
        step_bias_row, decay_log, skip_row,
    )
    prompt_state = got_final.astype(F32).reshape(groups * PAIR, states, channels)
    return (decode_out, final_state, final_conv, prefill_out, prompt_state, prompt_conv)


def solution(mesh):
    whole = P("group", None, "mp")
    return jax.shard_map(
        on_device,
        mesh=mesh,
        in_specs=(
            whole,
            whole,
            P("group"),
            whole,
            whole,
            whole,
            whole,
            P("group"),
            P("group", None),
            P(None, "mp"),
            P("mp"),
            P("mp", None),
            P("mp", None),
            P(None, "mp"),
            P("mp"),
            P(None, "mp"),
            P("mp"),
        ),
        out_specs=(whole,) * 6,
        check_vma=False,
    )
```

```python
import jax
import jax.numpy as jnp
from jax import lax
from jax.experimental import pallas as pl
from jax.experimental.pallas import tpu as pltpu
from jax.sharding import PartitionSpec as P

MIG = 4
PAIR = 2
EPS = 1e-06
LANES = 128
ROWS0 = 24
PROMPT_GROUPS = 16
STATE_ROW = 14
TAIL_ROW = 18
LOG2E = 1.4426950408889634

F32 = jnp.float32
BF16 = jnp.bfloat16
VMEM = pl.BlockSpec(memory_space=pltpu.VMEM)
SMEM = pl.BlockSpec(memory_space=pltpu.SMEM)
PARAMS = pltpu.CompilerParams(vmem_limit_bytes=40 * 1024 * 1024)
ALL_VMEM = pltpu.CompilerParams(vmem_limit_bytes=60 * 1024 * 1024)


def silu(x):
    return x / (1.0 + jnp.exp(-x))


def softplus(x):
    return jnp.maximum(x, 0.0) + jnp.log1p(jnp.exp(-jnp.abs(x)))


def iota(shape, dim):
    return lax.broadcasted_iota(jnp.int32, shape, dim)


def from_scalars(ref, count, shape):
    rows = iota(shape, 0)
    out = jnp.zeros(shape, jnp.int32)
    for i in range(count):
        out = jnp.where(rows == i, ref[i], out)
    return out


def slots_of(dest_ref, count):
    dests = [dest_ref[i] for i in range(count)]
    ranks = []
    for i in range(count):
        rank = jnp.int32(0)
        for j in range(i):
            rank = rank + (dests[j] == dests[i]).astype(jnp.int32)
        ranks.append(rank)
    return dests, ranks


def picks_of(mig_ref, reqs):
    own = lax.axis_index("group")
    count = jnp.int32(0)
    picks = [jnp.int32(0) for _ in range(MIG)]
    for r in range(reqs):
        moved = mig_ref[r] != own * reqs + r
        for k in range(MIG):
            picks[k] = jnp.where(moved & (count == k), r, picks[k])
        count = count + moved.astype(jnp.int32)
    return own, picks


def pack_kernel(
    mig_ref, dest_ref, len_ref, conv_ref, state_ref, u_ref, pay_ref, scr, conv_scr, u_scr, held, sems
):
    groups = pay_ref.shape[0]
    _, reqs, channels = conv_ref.shape
    prompts, steps, _ = u_ref.shape
    states = state_ref.shape[1]
    own, picks = picks_of(mig_ref, reqs)
    copies = [
        pltpu.make_async_copy(state_ref.at[picks[k]], held.at[k], sems.at[k]) for k in range(MIG)
    ]
    for copy in copies:
        copy.start()
    base = scr.at[groups]
    base[...] = jnp.zeros(base.shape, F32)
    lane = iota((1, channels), 1)
    ids = jnp.zeros((1, channels), jnp.int32)
    wanted = jnp.zeros((1, channels), jnp.int32)
    for j in range(3):
        conv_scr[j * reqs : (j + 1) * reqs, :] = conv_ref[j].astype(F32)
    for k in range(MIG):
        for at in (k, 4 + k, 8 + k, STATE_ROW + k):
            ids = jnp.where(lane == own * ROWS0 + at, own * reqs + picks[k], ids)
        wanted = jnp.where(lane == own * MIG + k, mig_ref[picks[k]], wanted)
        for j in range(3):
            at = 4 * j + k
            base[at : at + 1, :] = conv_scr[pl.ds(j * reqs + picks[k], 1), :]
    base[12:13, :] = ids.astype(F32)
    base[13:14, :] = wanted.astype(F32)
    for d in range(groups):
        scr[d] = base[...]
    dests, ranks = slots_of(dest_ref, prompts)
    pad = u_scr.shape[0] // prompts
    for i in range(prompts):
        u_scr[i * pad : i * pad + 8, :] = jnp.zeros((8, channels), F32)
        u_scr[i * pad + 8 : i * pad + 8 + steps, :] = u_ref[i].astype(F32)
    for i in range(prompts):
        tails = [u_scr[pl.ds(i * pad + 5 + j + len_ref[i], 1), :] for j in range(3)]
        for q in range(PAIR):

            @pl.when(ranks[i] == q)
            def _():
                for j in range(3):
                    at = TAIL_ROW + 3 * q + j
                    scr[dests[i], at : at + 1, :] = tails[j]

    for copy in copies:
        copy.wait()
    for k in range(MIG):
        for n in range(states):
            scr[n, STATE_ROW + k : STATE_ROW + k + 1, :] = held[k, n : n + 1, :]
    for d in range(groups):
        pay_ref[d] = scr[d].astype(BF16)


def put_lanes(ref, start, value):
    for l in range(ref.shape[0]):
        ref[l, start : start + value.shape[0], :] = value[:, l * LANES : (l + 1) * LANES]


def project(x, rank_ref, select_ref):
    low = jnp.dot(x, rank_ref[...], preferred_element_type=F32)
    sel = lax.dot_general(
        x, select_ref[...], (((1,), (1,)), ((), ())), preferred_element_type=F32
    )
    return low, sel


def put_tiles(scr, first, low, sel):
    tiles = low.shape[1] // LANES
    width = sel.shape[1]
    share = LANES // width
    for g in range(low.shape[0] // 8):
        rows = slice(8 * g, 8 * g + 8)
        for l in range(tiles):
            owner, place = divmod((first + g) * tiles + l, 3)
            scr[owner, 8 * place : 8 * place + 8, :] = low[rows, l * LANES : (l + 1) * LANES]
        owner, place = divmod(first + g, share)
        scr[owner, 24:32, place * width : (place + 1) * width] = sel[rows]


def take_tiles(rows_ref, first, low_scr, sel_scr):
    count, channels = low_scr.shape
    tiles = channels // LANES
    for g in range(count // 8):
        rows = slice(8 * g, 8 * g + 8)
        for l in range(tiles):
            owner, place = divmod((first + g) * tiles + l, 3)
            low_scr[rows, l * LANES : (l + 1) * LANES] = rows_ref[owner].astype(F32)[
                8 * place : 8 * place + 8
            ]
        owner, place = divmod(first + g, 4)
        pair = rows_ref[owner].astype(F32)[24:32]
        sel_scr[rows, :] = pltpu.roll(pair, (LANES - 32 * place) % LANES, 1) if place else pair


def prompt_kernel(
    u_ref, cw_ref, cb_ref, rank_ref, select_ref, low_ref, sel_ref, x_ref, scr, x_scr
):
    prompts, steps, channels = u_ref.shape
    for i in range(prompts):
        put_lanes(scr, i * steps, u_ref[i].astype(F32))
    for l in range(channels // LANES):
        cols = slice(l * LANES, (l + 1) * LANES)
        taps = [cw_ref[k : k + 1, cols] for k in range(4)]
        bias = cb_ref[:, cols]
        window = [jnp.zeros((prompts, LANES), F32) for _ in range(3)]
        for t in range(steps):
            window.append(scr[l, pl.ds(t, prompts, stride=steps), :])
            acc = bias
            for k in range(4):
                acc = acc + taps[k] * window[t + k]
            x_scr[t * prompts : (t + 1) * prompts, cols] = silu(acc)
    x = x_scr[...].astype(BF16)
    x_ref[...] = x
    low, sel = project(x, rank_ref, select_ref)
    low_ref[...] = low
    sel_ref[...] = sel


def decode_kernel(
    mig_ref, got_ref, conv_ref, u_ref, cw_ref, cb_ref, rank_ref, select_ref, prompt_low_ref,
    prompt_sel_ref, pay_ref, x_ref, pass_ref, final_conv_ref, prompt_conv_ref, pool_scr, pay_scr,
    scr, x_scr,
):
    groups = got_ref.shape[0]
    reqs, steps, channels = u_ref.shape
    table = groups * ROWS0
    own = lax.axis_index("group")
    marks = jnp.zeros((8, channels), F32)
    for s in range(groups):
        block = got_ref[s].astype(F32)
        pool_scr[s * ROWS0 : (s + 1) * ROWS0, :] = block
        marks = marks + block[8:16]
        for q in range(PAIR):
            for j in range(3):
                at = TAIL_ROW + 3 * q + j
                prompt_conv_ref[j, s * PAIR + q : s * PAIR + q + 1, :] = block[at : at + 1]
    for r in range(reqs):
        put_lanes(scr, 8 * r, u_ref[r].astype(F32))
    pool = pool_scr[...].astype(BF16)
    ids = marks[4:5, :table]
    place = lax.rem(iota((1, table), 1), ROWS0)
    moves = groups * MIG
    square = (moves, LANES)
    wanted = jnp.sum(
        jnp.where(
            iota(square, 0) == iota(square, 1), jnp.broadcast_to(marks[5:6, :LANES], square), 0.0
        ),
        axis=1,
        keepdims=True,
    )
    passed = (wanted == ids) & (place >= STATE_ROW) & (place < STATE_ROW + MIG)
    relay = jnp.dot(jnp.where(passed, 1.0, 0.0).astype(BF16), pool, preferred_element_type=F32)
    for d in range(groups):
        own_rows = relay[d * MIG : (d + 1) * MIG]
        pass_ref[d] = jnp.concatenate([own_rows, own_rows], axis=0).astype(BF16)
    wide = (reqs, channels)
    moved_wide = from_scalars(mig_ref, reqs, wide) != own * reqs + iota(wide, 0)
    shape = (reqs, table)
    needs = from_scalars(mig_ref, reqs, shape)
    found = (needs != own * reqs + iota(shape, 0)) & (
        jnp.broadcast_to(ids, shape) == needs.astype(F32)
    )
    hist = []
    for j in range(3):
        hit = jnp.where(found & (place >= 4 * j) & (place < 4 * j + 4), 1.0, 0.0).astype(BF16)
        taken = jnp.dot(hit, pool, preferred_element_type=F32)
        hist.append(jnp.where(moved_wide, taken, conv_ref[j].astype(F32)))
    for l in range(channels // LANES):
        cols = slice(l * LANES, (l + 1) * LANES)
        taps = [cw_ref[k : k + 1, cols] for k in range(4)]
        bias = cb_ref[:, cols]
        window = [hist[j][:, cols] for j in range(3)]
        for t in range(steps):
            window.append(scr[l, pl.ds(t, reqs, stride=8), :])
            acc = bias
            for k in range(4):
                acc = acc + taps[k] * window[t + k]
            x_scr[t * reqs : (t + 1) * reqs, cols] = silu(acc)
        for j in range(3):
            final_conv_ref[j, :, cols] = window[steps + j].astype(BF16)
    x = x_scr[...].astype(BF16)
    x_ref[...] = x
    low, sel = project(x, rank_ref, select_ref)
    prompt_groups = prompt_low_ref.shape[0] // 8
    pay_scr[...] = jnp.zeros(pay_scr.shape, F32)
    put_tiles(pay_scr, 0, prompt_low_ref[...], prompt_sel_ref[...])
    put_tiles(pay_scr, prompt_groups, low, sel)
    pay_ref[...] = pay_scr[...].astype(BF16)


def sum_kernel(got_ref, out_ref):
    total = got_ref[0].astype(F32)
    for j in range(1, got_ref.shape[0]):
        total = total + got_ref[j].astype(F32)
    own_rows = total.astype(BF16)
    for j in range(out_ref.shape[0]):
        out_ref[j] = own_rows


def steps_of(low_scr, step_w_ref, step_b):
    low = low_scr[...]
    scale = lax.rsqrt(jnp.mean(low * low, axis=-1, keepdims=True) + EPS)
    raw = jnp.dot(low.astype(BF16), step_w_ref[...], preferred_element_type=F32)
    return softplus(raw * scale + step_b)


def scan(t, items, live, x, gate, sel, step, decay, skip, h_scr, y_scr, y_stride):
    states = decay.shape[1] // 8
    for g in range(items // 8):
        rows = slice(t * items + 8 * g, t * items + 8 * g + 8)
        alive = None if live is None else live[8 * g : 8 * g + 8]
        pair = sel[rows, :]
        lanes = range(h_scr.shape[0])
        steps, drive, y = [], [], []
        for l in lanes:
            cols = slice(l * LANES, (l + 1) * LANES)
            step_l = step[rows, cols]
            if alive is not None:
                step_l = jnp.where(alive, step_l, 0.0)
            x_l = x[rows, cols]
            steps.append(step_l)
            drive.append(step_l * x_l)
            y.append(skip[:, cols] * x_l)
        for n in range(states):
            b = jnp.broadcast_to(pair[:, n : n + 1], (8, LANES))
            c = jnp.broadcast_to(pair[:, states + n : states + n + 1], (8, LANES))
            at = slice(n * items + 8 * g, n * items + 8 * g + 8)
            for l in lanes:
                keep = jnp.exp2(steps[l] * decay[l, 8 * n : 8 * n + 8, :])
                h = keep * h_scr[l, at, :] + drive[l] * b
                h_scr[l, at, :] = h
                y[l] = y[l] + c * h
        for l in lanes:
            cols = slice(l * LANES, (l + 1) * LANES)
            out = y[l] * gate[rows, cols]
            if alive is not None:
                out = jnp.where(alive, out, 0.0)
            y_scr[l, pl.ds(8 * g * y_stride + t, 8, stride=y_stride), :] = out


def prompt_prepare_kernel(
    gate_ref, decay_ref, step_b_ref, skip_ref, gate_out_ref, decay_out_ref, rows_out_ref, scr
):
    prompts, steps, channels = gate_ref.shape
    rows_out_ref[0:1, :] = step_b_ref[...]
    rows_out_ref[1:2, :] = skip_ref[...]
    decay = jnp.exp(decay_ref[...]) * -LOG2E
    for n in range(decay.shape[0]):
        put_lanes(decay_out_ref, 8 * n, jnp.broadcast_to(decay[n : n + 1], (8, channels)))
    for i in range(prompts):
        put_lanes(scr, i * steps, silu(gate_ref[i].astype(F32)))
    for l in range(channels // LANES):
        cols = slice(l * LANES, (l + 1) * LANES)
        for t in range(steps):
            gate_out_ref[t * prompts : (t + 1) * prompts, cols] = scr[
                l, pl.ds(t, prompts, stride=steps), :
            ]


def prefill_kernel(
    len_ref, dest_ref, rows_ref, x_ref, gate_ref, step_w_ref, decay_ref, extra_ref, relay_ref,
    out_ref, pay_ref, low_scr, sel_scr, step_scr, x_scr, h_scr, y_scr,
):
    prompts, steps, channels = out_ref.shape
    states = decay_ref.shape[1] // 8
    take_tiles(rows_ref, 0, low_scr, sel_scr)
    step_scr[...] = steps_of(low_scr, step_w_ref, extra_ref[0:1, :])
    x_scr[...] = x_ref[...].astype(F32)
    h_scr[...] = jnp.zeros(h_scr.shape, F32)
    lengths = from_scalars(len_ref, prompts, (prompts, LANES))
    skip = extra_ref[1:2, :]
    for t in range(steps):
        scan(
            t, prompts, t < lengths, x_scr, gate_ref, sel_scr, step_scr, decay_ref, skip, h_scr,
            y_scr, steps,
        )
    dests, ranks = slots_of(dest_ref, prompts)
    groups = pay_ref.shape[0]
    slots = PAIR * states
    for d in range(groups):
        pay_ref[d, :slots, :] = jnp.zeros((slots, channels), BF16)
        pay_ref[d, slots:, :] = relay_ref[d]
    for i in range(prompts):
        final = []
        for l in range(channels // LANES):
            cols = slice(l * LANES, (l + 1) * LANES)
            out_ref[i, :, cols] = y_scr[l, i * steps : (i + 1) * steps, :].astype(BF16)
            final.append(h_scr[l, pl.ds(i, states, stride=prompts), :])
        for q in range(PAIR):

            @pl.when(ranks[i] == q)
            def _():
                for l in range(channels // LANES):
                    cols = slice(l * LANES, (l + 1) * LANES)
                    pay_ref[dests[i], q * states : (q + 1) * states, cols] = final[l].astype(BF16)


def decode_prepare_kernel(
    rows_ref, gate_ref, state_ref, step_w_ref, extra_ref, step_ref, sel_ref, gate_out_ref, h_ref,
    low_scr, scr,
):
    reqs, steps, channels = gate_ref.shape
    states = state_ref.shape[1]
    take_tiles(rows_ref, PROMPT_GROUPS, low_scr, sel_ref)
    step_ref[...] = steps_of(low_scr, step_w_ref, extra_ref[0:1, :])
    for r in range(reqs):
        put_lanes(scr, 8 * r, silu(gate_ref[r].astype(F32)))
        for l in range(channels // LANES):
            cols = slice(l * LANES, (l + 1) * LANES)
            h_ref[l, pl.ds(r, states, stride=reqs), :] = state_ref[r, :, cols]
    for l in range(channels // LANES):
        cols = slice(l * LANES, (l + 1) * LANES)
        for t in range(steps):
            gate_out_ref[t * reqs : (t + 1) * reqs, cols] = scr[l, pl.ds(t, reqs, stride=8), :]


def decode_scan_kernel(
    mig_ref, got_ref, x_ref, gate_ref, step_ref, sel_ref, decay_ref, extra_ref, h_ref, out_ref,
    final_ref, prompt_state_ref, x_scr, h_scr, y_scr, moved_scr,
):
    reqs, steps, channels = out_ref.shape
    groups = got_ref.shape[0]
    states = decay_ref.shape[1] // 8
    slots = PAIR * states
    x_scr[...] = x_ref[...].astype(F32)
    h_scr[...] = h_ref[...]
    for n in range(states):
        put_lanes(moved_scr, n * MIG, got_ref[n, slots:, :].astype(F32)[:MIG])
    _, picks = picks_of(mig_ref, reqs)
    for k in range(MIG):
        for l in range(channels // LANES):
            h_scr[l, pl.ds(picks[k], states, stride=reqs), :] = moved_scr[
                l, pl.ds(k, states, stride=MIG), :
            ]
    for s in range(groups):
        for q in range(PAIR):
            prompt_state_ref[s * PAIR + q] = got_ref[s, q * states : (q + 1) * states, :].astype(F32)

    skip = extra_ref[1:2, :]
    for t in range(steps):
        scan(t, reqs, None, x_scr, gate_ref, sel_ref, step_ref, decay_ref, skip, h_scr, y_scr, 8)

    for r in range(reqs):
        for l in range(channels // LANES):
            cols = slice(l * LANES, (l + 1) * LANES)
            out_ref[r, :, cols] = y_scr[l, 8 * r : 8 * r + steps, :].astype(BF16)
            final_ref[r, :, cols] = h_scr[l, pl.ds(r, states, stride=reqs), :]


def exchange(value, axis):
    return lax.all_to_all(value, axis, split_axis=0, concat_axis=0, tiled=True)


def on_device(
    resident_state,
    resident_conv,
    migrate_from,
    decode_inputs,
    decode_gates,
    prompt_inputs,
    prompt_gates,
    prompt_length,
    prompt_dest,
    conv_weight,
    conv_bias,
    rank_weight,
    select_weight,
    step_weight,
    step_bias,
    decay_log,
    skip_gain,
):
    groups = lax.axis_size("group")
    peers = lax.axis_size("mp")
    reqs, states, channels = resident_state.shape
    prompts, steps, _ = prompt_inputs.shape
    decode_steps = decode_inputs.shape[1]
    tiles = channels // LANES
    rank = rank_weight.shape[1]
    selects = select_weight.shape[1]
    prompt_rows = prompts * steps
    decode_rows = reqs * decode_steps
    bias_row = conv_bias.reshape(1, channels)
    step_bias_row = step_bias.reshape(1, channels)
    skip_row = skip_gain.reshape(1, channels)

    def struct(shape, dtype):
        return jax.ShapeDtypeStruct(shape, dtype)

    def scratch(shape):
        return pltpu.VMEM(shape, F32)

    def cost(flops, size):
        return pl.CostEstimate(flops=flops, bytes_accessed=size, transcendentals=0)

    dest = prompt_dest.reshape(prompts)
    conv_rows = jnp.transpose(resident_conv, (1, 0, 2))
    select_rows = jnp.transpose(select_weight)

    send_first = pl.pallas_call(
        pack_kernel,
        out_shape=struct((groups, ROWS0, channels), BF16),
        in_specs=[SMEM] * 3 + [VMEM, pl.BlockSpec(memory_space=pl.ANY), VMEM],
        out_specs=VMEM,
        scratch_shapes=[
            scratch((groups + 1, ROWS0, channels)),
            scratch((3 * reqs, channels)),
            scratch((prompts * (steps + 8), channels)),
            scratch((MIG, states, channels)),
            pltpu.SemaphoreType.DMA((MIG,)),
        ],
        compiler_params=ALL_VMEM,
        name="pack",
    )(migrate_from, dest, prompt_length, conv_rows, resident_state, prompt_inputs)
    got_first = exchange(send_first, "group")

    prompt_low, prompt_sel, prompt_x = pl.pallas_call(
        prompt_kernel,
        out_shape=(
            struct((prompt_rows, rank), F32),
            struct((prompt_rows, selects), F32),
            struct((prompt_rows, channels), BF16),
        ),
        in_specs=[VMEM] * 5,
        out_specs=(VMEM,) * 3,
        scratch_shapes=[scratch((tiles, prompt_rows, LANES)), scratch((prompt_rows, channels))],
        compiler_params=PARAMS,
        cost_estimate=cost(10**9, 2 * 10**6),
        name="prompt_features",
    )(prompt_inputs, conv_weight, bias_row, rank_weight, select_rows)

    gate_rows, decay, extra = pl.pallas_call(
        prompt_prepare_kernel,
        out_shape=(
            struct((prompt_rows, channels), F32),
            struct((tiles, 8 * states, LANES), F32),
            struct((2, channels), F32),
        ),
        in_specs=[VMEM] * 4,
        out_specs=(VMEM,) * 3,
        scratch_shapes=[scratch((tiles, prompt_rows, LANES))],
        compiler_params=PARAMS,
        cost_estimate=cost(10**9, 2 * 10**6),
        name="prompt_prepare",
    )(prompt_gates, decay_log, step_bias_row, skip_row)

    pay, decode_x, relay, final_conv, prompt_conv = pl.pallas_call(
        decode_kernel,
        out_shape=(
            struct((peers, 32, LANES), BF16),
            struct((decode_rows, channels), BF16),
            struct((groups, 8, channels), BF16),
            struct((3, reqs, channels), BF16),
            struct((3, groups * PAIR, channels), F32),
        ),
        in_specs=[SMEM] + [VMEM] * 9,
        out_specs=(VMEM,) * 5,
        scratch_shapes=[
            scratch((groups * ROWS0, channels)),
            scratch((peers, 32, LANES)),
            scratch((tiles, reqs * 8, LANES)),
            scratch((decode_rows, channels)),
        ],
        compiler_params=PARAMS,
        name="decode_features",
    )(
        migrate_from, got_first, conv_rows, decode_inputs, conv_weight, bias_row, rank_weight,
        select_rows, prompt_low, prompt_sel,
    )

    parts = exchange(pay, "mp")
    shares = pl.pallas_call(
        sum_kernel,
        out_shape=struct(parts.shape, BF16),
        in_specs=[VMEM],
        out_specs=VMEM,
        compiler_params=PARAMS,
        name="sum_parts",
    )(parts)
    rows = exchange(shares, "mp")

    prefill_out, send_final = pl.pallas_call(
        prefill_kernel,
        out_shape=(
            struct(prompt_inputs.shape, BF16),
            struct((groups, PAIR * states + 8, channels), BF16),
        ),
        in_specs=[SMEM] * 2 + [VMEM] * 7,
        out_specs=(VMEM, VMEM),
        scratch_shapes=[
            scratch((prompt_rows, rank)),
            scratch((prompt_rows, LANES)),
            scratch((prompt_rows, channels)),
            scratch((prompt_rows, channels)),
            scratch((tiles, prompts * states, LANES)),
            scratch((tiles, prompt_rows, LANES)),
        ],
        compiler_params=PARAMS,
        name="prefill_scan",
    )(
        prompt_length, dest, rows, prompt_x, gate_rows, step_weight, decay, extra, relay,
    )
    got_final = exchange(send_final, "group")

    decode_step, decode_sel, decode_gate, first_state = pl.pallas_call(
        decode_prepare_kernel,
        out_shape=(
            struct((decode_rows, channels), F32),
            struct((decode_rows, LANES), F32),
            struct((decode_rows, channels), F32),
            struct((tiles, reqs * states, LANES), F32),
        ),
        in_specs=[VMEM] * 5,
        out_specs=(VMEM,) * 4,
        scratch_shapes=[scratch((decode_rows, rank)), scratch((tiles, reqs * 8, LANES))],
        compiler_params=PARAMS,
        cost_estimate=cost(4 * 10**9, 4 * 10**6),
        name="decode_prepare",
    )(rows, decode_gates, resident_state, step_weight, extra)

    decode_out, final_state, prompt_state = pl.pallas_call(
        decode_scan_kernel,
        out_shape=(
            struct(decode_inputs.shape, BF16),
            struct(resident_state.shape, F32),
            struct((groups * PAIR, states, channels), F32),
        ),
        in_specs=[SMEM] + [VMEM] * 8,
        out_specs=(VMEM,) * 3,
        scratch_shapes=[
            scratch((decode_rows, channels)),
            scratch((tiles, reqs * states, LANES)),
            scratch((tiles, reqs * 8, LANES)),
            scratch((tiles, states * MIG, LANES)),
        ],
        compiler_params=PARAMS,
        name="decode_scan",
    )(
        migrate_from, got_final, decode_x, decode_gate, decode_step, decode_sel, decay, extra,
        first_state,
    )
    final_conv = jnp.transpose(final_conv, (1, 0, 2))
    prompt_conv = jnp.transpose(prompt_conv, (1, 0, 2)).astype(BF16)
    return (decode_out, final_state, final_conv, prefill_out, prompt_state, prompt_conv)


def solution(mesh):
    whole = P("group", None, "mp")
    return jax.shard_map(
        on_device,
        mesh=mesh,
        in_specs=(
            whole,
            whole,
            P("group"),
            whole,
            whole,
            whole,
            whole,
            P("group"),
            P("group", None),
            P(None, "mp"),
            P("mp"),
            P("mp", None),
            P("mp", None),
            P(None, "mp"),
            P("mp"),
            P(None, "mp"),
            P("mp"),
        ),
        out_specs=(whole,) * 6,
        check_vma=False,
    )
```

```python
import jax
import jax.numpy as jnp
from jax import lax
from jax.experimental import pallas as pl
from jax.experimental.pallas import tpu as pltpu
from jax.sharding import PartitionSpec as P

MIG = 4
PAIR = 2
EPS = 1e-06
LANES = 128
ROWS0 = 24
PROMPT_GROUPS = 16
STATE_ROW = 14
TAIL_ROW = 18
LOG2E = 1.4426950408889634

F32 = jnp.float32
BF16 = jnp.bfloat16
VMEM = pl.BlockSpec(memory_space=pltpu.VMEM)
SMEM = pl.BlockSpec(memory_space=pltpu.SMEM)
PARAMS = pltpu.CompilerParams(vmem_limit_bytes=40 * 1024 * 1024)
ALL_VMEM = pltpu.CompilerParams(vmem_limit_bytes=60 * 1024 * 1024)


def silu(x):
    return x / (1.0 + jnp.exp(-x))


def softplus(x):
    return jnp.maximum(x, 0.0) + jnp.log1p(jnp.exp(-jnp.abs(x)))


def iota(shape, dim):
    return lax.broadcasted_iota(jnp.int32, shape, dim)


def from_scalars(ref, count, shape, first=0):
    rows = iota(shape, 0)
    out = jnp.zeros(shape, jnp.int32)
    for i in range(count):
        out = jnp.where(rows == i, ref[first + i], out)
    return out


def slots_of(dest_ref, count, first=0):
    dests = [dest_ref[first + i] for i in range(count)]
    ranks = []
    for i in range(count):
        rank = jnp.int32(0)
        for j in range(i):
            rank = rank + (dests[j] == dests[i]).astype(jnp.int32)
        ranks.append(rank)
    return dests, ranks


def picks_of(mig_ref, reqs):
    own = lax.axis_index("group")
    count = jnp.int32(0)
    picks = [jnp.int32(0) for _ in range(MIG)]
    for r in range(reqs):
        moved = mig_ref[r] != own * reqs + r
        for k in range(MIG):
            picks[k] = jnp.where(moved & (count == k), r, picks[k])
        count = count + moved.astype(jnp.int32)
    return own, picks


def pack_kernel(
    mig_ref, dest_ref, len_ref, conv_ref, state_ref, u_ref, pay_ref, scr, conv_scr, u_scr
):
    groups = pay_ref.shape[0]
    _, reqs, channels = conv_ref.shape
    prompts, steps, _ = u_ref.shape
    states = state_ref.shape[1]
    own, picks = picks_of(mig_ref, reqs)
    base = scr.at[groups]
    base[...] = jnp.zeros(base.shape, F32)
    lane = iota((1, channels), 1)
    ids = jnp.zeros((1, channels), jnp.int32)
    wanted = jnp.zeros((1, channels), jnp.int32)
    for j in range(3):
        conv_scr[j * reqs : (j + 1) * reqs, :] = conv_ref[j].astype(F32)
    for k in range(MIG):
        for at in (k, 4 + k, 8 + k, STATE_ROW + k):
            ids = jnp.where(lane == own * ROWS0 + at, own * reqs + picks[k], ids)
        wanted = jnp.where(lane == own * MIG + k, mig_ref[picks[k]], wanted)
        for j in range(3):
            at = 4 * j + k
            base[at : at + 1, :] = conv_scr[pl.ds(j * reqs + picks[k], 1), :]
    base[12:13, :] = ids.astype(F32)
    base[13:14, :] = wanted.astype(F32)
    for d in range(groups):
        scr[d] = base[...]
    dests, ranks = slots_of(dest_ref, prompts)
    pad = u_scr.shape[0] // prompts
    for i in range(prompts):
        u_scr[i * pad : i * pad + 8, :] = jnp.zeros((8, channels), F32)
        u_scr[i * pad + 8 : i * pad + 8 + steps, :] = u_ref[i].astype(F32)
    for i in range(prompts):
        tails = [u_scr[pl.ds(i * pad + 5 + j + len_ref[i], 1), :] for j in range(3)]
        for q in range(PAIR):

            @pl.when(ranks[i] == q)
            def _():
                for j in range(3):
                    at = TAIL_ROW + 3 * q + j
                    scr[dests[i], at : at + 1, :] = tails[j]

    for k in range(MIG):
        state = state_ref[picks[k]]
        for n in range(states):
            scr[n, STATE_ROW + k : STATE_ROW + k + 1, :] = state[n : n + 1, :]
    for d in range(groups):
        pay_ref[d] = scr[d].astype(BF16)


def put_lanes(ref, start, value):
    for l in range(ref.shape[0]):
        ref[l, start : start + value.shape[0], :] = value[:, l * LANES : (l + 1) * LANES]


def project(x, rank_ref, select_ref):
    low = jnp.dot(x, rank_ref[...], preferred_element_type=F32)
    sel = lax.dot_general(
        x, select_ref[...], (((1,), (1,)), ((), ())), preferred_element_type=F32
    )
    return low, sel


def put_tiles(scr, first, low, sel):
    tiles = low.shape[1] // LANES
    width = sel.shape[1]
    share = LANES // width
    for g in range(low.shape[0] // 8):
        rows = slice(8 * g, 8 * g + 8)
        for l in range(tiles):
            owner, place = divmod((first + g) * tiles + l, 3)
            scr[owner, 8 * place : 8 * place + 8, :] = low[rows, l * LANES : (l + 1) * LANES]
        pair, place = divmod(first + g, share)
        cols = slice(place * width, (place + 1) * width)
        scr[2 * pair, 24:28, cols] = sel[8 * g : 8 * g + 4]
        scr[2 * pair + 1, 24:28, cols] = sel[8 * g + 4 : 8 * g + 8]


def take_tiles(rows_ref, first, low_scr, sel_scr):
    count, channels = low_scr.shape
    tiles = channels // LANES
    for g in range(count // 8):
        upper, lower = slice(8 * g, 8 * g + 4), slice(8 * g + 4, 8 * g + 8)
        for l in range(tiles):
            cols = slice(l * LANES, (l + 1) * LANES)
            owner, place = divmod((first + g) * tiles + l, 3)
            low_scr[upper, cols] = rows_ref[owner, 2 * place].astype(F32)
            low_scr[lower, cols] = rows_ref[owner, 2 * place + 1].astype(F32)
        pair, place = divmod(first + g, 4)
        sel_scr[upper, :] = rows_ref[2 * pair, 6].astype(F32)
        sel_scr[lower, :] = rows_ref[2 * pair + 1, 6].astype(F32)
    for g in range(count // 8):
        place = (first + g) % 4
        if place:
            rows = slice(8 * g, 8 * g + 8)
            sel_scr[rows, :] = pltpu.roll(sel_scr[rows, :], LANES - 32 * place, 1)


def prompt_kernel(
    mig_ref, dest_ref, len_ref, u_ref, gate_ref, cw_ref, cb_ref, rank_ref, select_ref, decay_ref,
    step_b_ref, skip_ref, low_ref, sel_ref, x_ref, gate_out_ref, decay_out_ref, extra_ref,
    plan_ref, scr, x_scr,
):
    prompts, steps, channels = u_ref.shape
    reqs = mig_ref.shape[0]
    for i in range(reqs):
        plan_ref[i] = mig_ref[i]
    for i in range(prompts):
        plan_ref[reqs + i] = dest_ref[i]
        plan_ref[reqs + prompts + i] = len_ref[i]
    extra_ref[0:1, :] = step_b_ref[...]
    extra_ref[1:2, :] = skip_ref[...]
    extra_ref[2:3, :] = cb_ref[...]
    extra_ref[3:8, :] = jnp.zeros((5, channels), F32)
    decay = jnp.exp(decay_ref[...]) * -LOG2E
    for n in range(decay.shape[0]):
        put_lanes(decay_out_ref, 8 * n, jnp.broadcast_to(decay[n : n + 1], (8, channels)))
    for i in range(prompts):
        put_lanes(scr, i * steps, silu(gate_ref[i].astype(F32)))
    for l in range(channels // LANES):
        cols = slice(l * LANES, (l + 1) * LANES)
        for t in range(steps):
            gate_out_ref[t * prompts : (t + 1) * prompts, cols] = scr[
                l, pl.ds(t, prompts, stride=steps), :
            ]
    for i in range(prompts):
        put_lanes(scr, i * steps, u_ref[i].astype(F32))
    for l in range(channels // LANES):
        cols = slice(l * LANES, (l + 1) * LANES)
        taps = [cw_ref[k : k + 1, cols] for k in range(4)]
        bias = cb_ref[:, cols]
        window = [jnp.zeros((prompts, LANES), F32) for _ in range(3)]
        for t in range(steps):
            window.append(scr[l, pl.ds(t, prompts, stride=steps), :])
            acc = bias
            for k in range(4):
                acc = acc + taps[k] * window[t + k]
            x_scr[t * prompts : (t + 1) * prompts, cols] = silu(acc)
    x = x_scr[...].astype(BF16)
    x_ref[...] = x
    low, sel = project(x, rank_ref, select_ref)
    low_ref[...] = low
    sel_ref[...] = sel


def decode_kernel(
    plan_ref, got_ref, conv_ref, u_ref, cw_ref, extra_ref, rank_ref, select_ref, prompt_low_ref,
    prompt_sel_ref, pay_ref, x_ref, pass_ref, pool_scr, pay_scr, scr, x_scr,
):
    groups = got_ref.shape[0]
    reqs, steps, channels = u_ref.shape
    table = groups * ROWS0
    own = lax.axis_index("group")
    marks = jnp.zeros((8, channels), F32)
    for s in range(groups):
        block = got_ref[s].astype(F32)
        pool_scr[s * ROWS0 : (s + 1) * ROWS0, :] = block
        marks = marks + block[8:16]
    for r in range(reqs):
        put_lanes(scr, 8 * r, u_ref[r].astype(F32))
    pool = pool_scr[...].astype(BF16)
    ids = marks[4:5, :table]
    place = lax.rem(iota((1, table), 1), ROWS0)
    moves = groups * MIG
    square = (moves, LANES)
    wanted = jnp.sum(
        jnp.where(
            iota(square, 0) == iota(square, 1), jnp.broadcast_to(marks[5:6, :LANES], square), 0.0
        ),
        axis=1,
        keepdims=True,
    )
    passed = (wanted == ids) & (place >= STATE_ROW) & (place < STATE_ROW + MIG)
    relay = jnp.dot(jnp.where(passed, 1.0, 0.0).astype(BF16), pool, preferred_element_type=F32)
    for d in range(groups):
        pass_ref[d] = relay[d * MIG : (d + 1) * MIG].astype(BF16)
    wide = (reqs, channels)
    moved_wide = from_scalars(plan_ref, reqs, wide) != own * reqs + iota(wide, 0)
    shape = (reqs, table)
    needs = from_scalars(plan_ref, reqs, shape)
    found = (needs != own * reqs + iota(shape, 0)) & (
        jnp.broadcast_to(ids, shape) == needs.astype(F32)
    )
    hist = []
    for j in range(3):
        hit = jnp.where(found & (place >= 4 * j) & (place < 4 * j + 4), 1.0, 0.0).astype(BF16)
        taken = jnp.dot(hit, pool, preferred_element_type=F32)
        hist.append(jnp.where(moved_wide, taken, conv_ref[j].astype(F32)))
    for l in range(channels // LANES):
        cols = slice(l * LANES, (l + 1) * LANES)
        taps = [cw_ref[k : k + 1, cols] for k in range(4)]
        bias = extra_ref[2:3, cols]
        window = [hist[j][:, cols] for j in range(3)]
        for t in range(steps):
            window.append(scr[l, pl.ds(t, reqs, stride=8), :])
            acc = bias
            for k in range(4):
                acc = acc + taps[k] * window[t + k]
            x_scr[t * reqs : (t + 1) * reqs, cols] = silu(acc)
    x = x_scr[...].astype(BF16)
    x_ref[...] = x
    low, sel = project(x, rank_ref, select_ref)
    prompt_groups = prompt_low_ref.shape[0] // 8
    pay_scr[...] = jnp.zeros(pay_scr.shape, F32)
    put_tiles(pay_scr, 0, prompt_low_ref[...], prompt_sel_ref[...])
    put_tiles(pay_scr, prompt_groups, low, sel)
    peers, blocks, four, _ = pay_ref.shape
    for j in range(peers):
        for a in range(blocks):
            pay_ref[j, a] = pay_scr[j, four * a : four * (a + 1), :].astype(BF16)


def sum_kernel(got_ref, out_ref):
    total = got_ref[0].astype(F32)
    for j in range(1, got_ref.shape[0]):
        total = total + got_ref[j].astype(F32)
    own_rows = total.astype(BF16)
    for j in range(out_ref.shape[0]):
        out_ref[j] = own_rows


def steps_of(low_scr, step_w_ref, step_b):
    low = low_scr[...]
    scale = lax.rsqrt(jnp.mean(low * low, axis=-1, keepdims=True) + EPS)
    raw = jnp.dot(low.astype(BF16), step_w_ref[...], preferred_element_type=F32)
    return softplus(raw * scale + step_b)


def scan(t, items, live, x, gate, sel, step, decay, skip, h_scr, y_scr, y_stride):
    states = decay.shape[1] // 8
    for g in range(items // 8):
        rows = slice(t * items + 8 * g, t * items + 8 * g + 8)
        alive = None if live is None else live[8 * g : 8 * g + 8]
        pair = sel[rows, :]
        lanes = range(h_scr.shape[0])
        steps, drive, y = [], [], []
        for l in lanes:
            cols = slice(l * LANES, (l + 1) * LANES)
            step_l = step[rows, cols]
            if alive is not None:
                step_l = jnp.where(alive, step_l, 0.0)
            x_l = x[rows, cols]
            steps.append(step_l)
            drive.append(step_l * x_l)
            y.append(skip[:, cols] * x_l)
        for n in range(states):
            b = jnp.broadcast_to(pair[:, n : n + 1], (8, LANES))
            c = jnp.broadcast_to(pair[:, states + n : states + n + 1], (8, LANES))
            at = slice(n * items + 8 * g, n * items + 8 * g + 8)
            for l in lanes:
                keep = jnp.exp2(steps[l] * decay[l, 8 * n : 8 * n + 8, :])
                h = keep * h_scr[l, at, :] + drive[l] * b
                h_scr[l, at, :] = h
                y[l] = y[l] + c * h
        for l in lanes:
            cols = slice(l * LANES, (l + 1) * LANES)
            out = y[l] * gate[rows, cols]
            if alive is not None:
                out = jnp.where(alive, out, 0.0)
            y_scr[l, pl.ds(8 * g * y_stride + t, 8, stride=y_stride), :] = out


def prefill_kernel(
    plan_ref, rows_ref, x_ref, gate_ref, step_w_ref, decay_ref, extra_ref, relay_ref,
    out_ref, pay_ref, low_scr, sel_scr, step_scr, x_scr, h_scr, y_scr,
):
    prompts, steps, channels = out_ref.shape
    states = decay_ref.shape[1] // 8
    reqs = plan_ref.shape[0] - 2 * prompts
    take_tiles(rows_ref, 0, low_scr, sel_scr)
    step_scr[...] = steps_of(low_scr, step_w_ref, extra_ref[0:1, :])
    x_scr[...] = x_ref[...].astype(F32)
    h_scr[...] = jnp.zeros(h_scr.shape, F32)
    lengths = from_scalars(plan_ref, prompts, (prompts, LANES), reqs + prompts)
    skip = extra_ref[1:2, :]
    for t in range(steps):
        scan(
            t, prompts, t < lengths, x_scr, gate_ref, sel_scr, step_scr, decay_ref, skip, h_scr,
            y_scr, steps,
        )
    dests, ranks = slots_of(plan_ref, prompts, reqs)
    groups, blocks, four, _ = pay_ref.shape
    parts = states // four
    for d in range(groups):
        pay_ref[d, : blocks - 1] = jnp.zeros((blocks - 1, four, channels), BF16)
        pay_ref[d, blocks - 1] = relay_ref[d]
    for i in range(prompts):
        at = ranks[i] * parts
        for l in range(channels // LANES):
            cols = slice(l * LANES, (l + 1) * LANES)
            out_ref[i, :, cols] = y_scr[l, i * steps : (i + 1) * steps, :].astype(BF16)
            final = h_scr[l, pl.ds(i, states, stride=prompts), :]
            for p in range(parts):
                pay_ref[dests[i], at + p, :, cols] = final[p * four : (p + 1) * four].astype(BF16)


def decode_scan_kernel(
    plan_ref, rows_ref, x_ref, u_ref, gate_ref, state_ref, step_w_ref, decay_ref, extra_ref,
    got_ref, out_ref, final_ref, base_ref, held_ref, weight_ref, keep_ref, pick_ref,
    final_conv_ref, prompt_conv_ref, low_scr, sel_scr, step_scr, x_scr, gate_scr, scr, h_scr, y_scr,
    conv_scr,
):
    reqs, steps, channels = gate_ref.shape
    states = state_ref.shape[1]
    lanes = channels // LANES
    own, picks = picks_of(plan_ref, reqs)
    take_tiles(rows_ref, PROMPT_GROUPS, low_scr, sel_scr)
    step_scr[...] = steps_of(low_scr, step_w_ref, extra_ref[0:1, :])
    x_scr[...] = x_ref[...].astype(F32)
    for r in range(reqs):
        put_lanes(scr, 8 * r, silu(gate_ref[r].astype(F32)))
        kept = plan_ref[r] == own * reqs + r
        for l in range(lanes):
            cols = slice(l * LANES, (l + 1) * LANES)
            h_scr[l, pl.ds(r, states, stride=reqs), :] = jnp.where(
                kept, state_ref[r, :, cols], 0.0
            )
    for l in range(lanes):
        cols = slice(l * LANES, (l + 1) * LANES)
        for t in range(steps):
            gate_scr[t * reqs : (t + 1) * reqs, cols] = scr[l, pl.ds(t, reqs, stride=8), :]
    skip = extra_ref[1:2, :]
    for t in range(steps):
        scan(t, reqs, None, x_scr, gate_scr, sel_scr, step_scr, decay_ref, skip, h_scr, y_scr, 8)
    for r in range(reqs):
        final_conv_ref[:, r : r + 1, :] = u_ref[r].astype(F32)[1:4].reshape(3, 1, channels)
        for l in range(lanes):
            cols = slice(l * LANES, (l + 1) * LANES)
            final_ref[r, :, cols] = h_scr[l, pl.ds(r, states, stride=reqs), :]
            out_ref[r, :, cols] = y_scr[l, 8 * r : 8 * r + steps, :].astype(BF16)
    outward = jnp.transpose(sel_scr[...])[states : 2 * states]
    column = iota(outward.shape, 1)
    for k in range(MIG):
        pick_ref[k : k + 1, :] = jnp.broadcast_to(picks[k], (1, LANES)).astype(F32)
        held_ref[k] = final_ref[picks[k]]
        total = jnp.zeros((1, channels), F32)
        for t in range(steps):
            row = t * reqs + picks[k]
            total = total + step_scr[pl.ds(row, 1), :]
            gate = gate_scr[pl.ds(row, 1), :]
            c = jnp.sum(jnp.where(column == row, outward, 0.0), axis=1, keepdims=True)
            for l in range(lanes):
                cols = slice(l * LANES, (l + 1) * LANES)
                keep = jnp.exp2(total[:, cols] * decay_ref[l, pl.ds(0, states, stride=8), :])
                weight_ref[k * steps + t, :, cols] = keep * c * gate[:, cols]
                base_ref[k * steps + t : k * steps + t + 1, cols] = y_scr[
                    l, pl.ds(8 * picks[k] + t, 1), :
                ]
                if t == steps - 1:
                    keep_ref[k, :, cols] = keep
    pick_ref[MIG:, :] = jnp.zeros((pick_ref.shape[0] - MIG, LANES), F32)
    for s in range(got_ref.shape[0]):
        block = got_ref[s].astype(F32)
        for q in range(PAIR):
            for j in range(3):
                at = TAIL_ROW + 3 * q + j
                conv_scr[j, s * PAIR + q : s * PAIR + q + 1, :] = block[at : at + 1]
    prompt_conv_ref[...] = conv_scr[...].astype(BF16)


def finish_kernel(
    got_ref, base_ref, held_ref, weight_ref, keep_ref, pick_ref, _out, _final, out_ref, final_ref,
    prompt_state_ref, state_scr, moved_scr, out_scr, final_scr, sems,
):
    groups, blocks, four, channels = got_ref.shape
    slots, states, _ = state_scr.shape
    steps = base_ref.shape[0] // MIG
    lanes = channels // LANES
    parts = states // four
    copies = []
    for n in range(states):
        put_lanes(moved_scr, n * MIG, got_ref[n, blocks - 1].astype(F32))
    for k in range(MIG):
        pick = jnp.max(pick_ref[k : k + 1, :]).astype(jnp.int32)
        for l in range(lanes):
            cols = slice(l * LANES, (l + 1) * LANES)
            start = moved_scr[l, pl.ds(k, states, stride=MIG), :]
            final_scr[k, :, cols] = held_ref[k, :, cols] + keep_ref[k, :, cols] * start
            rows = []
            for t in range(steps):
                at = k * steps + t
                more = jnp.sum(weight_ref[at, :, cols] * start, axis=0, keepdims=True)
                rows.append(base_ref[at : at + 1, cols] + more)
            out_scr[k, :, cols] = jnp.concatenate(rows, axis=0).astype(BF16)
        copies.append(
            pltpu.make_async_copy(final_scr.at[k], final_ref.at[pick], sems.at[groups + k])
        )
        copies.append(
            pltpu.make_async_copy(out_scr.at[k], out_ref.at[pick], sems.at[groups + MIG + k])
        )
        copies[-2].start()
        copies[-1].start()
    for s in range(groups):
        for q in range(PAIR):
            for p in range(parts):
                state_scr[s * PAIR + q, p * four : (p + 1) * four, :] = got_ref[
                    s, q * parts + p
                ].astype(F32)
        here = pl.ds(s * PAIR, PAIR)
        copies.append(
            pltpu.make_async_copy(state_scr.at[here], prompt_state_ref.at[here], sems.at[s])
        )
        copies[-1].start()
    for copy in copies:
        copy.wait()


def exchange(value, axis):
    return lax.all_to_all(value, axis, split_axis=0, concat_axis=0, tiled=True)


def on_device(
    resident_state,
    resident_conv,
    migrate_from,
    decode_inputs,
    decode_gates,
    prompt_inputs,
    prompt_gates,
    prompt_length,
    prompt_dest,
    conv_weight,
    conv_bias,
    rank_weight,
    select_weight,
    step_weight,
    step_bias,
    decay_log,
    skip_gain,
):
    groups = lax.axis_size("group")
    peers = lax.axis_size("mp")
    reqs, states, channels = resident_state.shape
    prompts, steps, _ = prompt_inputs.shape
    decode_steps = decode_inputs.shape[1]
    tiles = channels // LANES
    rank = rank_weight.shape[1]
    selects = select_weight.shape[1]
    prompt_rows = prompts * steps
    decode_rows = reqs * decode_steps
    bias_row = conv_bias.reshape(1, channels)
    step_bias_row = step_bias.reshape(1, channels)
    skip_row = skip_gain.reshape(1, channels)

    def struct(shape, dtype):
        return jax.ShapeDtypeStruct(shape, dtype)

    def scratch(shape):
        return pltpu.VMEM(shape, F32)

    def cost(flops, size):
        return pl.CostEstimate(flops=flops, bytes_accessed=size, transcendentals=0)

    dest = prompt_dest.reshape(prompts)
    conv_rows = jnp.transpose(resident_conv, (1, 0, 2))
    select_rows = jnp.transpose(select_weight)

    send_first = pl.pallas_call(
        pack_kernel,
        out_shape=struct((groups, ROWS0, channels), BF16),
        in_specs=[SMEM] * 3 + [VMEM] * 3,
        out_specs=VMEM,
        scratch_shapes=[
            scratch((groups + 1, ROWS0, channels)),
            scratch((3 * reqs, channels)),
            scratch((prompts * (steps + 8), channels)),
        ],
        compiler_params=ALL_VMEM,
        name="pack",
    )(migrate_from, dest, prompt_length, conv_rows, resident_state, prompt_inputs)
    got_first = exchange(send_first, "group")

    prompt_low, prompt_sel, prompt_x, gate_rows, decay, extra, plan = pl.pallas_call(
        prompt_kernel,
        out_shape=(
            struct((prompt_rows, rank), F32),
            struct((prompt_rows, selects), F32),
            struct((prompt_rows, channels), BF16),
            struct((prompt_rows, channels), F32),
            struct((tiles, 8 * states, LANES), F32),
            struct((8, channels), F32),
            struct((reqs + 2 * prompts,), jnp.int32),
        ),
        in_specs=[SMEM] * 3 + [VMEM] * 9,
        out_specs=(VMEM,) * 6 + (SMEM,),
        scratch_shapes=[scratch((tiles, prompt_rows, LANES)), scratch((prompt_rows, channels))],
        compiler_params=PARAMS,
        cost_estimate=cost(10**9, 2 * 10**6),
        name="prompt_features",
    )(
        migrate_from, dest, prompt_length, prompt_inputs, prompt_gates, conv_weight, bias_row,
        rank_weight, select_rows, decay_log, step_bias_row, skip_row,
    )

    pay, decode_x, relay = pl.pallas_call(
        decode_kernel,
        out_shape=(
            struct((peers, 7, 4, LANES), BF16),
            struct((decode_rows, channels), BF16),
            struct((groups, MIG, channels), BF16),
        ),
        in_specs=[SMEM] + [VMEM] * 9,
        out_specs=(VMEM,) * 3,
        scratch_shapes=[
            scratch((groups * ROWS0, channels)),
            scratch((peers, 32, LANES)),
            scratch((tiles, reqs * 8, LANES)),
            scratch((decode_rows, channels)),
        ],
        compiler_params=PARAMS,
        name="decode_features",
    )(
        plan, got_first, conv_rows, decode_inputs, conv_weight, extra, rank_weight, select_rows,
        prompt_low, prompt_sel,
    )

    parts = exchange(pay, "mp")
    shares = pl.pallas_call(
        sum_kernel,
        out_shape=struct(parts.shape, BF16),
        in_specs=[VMEM],
        out_specs=VMEM,
        compiler_params=PARAMS,
        name="sum_parts",
    )(parts)
    rows = exchange(shares, "mp")

    prefill_out, send_final = pl.pallas_call(
        prefill_kernel,
        out_shape=(
            struct(prompt_inputs.shape, BF16),
            struct((groups, PAIR * states // MIG + 1, MIG, channels), BF16),
        ),
        in_specs=[SMEM] + [VMEM] * 7,
        out_specs=(VMEM, VMEM),
        scratch_shapes=[
            scratch((prompt_rows, rank)),
            scratch((prompt_rows, LANES)),
            scratch((prompt_rows, channels)),
            scratch((prompt_rows, channels)),
            scratch((tiles, prompts * states, LANES)),
            scratch((tiles, prompt_rows, LANES)),
        ],
        compiler_params=PARAMS,
        name="prefill_scan",
    )(plan, rows, prompt_x, gate_rows, step_weight, decay, extra, relay)
    got_final = exchange(send_final, "group")

    early_out, early_final, base, held, weight, keep, pick, final_conv, prompt_conv = pl.pallas_call(
        decode_scan_kernel,
        out_shape=(
            struct(decode_inputs.shape, BF16),
            struct(resident_state.shape, F32),
            struct((MIG * decode_steps, channels), F32),
            struct((MIG, states, channels), F32),
            struct((MIG * decode_steps, states, channels), F32),
            struct((MIG, states, channels), F32),
            struct((8, LANES), F32),
            struct((3, reqs, channels), F32),
            struct((3, groups * PAIR, channels), BF16),
        ),
        in_specs=[SMEM] + [VMEM] * 9,
        out_specs=(VMEM,) * 9,
        scratch_shapes=[
            scratch((decode_rows, rank)),
            scratch((decode_rows, LANES)),
            scratch((decode_rows, channels)),
            scratch((decode_rows, channels)),
            scratch((decode_rows, channels)),
            scratch((tiles, reqs * 8, LANES)),
            scratch((tiles, reqs * states, LANES)),
            scratch((tiles, reqs * 8, LANES)),
            scratch((3, groups * PAIR, channels)),
        ],
        compiler_params=PARAMS,
        cost_estimate=cost(6 * 10**9, 8 * 10**6),
        name="decode_scan",
    )(
        plan, rows, decode_x, decode_inputs, decode_gates, resident_state, step_weight, decay,
        extra, got_first,
    )

    anywhere = pl.BlockSpec(memory_space=pl.ANY)
    decode_out, final_state, prompt_state = pl.pallas_call(
        finish_kernel,
        out_shape=(
            struct(decode_inputs.shape, BF16),
            struct(resident_state.shape, F32),
            struct((groups * PAIR, states, channels), F32),
        ),
        in_specs=[VMEM] * 6 + [anywhere] * 2,
        out_specs=(anywhere,) * 3,
        scratch_shapes=[
            scratch((groups * PAIR, states, channels)),
            scratch((tiles, states * MIG, LANES)),
            pltpu.VMEM((MIG, decode_steps, channels), BF16),
            scratch((MIG, states, channels)),
            pltpu.SemaphoreType.DMA((groups + 2 * MIG,)),
        ],
        input_output_aliases={6: 0, 7: 1},
        compiler_params=PARAMS,
        name="finish",
    )(got_final, base, held, weight, keep, pick, early_out, early_final)
    final_conv = jnp.transpose(final_conv, (1, 0, 2)).astype(BF16)
    prompt_conv = jnp.transpose(prompt_conv, (1, 0, 2))
    return (decode_out, final_state, final_conv, prefill_out, prompt_state, prompt_conv)


def solution(mesh):
    whole = P("group", None, "mp")
    return jax.shard_map(
        on_device,
        mesh=mesh,
        in_specs=(
            whole,
            whole,
            P("group"),
            whole,
            whole,
            whole,
            whole,
            P("group"),
            P("group", None),
            P(None, "mp"),
            P("mp"),
            P("mp", None),
            P("mp", None),
            P(None, "mp"),
            P("mp"),
            P(None, "mp"),
            P("mp"),
        ),
        out_specs=(whole,) * 6,
        check_vma=False,
    )
```

```python
import jax
import jax.numpy as jnp
from jax import lax
from jax.experimental import pallas as pl
from jax.experimental.pallas import tpu as pltpu
from jax.sharding import PartitionSpec as P

MIG = 4
PAIR = 2
EPS = 1e-06
LANES = 128
ROWS0 = 24
PROMPT_GROUPS = 16
STATE_ROW = 14
TAIL_ROW = 18
LOG2E = 1.4426950408889634

F32 = jnp.float32
BF16 = jnp.bfloat16
VMEM = pl.BlockSpec(memory_space=pltpu.VMEM)
SMEM = pl.BlockSpec(memory_space=pltpu.SMEM)
PARAMS = pltpu.CompilerParams(vmem_limit_bytes=40 * 1024 * 1024)
ALL_VMEM = pltpu.CompilerParams(vmem_limit_bytes=60 * 1024 * 1024)


def silu(x):
    return x / (1.0 + jnp.exp(-x))


def softplus(x):
    return jnp.maximum(x, 0.0) + jnp.log1p(jnp.exp(-jnp.abs(x)))


def iota(shape, dim):
    return lax.broadcasted_iota(jnp.int32, shape, dim)


def from_scalars(ref, count, shape, first=0):
    rows = iota(shape, 0)
    out = jnp.zeros(shape, jnp.int32)
    for i in range(count):
        out = jnp.where(rows == i, ref[first + i], out)
    return out


def slots_of(dest_ref, count, first=0):
    dests = [dest_ref[first + i] for i in range(count)]
    ranks = []
    for i in range(count):
        rank = jnp.int32(0)
        for j in range(i):
            rank = rank + (dests[j] == dests[i]).astype(jnp.int32)
        ranks.append(rank)
    return dests, ranks


def picks_of(mig_ref, reqs):
    own = lax.axis_index("group")
    count = jnp.int32(0)
    picks = [jnp.int32(0) for _ in range(MIG)]
    for r in range(reqs):
        moved = mig_ref[r] != own * reqs + r
        for k in range(MIG):
            picks[k] = jnp.where(moved & (count == k), r, picks[k])
        count = count + moved.astype(jnp.int32)
    return own, picks


def pack_kernel(
    mig_ref, dest_ref, len_ref, conv_ref, state_ref, u_ref, pay_ref, scr, conv_scr, u_scr
):
    groups = pay_ref.shape[0]
    _, reqs, channels = conv_ref.shape
    prompts, steps, _ = u_ref.shape
    states = state_ref.shape[1]
    own, picks = picks_of(mig_ref, reqs)
    base = scr.at[groups]
    base[...] = jnp.zeros(base.shape, F32)
    lane = iota((1, channels), 1)
    ids = jnp.zeros((1, channels), jnp.int32)
    wanted = jnp.zeros((1, channels), jnp.int32)
    for j in range(3):
        conv_scr[j * reqs : (j + 1) * reqs, :] = conv_ref[j].astype(F32)
    for k in range(MIG):
        for at in (k, 4 + k, 8 + k, STATE_ROW + k):
            ids = jnp.where(lane == own * ROWS0 + at, own * reqs + picks[k], ids)
        wanted = jnp.where(lane == own * MIG + k, mig_ref[picks[k]], wanted)
        for j in range(3):
            at = 4 * j + k
            base[at : at + 1, :] = conv_scr[pl.ds(j * reqs + picks[k], 1), :]
    base[12:13, :] = ids.astype(F32)
    base[13:14, :] = wanted.astype(F32)
    for d in range(groups):
        scr[d] = base[...]
    dests, ranks = slots_of(dest_ref, prompts)
    pad = u_scr.shape[0] // prompts
    for i in range(prompts):
        u_scr[i * pad : i * pad + 8, :] = jnp.zeros((8, channels), F32)
        u_scr[i * pad + 8 : i * pad + 8 + steps, :] = u_ref[i].astype(F32)
    for i in range(prompts):
        tails = [u_scr[pl.ds(i * pad + 5 + j + len_ref[i], 1), :] for j in range(3)]
        for q in range(PAIR):

            @pl.when(ranks[i] == q)
            def _():
                for j in range(3):
                    at = TAIL_ROW + 3 * q + j
                    scr[dests[i], at : at + 1, :] = tails[j]

    for k in range(MIG):
        state = state_ref[picks[k]]
        for n in range(states):
            scr[n, STATE_ROW + k : STATE_ROW + k + 1, :] = state[n : n + 1, :]
    for d in range(groups):
        pay_ref[d] = scr[d].astype(BF16)


def put_lanes(ref, start, value):
    for l in range(ref.shape[0]):
        ref[l, start : start + value.shape[0], :] = value[:, l * LANES : (l + 1) * LANES]


def project(x, rank_ref, select_ref):
    low = jnp.dot(x, rank_ref[...], preferred_element_type=F32)
    sel = lax.dot_general(
        x, select_ref[...], (((1,), (1,)), ((), ())), preferred_element_type=F32
    )
    return low, sel


def put_tiles(scr, first, low, sel):
    tiles = low.shape[1] // LANES
    width = sel.shape[1]
    share = LANES // width
    for g in range(low.shape[0] // 8):
        rows = slice(8 * g, 8 * g + 8)
        for l in range(tiles):
            owner, place = divmod((first + g) * tiles + l, 3)
            scr[owner, 8 * place : 8 * place + 8, :] = low[rows, l * LANES : (l + 1) * LANES]
        pair, place = divmod(first + g, share)
        cols = slice(place * width, (place + 1) * width)
        scr[2 * pair, 24:28, cols] = sel[8 * g : 8 * g + 4]
        scr[2 * pair + 1, 24:28, cols] = sel[8 * g + 4 : 8 * g + 8]


def take_tiles(rows_ref, first, low_scr, sel_scr):
    count, channels = low_scr.shape
    tiles = channels // LANES
    for g in range(count // 8):
        upper, lower = slice(8 * g, 8 * g + 4), slice(8 * g + 4, 8 * g + 8)
        for l in range(tiles):
            cols = slice(l * LANES, (l + 1) * LANES)
            owner, place = divmod((first + g) * tiles + l, 3)
            low_scr[upper, cols] = rows_ref[owner, 2 * place].astype(F32)
            low_scr[lower, cols] = rows_ref[owner, 2 * place + 1].astype(F32)
        pair, place = divmod(first + g, 4)
        sel_scr[upper, :] = rows_ref[2 * pair, 6].astype(F32)
        sel_scr[lower, :] = rows_ref[2 * pair + 1, 6].astype(F32)
    for g in range(count // 8):
        place = (first + g) % 4
        if place:
            rows = slice(8 * g, 8 * g + 8)
            sel_scr[rows, :] = pltpu.roll(sel_scr[rows, :], LANES - 32 * place, 1)


def prompt_kernel(
    mig_ref, dest_ref, len_ref, u_ref, gate_ref, cw_ref, cb_ref, rank_ref, select_ref, decay_ref,
    step_b_ref, skip_ref, low_ref, sel_ref, x_ref, gate_out_ref, decay_out_ref, extra_ref,
    plan_ref, items_ref, empty_ref, scr, x_scr, empty_scr, sem,
):
    prompts, steps, channels = u_ref.shape
    reqs = mig_ref.shape[0]
    empty_scr[...] = jnp.zeros(empty_scr.shape, BF16)
    empty = pltpu.make_async_copy(empty_scr, empty_ref, sem)
    empty.start()
    for i in range(reqs):
        plan_ref[i] = mig_ref[i]
    for i in range(prompts):
        plan_ref[reqs + i] = dest_ref[i]
        plan_ref[reqs + prompts + i] = len_ref[i]
    own = lax.axis_index("group")
    wanted = from_scalars(mig_ref, reqs, (reqs, LANES))
    moved = wanted != own * reqs + iota(wanted.shape, 0)
    items_ref[:reqs, :] = wanted.astype(F32)
    items_ref[reqs : 2 * reqs, :] = jnp.where(moved, 1.0, 0.0)
    items_ref[2 * reqs :, :] = from_scalars(len_ref, prompts, (prompts, LANES)).astype(F32)
    extra_ref[0:1, :] = step_b_ref[...]
    extra_ref[1:2, :] = skip_ref[...]
    extra_ref[2:3, :] = cb_ref[...]
    extra_ref[3:8, :] = jnp.zeros((5, channels), F32)
    decay = jnp.exp(decay_ref[...]) * -LOG2E
    for n in range(decay.shape[0]):
        put_lanes(decay_out_ref, 8 * n, jnp.broadcast_to(decay[n : n + 1], (8, channels)))
    for i in range(prompts):
        put_lanes(scr, i * steps, silu(gate_ref[i].astype(F32)))
    for l in range(channels // LANES):
        cols = slice(l * LANES, (l + 1) * LANES)
        for t in range(steps):
            gate_out_ref[t * prompts : (t + 1) * prompts, cols] = scr[
                l, pl.ds(t, prompts, stride=steps), :
            ]
    for i in range(prompts):
        put_lanes(scr, i * steps, u_ref[i].astype(F32))
    for l in range(channels // LANES):
        cols = slice(l * LANES, (l + 1) * LANES)
        taps = [cw_ref[k : k + 1, cols] for k in range(4)]
        bias = cb_ref[:, cols]
        window = [jnp.zeros((prompts, LANES), F32) for _ in range(3)]
        for t in range(steps):
            window.append(scr[l, pl.ds(t, prompts, stride=steps), :])
            acc = bias
            for k in range(4):
                acc = acc + taps[k] * window[t + k]
            x_scr[t * prompts : (t + 1) * prompts, cols] = silu(acc)
    x = x_scr[...].astype(BF16)
    x_ref[...] = x
    low, sel = project(x, rank_ref, select_ref)
    low_ref[...] = low
    sel_ref[...] = sel
    empty.wait()


def decode_kernel(
    items_ref, got_ref, conv_ref, u_ref, cw_ref, extra_ref, rank_ref, select_ref, prompt_low_ref,
    prompt_sel_ref, pay_ref, x_ref, pass_ref, pool_scr, pay_scr, scr, x_scr,
):
    groups = got_ref.shape[0]
    reqs, steps, channels = u_ref.shape
    table = groups * ROWS0
    marks = jnp.zeros((8, channels), F32)
    for s in range(groups):
        block = got_ref[s].astype(F32)
        pool_scr[s * ROWS0 : (s + 1) * ROWS0, :] = block
        marks = marks + block[8:16]
    for r in range(reqs):
        put_lanes(scr, 8 * r, u_ref[r].astype(F32))
    pool = pool_scr[...].astype(BF16)
    ids = marks[4:5, :table]
    place = lax.rem(iota((1, table), 1), ROWS0)
    moves = groups * MIG
    square = (moves, LANES)
    wanted = jnp.sum(
        jnp.where(
            iota(square, 0) == iota(square, 1), jnp.broadcast_to(marks[5:6, :LANES], square), 0.0
        ),
        axis=1,
        keepdims=True,
    )
    passed = (wanted == ids) & (place >= STATE_ROW) & (place < STATE_ROW + MIG)
    relay = jnp.dot(jnp.where(passed, 1.0, 0.0).astype(BF16), pool, preferred_element_type=F32)
    for d in range(groups):
        pass_ref[d] = relay[d * MIG : (d + 1) * MIG].astype(BF16)
    moved = items_ref[reqs : 2 * reqs, :] > 0.0
    moved_wide = jnp.concatenate([items_ref[reqs : 2 * reqs, :]] * (channels // LANES), axis=1) > 0.0
    needs = items_ref[:reqs, :]
    found = jnp.concatenate(
        [
            jnp.where(moved & (ids[:, at : at + LANES] == needs), 1.0, 0.0)
            for at in range(0, table, LANES)
        ],
        axis=1,
    )
    hist = []
    for j in range(3):
        hit = jnp.where((place >= 4 * j) & (place < 4 * j + 4), found, 0.0).astype(BF16)
        taken = jnp.dot(hit, pool, preferred_element_type=F32)
        hist.append(jnp.where(moved_wide, taken, conv_ref[j].astype(F32)))
    for l in range(channels // LANES):
        cols = slice(l * LANES, (l + 1) * LANES)
        taps = [cw_ref[k : k + 1, cols] for k in range(4)]
        bias = extra_ref[2:3, cols]
        window = [hist[j][:, cols] for j in range(3)]
        for t in range(steps):
            window.append(scr[l, pl.ds(t, reqs, stride=8), :])
            acc = bias
            for k in range(4):
                acc = acc + taps[k] * window[t + k]
            x_scr[t * reqs : (t + 1) * reqs, cols] = silu(acc)
    x = x_scr[...].astype(BF16)
    x_ref[...] = x
    low, sel = project(x, rank_ref, select_ref)
    prompt_groups = prompt_low_ref.shape[0] // 8
    pay_scr[...] = jnp.zeros(pay_scr.shape, F32)
    put_tiles(pay_scr, 0, prompt_low_ref[...], prompt_sel_ref[...])
    put_tiles(pay_scr, prompt_groups, low, sel)
    peers, blocks, four, _ = pay_ref.shape
    for j in range(peers):
        for a in range(blocks):
            pay_ref[j, a] = pay_scr[j, four * a : four * (a + 1), :].astype(BF16)


def sum_kernel(got_ref, out_ref):
    total = got_ref[0].astype(F32)
    for j in range(1, got_ref.shape[0]):
        total = total + got_ref[j].astype(F32)
    own_rows = total.astype(BF16)
    for j in range(out_ref.shape[0]):
        out_ref[j] = own_rows


def steps_of(low_scr, step_w_ref, step_b):
    low = low_scr[...]
    scale = lax.rsqrt(jnp.mean(low * low, axis=-1, keepdims=True) + EPS)
    raw = jnp.dot(low.astype(BF16), step_w_ref[...], preferred_element_type=F32)
    return softplus(raw * scale + step_b)


def scan(t, items, live, x, gate, sel, step, decay, skip, h_scr, y_scr, y_stride):
    states = decay.shape[1] // 8
    for g in range(items // 8):
        rows = slice(t * items + 8 * g, t * items + 8 * g + 8)
        alive = None if live is None else live[8 * g : 8 * g + 8]
        pair = sel[rows, :]
        lanes = range(h_scr.shape[0])
        steps, drive, y = [], [], []
        for l in lanes:
            cols = slice(l * LANES, (l + 1) * LANES)
            step_l = step[rows, cols]
            if alive is not None:
                step_l = jnp.where(alive, step_l, 0.0)
            x_l = x[rows, cols]
            steps.append(step_l)
            drive.append(step_l * x_l)
            y.append(skip[:, cols] * x_l)
        for n in range(states):
            b = jnp.broadcast_to(pair[:, n : n + 1], (8, LANES))
            c = jnp.broadcast_to(pair[:, states + n : states + n + 1], (8, LANES))
            at = slice(n * items + 8 * g, n * items + 8 * g + 8)
            for l in lanes:
                keep = jnp.exp2(steps[l] * decay[l, 8 * n : 8 * n + 8, :])
                h = keep * h_scr[l, at, :] + drive[l] * b
                h_scr[l, at, :] = h
                y[l] = y[l] + c * h
        for l in lanes:
            cols = slice(l * LANES, (l + 1) * LANES)
            out = y[l] * gate[rows, cols]
            if alive is not None:
                out = jnp.where(alive, out, 0.0)
            y_scr[l, pl.ds(8 * g * y_stride + t, 8, stride=y_stride), :] = out


def prefill_kernel(
    plan_ref, rows_ref, x_ref, gate_ref, step_w_ref, decay_ref, extra_ref, relay_ref,
    items_ref, _empty, out_ref, pay_ref, low_scr, sel_scr, step_scr, x_scr, h_scr, y_scr,
    final_scr, out_scr, plan_scr, sems,
):
    prompts, steps, channels = out_ref.shape
    states = decay_ref.shape[1] // 8
    reqs = plan_ref.shape[0] - 2 * prompts
    groups, blocks, four, _ = pay_ref.shape
    parts = states // four
    plan_copy = pltpu.make_async_copy(plan_ref, plan_scr, sems.at[0])
    plan_copy.start()
    passed = pltpu.make_async_copy(relay_ref, pay_ref.at[:, blocks - 1], sems.at[1])
    passed.start()
    take_tiles(rows_ref, 0, low_scr, sel_scr)
    step_scr[...] = steps_of(low_scr, step_w_ref, extra_ref[0:1, :])
    x_scr[...] = x_ref[...].astype(F32)
    h_scr[...] = jnp.zeros(h_scr.shape, F32)
    lengths = items_ref[2 * reqs :, :]
    skip = extra_ref[1:2, :]
    for t in range(steps):
        scan(
            t, prompts, t < lengths, x_scr, gate_ref, sel_scr, step_scr, decay_ref, skip, h_scr,
            y_scr, steps,
        )
    plan_copy.wait()
    dests, ranks = slots_of(plan_scr, prompts, reqs)
    passed.wait()
    copies = []
    for i in range(prompts):
        for l in range(channels // LANES):
            cols = slice(l * LANES, (l + 1) * LANES)
            for p in range(parts):
                final_scr[i, p, :, cols] = h_scr[
                    l, pl.ds(i + p * four * prompts, four, stride=prompts), :
                ].astype(BF16)
        place = pay_ref.at[dests[i], pl.ds(ranks[i] * parts, parts)]
        copies.append(pltpu.make_async_copy(final_scr.at[i], place, sems.at[2 + i]))
        copies[-1].start()
    for i in range(prompts):
        for l in range(channels // LANES):
            cols = slice(l * LANES, (l + 1) * LANES)
            out_scr[i, :, cols] = y_scr[l, i * steps : (i + 1) * steps, :].astype(BF16)
    copies.append(pltpu.make_async_copy(out_scr, out_ref, sems.at[2 + prompts]))
    copies[-1].start()
    for copy in copies:
        copy.wait()


def decode_scan_kernel(
    plan_ref, rows_ref, x_ref, u_ref, gate_ref, state_ref, step_w_ref, decay_ref, extra_ref,
    got_ref, out_ref, final_ref, base_ref, held_ref, weight_ref, keep_ref, pick_ref,
    final_conv_ref, prompt_conv_ref, low_scr, sel_scr, step_scr, x_scr, gate_scr, scr, h_scr, y_scr,
    conv_scr,
):
    reqs, steps, channels = gate_ref.shape
    states = state_ref.shape[1]
    lanes = channels // LANES
    own, picks = picks_of(plan_ref, reqs)
    take_tiles(rows_ref, PROMPT_GROUPS, low_scr, sel_scr)
    step_scr[...] = steps_of(low_scr, step_w_ref, extra_ref[0:1, :])
    x_scr[...] = x_ref[...].astype(F32)
    for r in range(reqs):
        put_lanes(scr, 8 * r, silu(gate_ref[r].astype(F32)))
        kept = plan_ref[r] == own * reqs + r
        for l in range(lanes):
            cols = slice(l * LANES, (l + 1) * LANES)
            h_scr[l, pl.ds(r, states, stride=reqs), :] = jnp.where(
                kept, state_ref[r, :, cols], 0.0
            )
    for l in range(lanes):
        cols = slice(l * LANES, (l + 1) * LANES)
        for t in range(steps):
            gate_scr[t * reqs : (t + 1) * reqs, cols] = scr[l, pl.ds(t, reqs, stride=8), :]
    skip = extra_ref[1:2, :]
    for t in range(steps):
        scan(t, reqs, None, x_scr, gate_scr, sel_scr, step_scr, decay_ref, skip, h_scr, y_scr, 8)
    for r in range(reqs):
        final_conv_ref[:, r : r + 1, :] = u_ref[r].astype(F32)[1:4].reshape(3, 1, channels)
        for l in range(lanes):
            cols = slice(l * LANES, (l + 1) * LANES)
            final_ref[r, :, cols] = h_scr[l, pl.ds(r, states, stride=reqs), :]
            out_ref[r, :, cols] = y_scr[l, 8 * r : 8 * r + steps, :].astype(BF16)
    outward = jnp.transpose(sel_scr[...])[states : 2 * states]
    column = iota(outward.shape, 1)
    for k in range(MIG):
        pick_ref[k : k + 1, :] = jnp.broadcast_to(picks[k], (1, LANES)).astype(F32)
        held_ref[k] = final_ref[picks[k]]
        total = jnp.zeros((1, channels), F32)
        for t in range(steps):
            row = t * reqs + picks[k]
            total = total + step_scr[pl.ds(row, 1), :]
            gate = gate_scr[pl.ds(row, 1), :]
            c = jnp.sum(jnp.where(column == row, outward, 0.0), axis=1, keepdims=True)
            for l in range(lanes):
                cols = slice(l * LANES, (l + 1) * LANES)
                keep = jnp.exp2(total[:, cols] * decay_ref[l, pl.ds(0, states, stride=8), :])
                weight_ref[k * steps + t, :, cols] = keep * c * gate[:, cols]
                base_ref[k * steps + t : k * steps + t + 1, cols] = y_scr[
                    l, pl.ds(8 * picks[k] + t, 1), :
                ]
                if t == steps - 1:
                    keep_ref[k, :, cols] = keep
    pick_ref[MIG:, :] = jnp.zeros((pick_ref.shape[0] - MIG, LANES), F32)
    for s in range(got_ref.shape[0]):
        block = got_ref[s].astype(F32)
        for q in range(PAIR):
            for j in range(3):
                at = TAIL_ROW + 3 * q + j
                conv_scr[j, s * PAIR + q : s * PAIR + q + 1, :] = block[at : at + 1]
    prompt_conv_ref[...] = conv_scr[...].astype(BF16)


def finish_kernel(
    got_ref, base_ref, held_ref, weight_ref, keep_ref, pick_ref, _out, _final, out_ref, final_ref,
    prompt_state_ref, state_scr, moved_scr, out_scr, final_scr, sems,
):
    groups, blocks, four, channels = got_ref.shape
    slots, states, _ = state_scr.shape
    steps = base_ref.shape[0] // MIG
    lanes = channels // LANES
    parts = states // four
    copies = []
    for s in range(groups):
        for q in range(PAIR):
            for p in range(parts):
                state_scr[s * PAIR + q, p * four : (p + 1) * four, :] = got_ref[
                    s, q * parts + p
                ].astype(F32)
        if s % 4 == 3:
            here = pl.ds((s - 3) * PAIR, 4 * PAIR)
            copies.append(
                pltpu.make_async_copy(state_scr.at[here], prompt_state_ref.at[here], sems.at[s])
            )
            copies[-1].start()
    for n in range(states):
        put_lanes(moved_scr, n * MIG, got_ref[n, blocks - 1].astype(F32))
    for k in range(MIG):
        pick = jnp.max(pick_ref[k : k + 1, :]).astype(jnp.int32)
        for l in range(lanes):
            cols = slice(l * LANES, (l + 1) * LANES)
            start = moved_scr[l, pl.ds(k, states, stride=MIG), :]
            final_scr[k, :, cols] = held_ref[k, :, cols] + keep_ref[k, :, cols] * start
            rows = []
            for t in range(steps):
                at = k * steps + t
                more = jnp.sum(weight_ref[at, :, cols] * start, axis=0, keepdims=True)
                rows.append(base_ref[at : at + 1, cols] + more)
            out_scr[k, :, cols] = jnp.concatenate(rows, axis=0).astype(BF16)
        copies.append(
            pltpu.make_async_copy(final_scr.at[k], final_ref.at[pick], sems.at[groups + k])
        )
        copies.append(
            pltpu.make_async_copy(out_scr.at[k], out_ref.at[pick], sems.at[groups + MIG + k])
        )
        copies[-2].start()
        copies[-1].start()
    for copy in copies:
        copy.wait()


def exchange(value, axis):
    return lax.all_to_all(value, axis, split_axis=0, concat_axis=0, tiled=True)


def on_device(
    resident_state,
    resident_conv,
    migrate_from,
    decode_inputs,
    decode_gates,
    prompt_inputs,
    prompt_gates,
    prompt_length,
    prompt_dest,
    conv_weight,
    conv_bias,
    rank_weight,
    select_weight,
    step_weight,
    step_bias,
    decay_log,
    skip_gain,
):
    groups = lax.axis_size("group")
    peers = lax.axis_size("mp")
    reqs, states, channels = resident_state.shape
    prompts, steps, _ = prompt_inputs.shape
    decode_steps = decode_inputs.shape[1]
    tiles = channels // LANES
    rank = rank_weight.shape[1]
    selects = select_weight.shape[1]
    prompt_rows = prompts * steps
    decode_rows = reqs * decode_steps
    bias_row = conv_bias.reshape(1, channels)
    step_bias_row = step_bias.reshape(1, channels)
    skip_row = skip_gain.reshape(1, channels)

    def struct(shape, dtype):
        return jax.ShapeDtypeStruct(shape, dtype)

    def scratch(shape):
        return pltpu.VMEM(shape, F32)

    def cost(flops, size):
        return pl.CostEstimate(flops=flops, bytes_accessed=size, transcendentals=0)

    anywhere = pl.BlockSpec(memory_space=pl.ANY)
    send_shape = (groups, PAIR * states // MIG + 1, MIG, channels)
    dest = prompt_dest.reshape(prompts)
    conv_rows = jnp.transpose(resident_conv, (1, 0, 2))
    select_rows = jnp.transpose(select_weight)

    send_first = pl.pallas_call(
        pack_kernel,
        out_shape=struct((groups, ROWS0, channels), BF16),
        in_specs=[SMEM] * 3 + [VMEM] * 3,
        out_specs=VMEM,
        scratch_shapes=[
            scratch((groups + 1, ROWS0, channels)),
            scratch((3 * reqs, channels)),
            scratch((prompts * (steps + 8), channels)),
        ],
        compiler_params=ALL_VMEM,
        name="pack",
    )(migrate_from, dest, prompt_length, conv_rows, resident_state, prompt_inputs)
    got_first = exchange(send_first, "group")

    prompt_low, prompt_sel, prompt_x, gate_rows, decay, extra, plan, items, empty = pl.pallas_call(
        prompt_kernel,
        out_shape=(
            struct((prompt_rows, rank), F32),
            struct((prompt_rows, selects), F32),
            struct((prompt_rows, channels), BF16),
            struct((prompt_rows, channels), F32),
            struct((tiles, 8 * states, LANES), F32),
            struct((8, channels), F32),
            struct((reqs + 2 * prompts,), jnp.int32),
            struct((2 * reqs + prompts, LANES), F32),
            struct(send_shape, BF16),
        ),
        in_specs=[SMEM] * 3 + [VMEM] * 9,
        out_specs=(VMEM,) * 6 + (SMEM, VMEM, anywhere),
        scratch_shapes=[
            scratch((tiles, prompt_rows, LANES)),
            scratch((prompt_rows, channels)),
            pltpu.VMEM(send_shape, BF16),
            pltpu.SemaphoreType.DMA,
        ],
        compiler_params=PARAMS,
        cost_estimate=cost(10**9, 2 * 10**6),
        name="prompt_features",
    )(
        migrate_from, dest, prompt_length, prompt_inputs, prompt_gates, conv_weight, bias_row,
        rank_weight, select_rows, decay_log, step_bias_row, skip_row,
    )

    pay, decode_x, relay = pl.pallas_call(
        decode_kernel,
        out_shape=(
            struct((peers, 7, 4, LANES), BF16),
            struct((decode_rows, channels), BF16),
            struct((groups, MIG, channels), BF16),
        ),
        in_specs=[VMEM] * 10,
        out_specs=(VMEM,) * 3,
        scratch_shapes=[
            scratch((groups * ROWS0, channels)),
            scratch((peers, 32, LANES)),
            scratch((tiles, reqs * 8, LANES)),
            scratch((decode_rows, channels)),
        ],
        compiler_params=PARAMS,
        name="decode_features",
    )(
        items, got_first, conv_rows, decode_inputs, conv_weight, extra, rank_weight, select_rows,
        prompt_low, prompt_sel,
    )

    parts = exchange(pay, "mp")
    shares = pl.pallas_call(
        sum_kernel,
        out_shape=struct(parts.shape, BF16),
        in_specs=[VMEM],
        out_specs=VMEM,
        compiler_params=PARAMS,
        name="sum_parts",
    )(parts)
    rows = exchange(shares, "mp")

    prefill_out, send_final = pl.pallas_call(
        prefill_kernel,
        out_shape=(
            struct(prompt_inputs.shape, BF16),
            struct(send_shape, BF16),
        ),
        in_specs=[anywhere] + [VMEM] * 8 + [anywhere],
        out_specs=(anywhere,) * 2,
        scratch_shapes=[
            scratch((prompt_rows, rank)),
            scratch((prompt_rows, LANES)),
            scratch((prompt_rows, channels)),
            scratch((prompt_rows, channels)),
            scratch((tiles, prompts * states, LANES)),
            scratch((tiles, prompt_rows, LANES)),
            pltpu.VMEM((prompts, states // MIG, MIG, channels), BF16),
            pltpu.VMEM(prompt_inputs.shape, BF16),
            pltpu.SMEM((reqs + 2 * prompts,), jnp.int32),
            pltpu.SemaphoreType.DMA((prompts + 3,)),
        ],
        input_output_aliases={9: 1},
        compiler_params=PARAMS,
        name="prefill_scan",
    )(plan, rows, prompt_x, gate_rows, step_weight, decay, extra, relay, items, empty)
    got_final = exchange(send_final, "group")

    early_out, early_final, base, held, weight, keep, pick, final_conv, prompt_conv = pl.pallas_call(
        decode_scan_kernel,
        out_shape=(
            struct(decode_inputs.shape, BF16),
            struct(resident_state.shape, F32),
            struct((MIG * decode_steps, channels), F32),
            struct((MIG, states, channels), F32),
            struct((MIG * decode_steps, states, channels), F32),
            struct((MIG, states, channels), F32),
            struct((8, LANES), F32),
            struct((3, reqs, channels), F32),
            struct((3, groups * PAIR, channels), BF16),
        ),
        in_specs=[SMEM] + [VMEM] * 9,
        out_specs=(VMEM,) * 9,
        scratch_shapes=[
            scratch((decode_rows, rank)),
            scratch((decode_rows, LANES)),
            scratch((decode_rows, channels)),
            scratch((decode_rows, channels)),
            scratch((decode_rows, channels)),
            scratch((tiles, reqs * 8, LANES)),
            scratch((tiles, reqs * states, LANES)),
            scratch((tiles, reqs * 8, LANES)),
            scratch((3, groups * PAIR, channels)),
        ],
        compiler_params=PARAMS,
        cost_estimate=cost(6 * 10**9, 8 * 10**6),
        name="decode_scan",
    )(
        plan, rows, decode_x, decode_inputs, decode_gates, resident_state, step_weight, decay,
        extra, got_first,
    )

    decode_out, final_state, prompt_state = pl.pallas_call(
        finish_kernel,
        out_shape=(
            struct(decode_inputs.shape, BF16),
            struct(resident_state.shape, F32),
            struct((groups * PAIR, states, channels), F32),
        ),
        in_specs=[VMEM] * 6 + [anywhere] * 2,
        out_specs=(anywhere,) * 3,
        scratch_shapes=[
            scratch((groups * PAIR, states, channels)),
            scratch((tiles, states * MIG, LANES)),
            pltpu.VMEM((MIG, decode_steps, channels), BF16),
            scratch((MIG, states, channels)),
            pltpu.SemaphoreType.DMA((groups + 2 * MIG,)),
        ],
        input_output_aliases={6: 0, 7: 1},
        compiler_params=PARAMS,
        name="finish",
    )(got_final, base, held, weight, keep, pick, early_out, early_final)
    final_conv = jnp.transpose(final_conv, (1, 0, 2)).astype(BF16)
    prompt_conv = jnp.transpose(prompt_conv, (1, 0, 2))
    return (decode_out, final_state, final_conv, prefill_out, prompt_state, prompt_conv)


def solution(mesh):
    whole = P("group", None, "mp")
    return jax.shard_map(
        on_device,
        mesh=mesh,
        in_specs=(
            whole,
            whole,
            P("group"),
            whole,
            whole,
            whole,
            whole,
            P("group"),
            P("group", None),
            P(None, "mp"),
            P("mp"),
            P("mp", None),
            P("mp", None),
            P(None, "mp"),
            P("mp"),
            P(None, "mp"),
            P("mp"),
        ),
        out_specs=(whole,) * 6,
        check_vma=False,
    )
```

```python
import jax
import jax.numpy as jnp
from jax import lax
from jax.experimental import pallas as pl
from jax.experimental.pallas import tpu as pltpu
from jax.sharding import PartitionSpec as P

MIG = 4
PAIR = 2
EPS = 1e-06
LANES = 128
ROWS0 = 24
PROMPT_GROUPS = 16
STATE_ROW = 14
TAIL_ROW = 18
LOG2E = 1.4426950408889634

F32 = jnp.float32
BF16 = jnp.bfloat16
VMEM = pl.BlockSpec(memory_space=pltpu.VMEM)
SMEM = pl.BlockSpec(memory_space=pltpu.SMEM)
PARAMS = pltpu.CompilerParams(vmem_limit_bytes=40 * 1024 * 1024)
ALL_VMEM = pltpu.CompilerParams(vmem_limit_bytes=60 * 1024 * 1024)


def silu(x):
    return x / (1.0 + jnp.exp(-x))


def softplus(x):
    return jnp.maximum(x, 0.0) + jnp.log1p(jnp.exp(-jnp.abs(x)))


def iota(shape, dim):
    return lax.broadcasted_iota(jnp.int32, shape, dim)


def from_scalars(ref, count, shape, first=0):
    rows = iota(shape, 0)
    out = jnp.zeros(shape, jnp.int32)
    for i in range(count):
        out = jnp.where(rows == i, ref[first + i], out)
    return out


def slots_of(dest_ref, count, first=0):
    dests = [dest_ref[first + i] for i in range(count)]
    ranks = []
    for i in range(count):
        rank = jnp.int32(0)
        for j in range(i):
            rank = rank + (dests[j] == dests[i]).astype(jnp.int32)
        ranks.append(rank)
    return dests, ranks


def picks_of(mig_ref, reqs):
    own = lax.axis_index("group")
    count = jnp.int32(0)
    picks = [jnp.int32(0) for _ in range(MIG)]
    for r in range(reqs):
        moved = mig_ref[r] != own * reqs + r
        for k in range(MIG):
            picks[k] = jnp.where(moved & (count == k), r, picks[k])
        count = count + moved.astype(jnp.int32)
    return own, picks


def pack_kernel(
    mig_hbm, dest_hbm, len_hbm, conv_hbm, state_hbm, u_hbm, pay_ref, mig_ref, dest_ref, len_ref,
    conv_ref, state_ref, u_ref, scr, conv_scr, u_scr, sems,
):
    pairs = (
        (mig_hbm, mig_ref), (conv_hbm, conv_ref), (state_hbm, state_ref), (u_hbm, u_ref),
        (dest_hbm, dest_ref), (len_hbm, len_ref),
    )
    copies = [pltpu.make_async_copy(a, b, sems.at[n]) for n, (a, b) in enumerate(pairs)]
    for copy in copies:
        copy.start()
    groups = pay_ref.shape[0]
    _, reqs, channels = conv_ref.shape
    prompts, steps, _ = u_ref.shape
    states = state_ref.shape[1]
    copies[0].wait()
    own, picks = picks_of(mig_ref, reqs)
    base = scr.at[groups]
    base[...] = jnp.zeros(base.shape, F32)
    lane = iota((1, channels), 1)
    ids = jnp.zeros((1, channels), jnp.int32)
    wanted = jnp.zeros((1, channels), jnp.int32)
    for copy in copies[1:]:
        copy.wait()
    for j in range(3):
        conv_scr[j * reqs : (j + 1) * reqs, :] = conv_ref[j].astype(F32)
    for k in range(MIG):
        for at in (k, 4 + k, 8 + k, STATE_ROW + k):
            ids = jnp.where(lane == own * ROWS0 + at, own * reqs + picks[k], ids)
        wanted = jnp.where(lane == own * MIG + k, mig_ref[picks[k]], wanted)
        for j in range(3):
            at = 4 * j + k
            base[at : at + 1, :] = conv_scr[pl.ds(j * reqs + picks[k], 1), :]
    base[12:13, :] = ids.astype(F32)
    base[13:14, :] = wanted.astype(F32)
    for d in range(groups):
        scr[d] = base[...]
    dests, ranks = slots_of(dest_ref, prompts)
    pad = u_scr.shape[0] // prompts
    for i in range(prompts):
        u_scr[i * pad : i * pad + 8, :] = jnp.zeros((8, channels), F32)
        u_scr[i * pad + 8 : i * pad + 8 + steps, :] = u_ref[i].astype(F32)
    for i in range(prompts):
        tails = [u_scr[pl.ds(i * pad + 5 + j + len_ref[i], 1), :] for j in range(3)]
        for q in range(PAIR):

            @pl.when(ranks[i] == q)
            def _():
                for j in range(3):
                    at = TAIL_ROW + 3 * q + j
                    scr[dests[i], at : at + 1, :] = tails[j]

    for k in range(MIG):
        state = state_ref[picks[k]]
        for n in range(states):
            scr[n, STATE_ROW + k : STATE_ROW + k + 1, :] = state[n : n + 1, :]
    for d in range(groups):
        pay_ref[d] = scr[d].astype(BF16)


def put_lanes(ref, start, value):
    for l in range(ref.shape[0]):
        ref[l, start : start + value.shape[0], :] = value[:, l * LANES : (l + 1) * LANES]


def project(x, rank_ref, select_ref):
    low = jnp.dot(x, rank_ref[...], preferred_element_type=F32)
    sel = lax.dot_general(
        x, select_ref[...], (((1,), (1,)), ((), ())), preferred_element_type=F32
    )
    return low, sel


def put_tiles(scr, first, low, sel):
    tiles = low.shape[1] // LANES
    width = sel.shape[1]
    share = LANES // width
    for g in range(low.shape[0] // 8):
        rows = slice(8 * g, 8 * g + 8)
        for l in range(tiles):
            owner, place = divmod((first + g) * tiles + l, 3)
            scr[owner, 8 * place : 8 * place + 8, :] = low[rows, l * LANES : (l + 1) * LANES]
        pair, place = divmod(first + g, share)
        cols = slice(place * width, (place + 1) * width)
        scr[2 * pair, 24:28, cols] = sel[8 * g : 8 * g + 4]
        scr[2 * pair + 1, 24:28, cols] = sel[8 * g + 4 : 8 * g + 8]


def take_tiles(rows_ref, first, low_scr, sel_scr):
    count, channels = low_scr.shape
    tiles = channels // LANES
    for g in range(count // 8):
        upper, lower = slice(8 * g, 8 * g + 4), slice(8 * g + 4, 8 * g + 8)
        for l in range(tiles):
            cols = slice(l * LANES, (l + 1) * LANES)
            owner, place = divmod((first + g) * tiles + l, 3)
            low_scr[upper, cols] = rows_ref[owner, 2 * place].astype(F32)
            low_scr[lower, cols] = rows_ref[owner, 2 * place + 1].astype(F32)
        pair, place = divmod(first + g, 4)
        sel_scr[upper, :] = rows_ref[2 * pair, 6].astype(F32)
        sel_scr[lower, :] = rows_ref[2 * pair + 1, 6].astype(F32)
    for g in range(count // 8):
        place = (first + g) % 4
        if place:
            rows = slice(8 * g, 8 * g + 8)
            sel_scr[rows, :] = pltpu.roll(sel_scr[rows, :], LANES - 32 * place, 1)


def prompt_kernel(
    mig_ref, dest_ref, len_ref, u_ref, gate_ref, cw_ref, cb_ref, rank_ref, select_ref, decay_ref,
    step_b_ref, skip_ref, low_ref, sel_ref, x_ref, gate_out_ref, decay_out_ref, extra_ref,
    plan_ref, items_ref, empty_ref, scr, x_scr, empty_scr, sem,
):
    prompts, steps, channels = u_ref.shape
    reqs = mig_ref.shape[0]
    empty_scr[...] = jnp.zeros(empty_scr.shape, BF16)
    empty = pltpu.make_async_copy(empty_scr, empty_ref, sem)
    empty.start()
    for i in range(reqs):
        plan_ref[i] = mig_ref[i]
    for i in range(prompts):
        plan_ref[reqs + i] = dest_ref[i]
        plan_ref[reqs + prompts + i] = len_ref[i]
    own = lax.axis_index("group")
    wanted = from_scalars(mig_ref, reqs, (reqs, LANES))
    moved = wanted != own * reqs + iota(wanted.shape, 0)
    items_ref[:reqs, :] = wanted.astype(F32)
    items_ref[reqs : 2 * reqs, :] = jnp.where(moved, 1.0, 0.0)
    items_ref[2 * reqs :, :] = from_scalars(len_ref, prompts, (prompts, LANES)).astype(F32)
    extra_ref[0:1, :] = step_b_ref[...]
    extra_ref[1:2, :] = skip_ref[...]
    extra_ref[2:3, :] = cb_ref[...]
    extra_ref[3:8, :] = jnp.zeros((5, channels), F32)
    decay = jnp.exp(decay_ref[...]) * -LOG2E
    for n in range(decay.shape[0]):
        put_lanes(decay_out_ref, 8 * n, jnp.broadcast_to(decay[n : n + 1], (8, channels)))
    for i in range(prompts):
        put_lanes(scr, i * steps, silu(gate_ref[i].astype(F32)))
    for l in range(channels // LANES):
        cols = slice(l * LANES, (l + 1) * LANES)
        for t in range(steps):
            gate_out_ref[t * prompts : (t + 1) * prompts, cols] = scr[
                l, pl.ds(t, prompts, stride=steps), :
            ]
    for i in range(prompts):
        put_lanes(scr, i * steps, u_ref[i].astype(F32))
    for l in range(channels // LANES):
        cols = slice(l * LANES, (l + 1) * LANES)
        taps = [cw_ref[k : k + 1, cols] for k in range(4)]
        bias = cb_ref[:, cols]
        window = [jnp.zeros((prompts, LANES), F32) for _ in range(3)]
        for t in range(steps):
            window.append(scr[l, pl.ds(t, prompts, stride=steps), :])
            acc = bias
            for k in range(4):
                acc = acc + taps[k] * window[t + k]
            x_scr[t * prompts : (t + 1) * prompts, cols] = silu(acc)
    x = x_scr[...].astype(BF16)
    x_ref[...] = x
    low, sel = project(x, rank_ref, select_ref)
    low_ref[...] = low
    sel_ref[...] = sel
    empty.wait()


def decode_kernel(
    items_ref, got_ref, conv_ref, u_ref, cw_ref, extra_ref, rank_ref, select_ref, prompt_low_ref,
    prompt_sel_ref, pay_ref, x_ref, pass_ref, pool_scr, pay_scr, scr, x_scr, pass_scr,
):
    groups = got_ref.shape[0]
    reqs, steps, channels = u_ref.shape
    table = groups * ROWS0
    marks = jnp.zeros((8, channels), F32)
    for s in range(groups):
        block = got_ref[s].astype(F32)
        pool_scr[s * ROWS0 : (s + 1) * ROWS0, :] = block
        marks = marks + block[8:16]
    for r in range(reqs):
        put_lanes(scr, 8 * r, u_ref[r].astype(F32))
    pool = pool_scr[...].astype(BF16)
    ids = marks[4:5, :table]
    place = lax.rem(iota((1, table), 1), ROWS0)
    moves = groups * MIG
    square = (moves, LANES)
    wanted = jnp.sum(
        jnp.where(
            iota(square, 0) == iota(square, 1), jnp.broadcast_to(marks[5:6, :LANES], square), 0.0
        ),
        axis=1,
        keepdims=True,
    )
    passed = (wanted == ids) & (place >= STATE_ROW) & (place < STATE_ROW + MIG)
    relay = jnp.dot(jnp.where(passed, 1.0, 0.0).astype(BF16), pool, preferred_element_type=F32)
    for d in range(groups):
        for l in range(channels // LANES):
            pass_scr[d, l * MIG : (l + 1) * MIG, :] = relay[
                d * MIG : (d + 1) * MIG, l * LANES : (l + 1) * LANES
            ]
    pass_ref[...] = pass_scr[...].astype(BF16)
    moved = items_ref[reqs : 2 * reqs, :] > 0.0
    moved_wide = jnp.concatenate([items_ref[reqs : 2 * reqs, :]] * (channels // LANES), axis=1) > 0.0
    needs = items_ref[:reqs, :]
    found = jnp.concatenate(
        [
            jnp.where(moved & (ids[:, at : at + LANES] == needs), 1.0, 0.0)
            for at in range(0, table, LANES)
        ],
        axis=1,
    )
    hist = []
    for j in range(3):
        hit = jnp.where((place >= 4 * j) & (place < 4 * j + 4), found, 0.0).astype(BF16)
        taken = jnp.dot(hit, pool, preferred_element_type=F32)
        hist.append(jnp.where(moved_wide, taken, conv_ref[j].astype(F32)))
    for l in range(channels // LANES):
        cols = slice(l * LANES, (l + 1) * LANES)
        taps = [cw_ref[k : k + 1, cols] for k in range(4)]
        bias = extra_ref[2:3, cols]
        window = [hist[j][:, cols] for j in range(3)]
        for t in range(steps):
            window.append(scr[l, pl.ds(t, reqs, stride=8), :])
            acc = bias
            for k in range(4):
                acc = acc + taps[k] * window[t + k]
            x_scr[t * reqs : (t + 1) * reqs, cols] = silu(acc)
    x = x_scr[...].astype(BF16)
    x_ref[...] = x
    low, sel = project(x, rank_ref, select_ref)
    prompt_groups = prompt_low_ref.shape[0] // 8
    pay_scr[...] = jnp.zeros(pay_scr.shape, F32)
    put_tiles(pay_scr, 0, prompt_low_ref[...], prompt_sel_ref[...])
    put_tiles(pay_scr, prompt_groups, low, sel)
    peers, blocks, four, _ = pay_ref.shape
    for j in range(peers):
        for a in range(blocks):
            pay_ref[j, a] = pay_scr[j, four * a : four * (a + 1), :].astype(BF16)


def sum_kernel(got_ref, out_ref):
    total = got_ref[0].astype(F32)
    for j in range(1, got_ref.shape[0]):
        total = total + got_ref[j].astype(F32)
    own_rows = total.astype(BF16)
    for j in range(out_ref.shape[0]):
        out_ref[j] = own_rows


def steps_of(low_scr, step_w_ref, step_b):
    low = low_scr[...]
    scale = lax.rsqrt(jnp.mean(low * low, axis=-1, keepdims=True) + EPS)
    raw = jnp.dot(low.astype(BF16), step_w_ref[...], preferred_element_type=F32)
    return softplus(raw * scale + step_b)


def scan(t, items, live, x, gate, sel, step, decay, skip, h_scr, y_scr, y_stride):
    states = decay.shape[1] // 8
    for g in range(items // 8):
        rows = slice(t * items + 8 * g, t * items + 8 * g + 8)
        alive = None if live is None else live[8 * g : 8 * g + 8]
        pair = sel[rows, :]
        lanes = range(h_scr.shape[0])
        steps, drive, y = [], [], []
        for l in lanes:
            cols = slice(l * LANES, (l + 1) * LANES)
            step_l = step[rows, cols]
            if alive is not None:
                step_l = jnp.where(alive, step_l, 0.0)
            x_l = x[rows, cols]
            steps.append(step_l)
            drive.append(step_l * x_l)
            y.append(skip[:, cols] * x_l)
        for n in range(states):
            b = jnp.broadcast_to(pair[:, n : n + 1], (8, LANES))
            c = jnp.broadcast_to(pair[:, states + n : states + n + 1], (8, LANES))
            at = slice(n * items + 8 * g, n * items + 8 * g + 8)
            for l in lanes:
                keep = jnp.exp2(steps[l] * decay[l, 8 * n : 8 * n + 8, :])
                h = keep * h_scr[l, at, :] + drive[l] * b
                h_scr[l, at, :] = h
                y[l] = y[l] + c * h
        for l in lanes:
            cols = slice(l * LANES, (l + 1) * LANES)
            out = y[l] * gate[rows, cols]
            if alive is not None:
                out = jnp.where(alive, out, 0.0)
            y_scr[l, pl.ds(8 * g * y_stride + t, 8, stride=y_stride), :] = out


def prefill_kernel(
    plan_ref, rows_ref, x_ref, gate_ref, step_w_ref, decay_ref, extra_ref, relay_ref,
    items_ref, _empty, out_ref, pay_ref, low_scr, sel_scr, step_scr, x_scr, h_scr, y_scr,
    final_scr, out_scr, plan_scr, sems,
):
    prompts, steps, channels = out_ref.shape
    states = decay_ref.shape[1] // 8
    reqs = plan_ref.shape[0] - 2 * prompts
    lanes = channels // LANES
    slot_rows = lanes * states
    passing = pay_ref.at[:, pl.ds(PAIR * slot_rows, MIG * lanes)]
    plan_copy = pltpu.make_async_copy(plan_ref, plan_scr, sems.at[0])
    plan_copy.start()
    passed = pltpu.make_async_copy(relay_ref, passing, sems.at[1])
    passed.start()
    take_tiles(rows_ref, 0, low_scr, sel_scr)
    step_scr[...] = steps_of(low_scr, step_w_ref, extra_ref[0:1, :])
    x_scr[...] = x_ref[...].astype(F32)
    h_scr[...] = jnp.zeros(h_scr.shape, F32)
    lengths = items_ref[2 * reqs :, :]
    skip = extra_ref[1:2, :]
    for t in range(steps):
        scan(
            t, prompts, t < lengths, x_scr, gate_ref, sel_scr, step_scr, decay_ref, skip, h_scr,
            y_scr, steps,
        )
    plan_copy.wait()
    dests, ranks = slots_of(plan_scr, prompts, reqs)
    passed.wait()
    copies = []
    for i in range(prompts):
        for l in range(lanes):
            final_scr[i, l * states : (l + 1) * states, :] = h_scr[
                l, pl.ds(i, states, stride=prompts), :
            ].astype(BF16)
        first = pl.multiple_of(ranks[i] * slot_rows, slot_rows)
        place = pay_ref.at[dests[i], pl.ds(first, slot_rows)]
        copies.append(pltpu.make_async_copy(final_scr.at[i], place, sems.at[2 + i]))
        copies[-1].start()
    for i in range(prompts):
        for l in range(channels // LANES):
            cols = slice(l * LANES, (l + 1) * LANES)
            out_scr[i, :, cols] = y_scr[l, i * steps : (i + 1) * steps, :].astype(BF16)
    copies.append(pltpu.make_async_copy(out_scr, out_ref, sems.at[2 + prompts]))
    copies[-1].start()
    for copy in copies:
        copy.wait()


def decode_scan_kernel(
    plan_ref, rows_ref, x_ref, u_ref, gate_ref, state_ref, step_w_ref, decay_ref, extra_ref,
    got_ref, out_ref, final_ref, base_ref, held_ref, weight_ref, keep_ref, pick_ref,
    final_conv_ref, prompt_conv_ref, low_scr, sel_scr, step_scr, x_scr, gate_scr, scr, h_scr, y_scr,
    conv_scr,
):
    reqs, steps, channels = gate_ref.shape
    states = state_ref.shape[1]
    lanes = channels // LANES
    own, picks = picks_of(plan_ref, reqs)
    take_tiles(rows_ref, PROMPT_GROUPS, low_scr, sel_scr)
    step_scr[...] = steps_of(low_scr, step_w_ref, extra_ref[0:1, :])
    x_scr[...] = x_ref[...].astype(F32)
    for r in range(reqs):
        put_lanes(scr, 8 * r, silu(gate_ref[r].astype(F32)))
        kept = plan_ref[r] == own * reqs + r
        for l in range(lanes):
            cols = slice(l * LANES, (l + 1) * LANES)
            h_scr[l, pl.ds(r, states, stride=reqs), :] = jnp.where(
                kept, state_ref[r, :, cols], 0.0
            )
    for l in range(lanes):
        cols = slice(l * LANES, (l + 1) * LANES)
        for t in range(steps):
            gate_scr[t * reqs : (t + 1) * reqs, cols] = scr[l, pl.ds(t, reqs, stride=8), :]
    skip = extra_ref[1:2, :]
    for t in range(steps):
        scan(t, reqs, None, x_scr, gate_scr, sel_scr, step_scr, decay_ref, skip, h_scr, y_scr, 8)
    for r in range(reqs):
        final_conv_ref[:, r : r + 1, :] = u_ref[r].astype(F32)[1:4].reshape(3, 1, channels)
        for l in range(lanes):
            cols = slice(l * LANES, (l + 1) * LANES)
            final_ref[r, :, cols] = h_scr[l, pl.ds(r, states, stride=reqs), :]
            out_ref[r, :, cols] = y_scr[l, 8 * r : 8 * r + steps, :].astype(BF16)
    outward = jnp.transpose(sel_scr[...])[states : 2 * states]
    column = iota(outward.shape, 1)
    for k in range(MIG):
        pick_ref[k : k + 1, :] = jnp.broadcast_to(picks[k], (1, LANES)).astype(F32)
        held_ref[k] = final_ref[picks[k]]
        total = jnp.zeros((1, channels), F32)
        for t in range(steps):
            row = t * reqs + picks[k]
            total = total + step_scr[pl.ds(row, 1), :]
            gate = gate_scr[pl.ds(row, 1), :]
            c = jnp.sum(jnp.where(column == row, outward, 0.0), axis=1, keepdims=True)
            for l in range(lanes):
                cols = slice(l * LANES, (l + 1) * LANES)
                keep = jnp.exp2(total[:, cols] * decay_ref[l, pl.ds(0, states, stride=8), :])
                weight_ref[k * steps + t, :, cols] = keep * c * gate[:, cols]
                base_ref[k * steps + t : k * steps + t + 1, cols] = y_scr[
                    l, pl.ds(8 * picks[k] + t, 1), :
                ]
                if t == steps - 1:
                    keep_ref[k, :, cols] = keep
    pick_ref[MIG:, :] = jnp.zeros((pick_ref.shape[0] - MIG, LANES), F32)
    for s in range(got_ref.shape[0]):
        block = got_ref[s].astype(F32)
        for q in range(PAIR):
            for j in range(3):
                at = TAIL_ROW + 3 * q + j
                conv_scr[j, s * PAIR + q : s * PAIR + q + 1, :] = block[at : at + 1]
    prompt_conv_ref[...] = conv_scr[...].astype(BF16)


def finish_kernel(
    got_ref, base_ref, held_ref, weight_ref, keep_ref, pick_ref, _out, _final, out_ref, final_ref,
    prompt_state_ref, state_scr, moved_scr, out_scr, final_scr, sems,
):
    groups = got_ref.shape[0]
    slots, states, channels = state_scr.shape
    steps = base_ref.shape[0] // MIG
    lanes = channels // LANES
    copies = []
    for s in range(groups):
        for q in range(PAIR):
            for l in range(lanes):
                at = (q * lanes + l) * states
                state_scr[s * PAIR + q, :, l * LANES : (l + 1) * LANES] = got_ref[
                    s, at : at + states, :
                ].astype(F32)
        if s % 4 == 3:
            here = pl.ds((s - 3) * PAIR, 4 * PAIR)
            copies.append(
                pltpu.make_async_copy(state_scr.at[here], prompt_state_ref.at[here], sems.at[s])
            )
            copies[-1].start()
    for n in range(states):
        arrived = got_ref[n, PAIR * lanes * states :, :].astype(F32)
        for l in range(lanes):
            moved_scr[l, n * MIG : (n + 1) * MIG, :] = arrived[l * MIG : (l + 1) * MIG]
    for k in range(MIG):
        pick = jnp.max(pick_ref[k : k + 1, :]).astype(jnp.int32)
        for l in range(lanes):
            cols = slice(l * LANES, (l + 1) * LANES)
            start = moved_scr[l, pl.ds(k, states, stride=MIG), :]
            final_scr[k, :, cols] = held_ref[k, :, cols] + keep_ref[k, :, cols] * start
            rows = []
            for t in range(steps):
                at = k * steps + t
                more = jnp.sum(weight_ref[at, :, cols] * start, axis=0, keepdims=True)
                rows.append(base_ref[at : at + 1, cols] + more)
            out_scr[k, :, cols] = jnp.concatenate(rows, axis=0).astype(BF16)
        copies.append(
            pltpu.make_async_copy(final_scr.at[k], final_ref.at[pick], sems.at[groups + k])
        )
        copies.append(
            pltpu.make_async_copy(out_scr.at[k], out_ref.at[pick], sems.at[groups + MIG + k])
        )
        copies[-2].start()
        copies[-1].start()
    for copy in copies:
        copy.wait()


def exchange(value, axis):
    return lax.all_to_all(value, axis, split_axis=0, concat_axis=0, tiled=True)


def on_device(
    resident_state,
    resident_conv,
    migrate_from,
    decode_inputs,
    decode_gates,
    prompt_inputs,
    prompt_gates,
    prompt_length,
    prompt_dest,
    conv_weight,
    conv_bias,
    rank_weight,
    select_weight,
    step_weight,
    step_bias,
    decay_log,
    skip_gain,
):
    groups = lax.axis_size("group")
    peers = lax.axis_size("mp")
    reqs, states, channels = resident_state.shape
    prompts, steps, _ = prompt_inputs.shape
    decode_steps = decode_inputs.shape[1]
    tiles = channels // LANES
    rank = rank_weight.shape[1]
    selects = select_weight.shape[1]
    prompt_rows = prompts * steps
    decode_rows = reqs * decode_steps
    bias_row = conv_bias.reshape(1, channels)
    step_bias_row = step_bias.reshape(1, channels)
    skip_row = skip_gain.reshape(1, channels)

    def struct(shape, dtype):
        return jax.ShapeDtypeStruct(shape, dtype)

    def scratch(shape):
        return pltpu.VMEM(shape, F32)

    def cost(flops, size):
        return pl.CostEstimate(flops=flops, bytes_accessed=size, transcendentals=0)

    anywhere = pl.BlockSpec(memory_space=pl.ANY)
    send_shape = (groups, (PAIR * states + MIG) * tiles, LANES)
    dest = prompt_dest.reshape(prompts)
    conv_rows = jnp.transpose(resident_conv, (1, 0, 2))
    select_rows = jnp.transpose(select_weight)

    send_first = pl.pallas_call(
        pack_kernel,
        out_shape=struct((groups, ROWS0, channels), BF16),
        in_specs=[anywhere] * 6,
        out_specs=VMEM,
        scratch_shapes=[
            pltpu.SMEM((reqs,), jnp.int32),
            pltpu.SMEM((prompts,), jnp.int32),
            pltpu.SMEM((prompts,), jnp.int32),
            pltpu.VMEM((3, reqs, channels), BF16),
            scratch((reqs, states, channels)),
            pltpu.VMEM((prompts, steps, channels), BF16),
            scratch((groups + 1, ROWS0, channels)),
            scratch((3 * reqs, channels)),
            scratch((prompts * (steps + 8), channels)),
            pltpu.SemaphoreType.DMA((6,)),
        ],
        compiler_params=ALL_VMEM,
        name="pack",
    )(migrate_from, dest, prompt_length, conv_rows, resident_state, prompt_inputs)
    got_first = exchange(send_first, "group")

    prompt_low, prompt_sel, prompt_x, gate_rows, decay, extra, plan, items, empty = pl.pallas_call(
        prompt_kernel,
        out_shape=(
            struct((prompt_rows, rank), F32),
            struct((prompt_rows, selects), F32),
            struct((prompt_rows, channels), BF16),
            struct((prompt_rows, channels), F32),
            struct((tiles, 8 * states, LANES), F32),
            struct((8, channels), F32),
            struct((reqs + 2 * prompts,), jnp.int32),
            struct((2 * reqs + prompts, LANES), F32),
            struct(send_shape, BF16),
        ),
        in_specs=[SMEM] * 3 + [VMEM] * 9,
        out_specs=(VMEM,) * 6 + (SMEM, VMEM, anywhere),
        scratch_shapes=[
            scratch((tiles, prompt_rows, LANES)),
            scratch((prompt_rows, channels)),
            pltpu.VMEM(send_shape, BF16),
            pltpu.SemaphoreType.DMA,
        ],
        compiler_params=PARAMS,
        cost_estimate=cost(10**9, 2 * 10**6),
        name="prompt_features",
    )(
        migrate_from, dest, prompt_length, prompt_inputs, prompt_gates, conv_weight, bias_row,
        rank_weight, select_rows, decay_log, step_bias_row, skip_row,
    )

    pay, decode_x, relay = pl.pallas_call(
        decode_kernel,
        out_shape=(
            struct((peers, 7, 4, LANES), BF16),
            struct((decode_rows, channels), BF16),
            struct((groups, MIG * tiles, LANES), BF16),
        ),
        in_specs=[VMEM] * 10,
        out_specs=(VMEM,) * 3,
        scratch_shapes=[
            scratch((groups * ROWS0, channels)),
            scratch((peers, 32, LANES)),
            scratch((tiles, reqs * 8, LANES)),
            scratch((decode_rows, channels)),
            scratch((groups, MIG * tiles, LANES)),
        ],
        compiler_params=PARAMS,
        name="decode_features",
    )(
        items, got_first, conv_rows, decode_inputs, conv_weight, extra, rank_weight, select_rows,
        prompt_low, prompt_sel,
    )

    parts = exchange(pay, "mp")
    shares = pl.pallas_call(
        sum_kernel,
        out_shape=struct(parts.shape, BF16),
        in_specs=[VMEM],
        out_specs=VMEM,
        compiler_params=PARAMS,
        name="sum_parts",
    )(parts)
    rows = exchange(shares, "mp")

    prefill_out, send_final = pl.pallas_call(
        prefill_kernel,
        out_shape=(
            struct(prompt_inputs.shape, BF16),
            struct(send_shape, BF16),
        ),
        in_specs=[anywhere] + [VMEM] * 8 + [anywhere],
        out_specs=(anywhere,) * 2,
        scratch_shapes=[
            scratch((prompt_rows, rank)),
            scratch((prompt_rows, LANES)),
            scratch((prompt_rows, channels)),
            scratch((prompt_rows, channels)),
            scratch((tiles, prompts * states, LANES)),
            scratch((tiles, prompt_rows, LANES)),
            pltpu.VMEM((prompts, tiles * states, LANES), BF16),
            pltpu.VMEM(prompt_inputs.shape, BF16),
            pltpu.SMEM((reqs + 2 * prompts,), jnp.int32),
            pltpu.SemaphoreType.DMA((prompts + 3,)),
        ],
        input_output_aliases={9: 1},
        compiler_params=PARAMS,
        name="prefill_scan",
    )(plan, rows, prompt_x, gate_rows, step_weight, decay, extra, relay, items, empty)
    got_final = exchange(send_final, "group")

    early_out, early_final, base, held, weight, keep, pick, final_conv, prompt_conv = pl.pallas_call(
        decode_scan_kernel,
        out_shape=(
            struct(decode_inputs.shape, BF16),
            struct(resident_state.shape, F32),
            struct((MIG * decode_steps, channels), F32),
            struct((MIG, states, channels), F32),
            struct((MIG * decode_steps, states, channels), F32),
            struct((MIG, states, channels), F32),
            struct((8, LANES), F32),
            struct((3, reqs, channels), F32),
            struct((3, groups * PAIR, channels), BF16),
        ),
        in_specs=[SMEM] + [VMEM] * 9,
        out_specs=(VMEM,) * 9,
        scratch_shapes=[
            scratch((decode_rows, rank)),
            scratch((decode_rows, LANES)),
            scratch((decode_rows, channels)),
            scratch((decode_rows, channels)),
            scratch((decode_rows, channels)),
            scratch((tiles, reqs * 8, LANES)),
            scratch((tiles, reqs * states, LANES)),
            scratch((tiles, reqs * 8, LANES)),
            scratch((3, groups * PAIR, channels)),
        ],
        compiler_params=PARAMS,
        cost_estimate=cost(6 * 10**9, 8 * 10**6),
        name="decode_scan",
    )(
        plan, rows, decode_x, decode_inputs, decode_gates, resident_state, step_weight, decay,
        extra, got_first,
    )

    decode_out, final_state, prompt_state = pl.pallas_call(
        finish_kernel,
        out_shape=(
            struct(decode_inputs.shape, BF16),
            struct(resident_state.shape, F32),
            struct((groups * PAIR, states, channels), F32),
        ),
        in_specs=[VMEM] * 6 + [anywhere] * 2,
        out_specs=(anywhere,) * 3,
        scratch_shapes=[
            scratch((groups * PAIR, states, channels)),
            scratch((tiles, states * MIG, LANES)),
            pltpu.VMEM((MIG, decode_steps, channels), BF16),
            scratch((MIG, states, channels)),
            pltpu.SemaphoreType.DMA((groups + 2 * MIG,)),
        ],
        input_output_aliases={6: 0, 7: 1},
        compiler_params=PARAMS,
        name="finish",
    )(got_final, base, held, weight, keep, pick, early_out, early_final)
    final_conv = jnp.transpose(final_conv, (1, 0, 2)).astype(BF16)
    prompt_conv = jnp.transpose(prompt_conv, (1, 0, 2))
    return (decode_out, final_state, final_conv, prefill_out, prompt_state, prompt_conv)


def solution(mesh):
    whole = P("group", None, "mp")
    return jax.shard_map(
        on_device,
        mesh=mesh,
        in_specs=(
            whole,
            whole,
            P("group"),
            whole,
            whole,
            whole,
            whole,
            P("group"),
            P("group", None),
            P(None, "mp"),
            P("mp"),
            P("mp", None),
            P("mp", None),
            P(None, "mp"),
            P("mp"),
            P(None, "mp"),
            P("mp"),
        ),
        out_specs=(whole,) * 6,
        check_vma=False,
    )
```

```python
import jax
import jax.numpy as jnp
from jax import lax
from jax.experimental import pallas as pl
from jax.experimental.pallas import tpu as pltpu
from jax.sharding import PartitionSpec as P

MIG = 4
PAIR = 2
EPS = 1e-06
LANES = 128
ROWS0 = 24
PROMPT_GROUPS = 16
STATE_ROW = 14
TAIL_ROW = 18
LOG2E = 1.4426950408889634

F32 = jnp.float32
BF16 = jnp.bfloat16
VMEM = pl.BlockSpec(memory_space=pltpu.VMEM)
SMEM = pl.BlockSpec(memory_space=pltpu.SMEM)
PARAMS = pltpu.CompilerParams(vmem_limit_bytes=40 * 1024 * 1024)
ALL_VMEM = pltpu.CompilerParams(vmem_limit_bytes=60 * 1024 * 1024)


def silu(x):
    return x / (1.0 + jnp.exp(-x))


def softplus(x):
    return jnp.maximum(x, 0.0) + jnp.log1p(jnp.exp(-jnp.abs(x)))


def iota(shape, dim):
    return lax.broadcasted_iota(jnp.int32, shape, dim)


def from_scalars(ref, count, shape, first=0):
    rows = iota(shape, 0)
    out = jnp.zeros(shape, jnp.int32)
    for i in range(count):
        out = jnp.where(rows == i, ref[first + i], out)
    return out


def slots_of(dest_ref, count, first=0):
    dests = [dest_ref[first + i] for i in range(count)]
    ranks = []
    for i in range(count):
        rank = jnp.int32(0)
        for j in range(i):
            rank = rank + (dests[j] == dests[i]).astype(jnp.int32)
        ranks.append(rank)
    return dests, ranks


def picks_of(mig_ref, reqs):
    own = lax.axis_index("group")
    count = jnp.int32(0)
    picks = [jnp.int32(0) for _ in range(MIG)]
    for r in range(reqs):
        moved = mig_ref[r] != own * reqs + r
        for k in range(MIG):
            picks[k] = jnp.where(moved & (count == k), r, picks[k])
        count = count + moved.astype(jnp.int32)
    return own, picks


def pack_kernel(
    mig_ref, dest_ref, len_ref, conv_ref, state_ref, u_ref, pay_ref, scr, conv_scr, u_scr, out_scr,
    sems,
):
    groups = pay_ref.shape[0]
    _, reqs, channels = conv_ref.shape
    prompts, steps, _ = u_ref.shape
    states = state_ref.shape[1]
    own, picks = picks_of(mig_ref, reqs)
    base = scr.at[groups]
    base[...] = jnp.zeros(base.shape, F32)
    lane = iota((1, channels), 1)
    ids = jnp.zeros((1, channels), jnp.int32)
    wanted = jnp.zeros((1, channels), jnp.int32)
    for j in range(3):
        conv_scr[j * reqs : (j + 1) * reqs, :] = conv_ref[j].astype(F32)
    for k in range(MIG):
        for at in (k, 4 + k, 8 + k, STATE_ROW + k):
            ids = jnp.where(lane == own * ROWS0 + at, own * reqs + picks[k], ids)
        wanted = jnp.where(lane == own * MIG + k, mig_ref[picks[k]], wanted)
        for j in range(3):
            at = 4 * j + k
            base[at : at + 1, :] = conv_scr[pl.ds(j * reqs + picks[k], 1), :]
    base[12:13, :] = ids.astype(F32)
    base[13:14, :] = wanted.astype(F32)
    for d in range(groups):
        scr[d] = base[...]
    dests, ranks = slots_of(dest_ref, prompts)
    pad = u_scr.shape[0] // prompts
    for i in range(prompts):
        u_scr[i * pad : i * pad + 8, :] = jnp.zeros((8, channels), F32)
        u_scr[i * pad + 8 : i * pad + 8 + steps, :] = u_ref[i].astype(F32)
    for i in range(prompts):
        tails = [u_scr[pl.ds(i * pad + 5 + j + len_ref[i], 1), :] for j in range(3)]
        for q in range(PAIR):

            @pl.when(ranks[i] == q)
            def _():
                for j in range(3):
                    at = TAIL_ROW + 3 * q + j
                    scr[dests[i], at : at + 1, :] = tails[j]

    for k in range(MIG):
        state = state_ref[picks[k]]
        for n in range(states):
            scr[n, STATE_ROW + k : STATE_ROW + k + 1, :] = state[n : n + 1, :]
    copies = []
    for d in range(groups):
        out_scr[d] = scr[d].astype(BF16)
        if d % 4 == 3:
            here = pl.ds(d - 3, 4)
            copies.append(
                pltpu.make_async_copy(out_scr.at[here], pay_ref.at[here], sems.at[d // 4])
            )
            copies[-1].start()
    for copy in copies:
        copy.wait()


def put_lanes(ref, start, value):
    for l in range(ref.shape[0]):
        ref[l, start : start + value.shape[0], :] = value[:, l * LANES : (l + 1) * LANES]


def project(x, rank_ref, select_ref):
    low = jnp.dot(x, rank_ref[...], preferred_element_type=F32)
    sel = lax.dot_general(
        x, select_ref[...], (((1,), (1,)), ((), ())), preferred_element_type=F32
    )
    return low, sel


def put_tiles(scr, first, low, sel):
    tiles = low.shape[1] // LANES
    width = sel.shape[1]
    share = LANES // width
    for g in range(low.shape[0] // 8):
        rows = slice(8 * g, 8 * g + 8)
        for l in range(tiles):
            owner, place = divmod((first + g) * tiles + l, 3)
            scr[owner, 8 * place : 8 * place + 8, :] = low[rows, l * LANES : (l + 1) * LANES]
        pair, place = divmod(first + g, share)
        cols = slice(place * width, (place + 1) * width)
        scr[2 * pair, 24:28, cols] = sel[8 * g : 8 * g + 4]
        scr[2 * pair + 1, 24:28, cols] = sel[8 * g + 4 : 8 * g + 8]


def take_tiles(rows_ref, first, low_scr, sel_scr):
    count, channels = low_scr.shape
    tiles = channels // LANES
    for g in range(count // 8):
        upper, lower = slice(8 * g, 8 * g + 4), slice(8 * g + 4, 8 * g + 8)
        for l in range(tiles):
            cols = slice(l * LANES, (l + 1) * LANES)
            owner, place = divmod((first + g) * tiles + l, 3)
            low_scr[upper, cols] = rows_ref[owner, 2 * place].astype(F32)
            low_scr[lower, cols] = rows_ref[owner, 2 * place + 1].astype(F32)
        pair, place = divmod(first + g, 4)
        sel_scr[upper, :] = rows_ref[2 * pair, 6].astype(F32)
        sel_scr[lower, :] = rows_ref[2 * pair + 1, 6].astype(F32)
    for g in range(count // 8):
        place = (first + g) % 4
        if place:
            rows = slice(8 * g, 8 * g + 8)
            sel_scr[rows, :] = pltpu.roll(sel_scr[rows, :], LANES - 32 * place, 1)


def prompt_kernel(
    mig_ref, dest_ref, len_ref, u_ref, gate_ref, cw_ref, cb_ref, rank_ref, select_ref, decay_ref,
    step_b_ref, skip_ref, low_ref, sel_ref, x_ref, gate_out_ref, decay_out_ref, extra_ref,
    plan_ref, items_ref, empty_ref, scr, x_scr, empty_scr, sem,
):
    prompts, steps, channels = u_ref.shape
    reqs = mig_ref.shape[0]
    empty_scr[...] = jnp.zeros(empty_scr.shape, BF16)
    empty = pltpu.make_async_copy(empty_scr, empty_ref, sem)
    empty.start()
    for i in range(reqs):
        plan_ref[i] = mig_ref[i]
    for i in range(prompts):
        plan_ref[reqs + i] = dest_ref[i]
        plan_ref[reqs + prompts + i] = len_ref[i]
    own = lax.axis_index("group")
    wanted = from_scalars(mig_ref, reqs, (reqs, LANES))
    moved = wanted != own * reqs + iota(wanted.shape, 0)
    items_ref[:reqs, :] = wanted.astype(F32)
    items_ref[reqs : 2 * reqs, :] = jnp.where(moved, 1.0, 0.0)
    items_ref[2 * reqs :, :] = from_scalars(len_ref, prompts, (prompts, LANES)).astype(F32)
    extra_ref[0:1, :] = step_b_ref[...]
    extra_ref[1:2, :] = skip_ref[...]
    extra_ref[2:3, :] = cb_ref[...]
    extra_ref[3:8, :] = jnp.zeros((5, channels), F32)
    decay = jnp.exp(decay_ref[...]) * -LOG2E
    for n in range(decay.shape[0]):
        put_lanes(decay_out_ref, 8 * n, jnp.broadcast_to(decay[n : n + 1], (8, channels)))
    for i in range(prompts):
        put_lanes(scr, i * steps, silu(gate_ref[i].astype(F32)))
    for l in range(channels // LANES):
        cols = slice(l * LANES, (l + 1) * LANES)
        for t in range(steps):
            gate_out_ref[t * prompts : (t + 1) * prompts, cols] = scr[
                l, pl.ds(t, prompts, stride=steps), :
            ]
    for i in range(prompts):
        put_lanes(scr, i * steps, u_ref[i].astype(F32))
    for l in range(channels // LANES):
        cols = slice(l * LANES, (l + 1) * LANES)
        taps = [cw_ref[k : k + 1, cols] for k in range(4)]
        bias = cb_ref[:, cols]
        window = [jnp.zeros((prompts, LANES), F32) for _ in range(3)]
        for t in range(steps):
            window.append(scr[l, pl.ds(t, prompts, stride=steps), :])
            acc = bias
            for k in range(4):
                acc = acc + taps[k] * window[t + k]
            x_scr[t * prompts : (t + 1) * prompts, cols] = silu(acc)
    x = x_scr[...].astype(BF16)
    x_ref[...] = x
    low, sel = project(x, rank_ref, select_ref)
    low_ref[...] = low
    sel_ref[...] = sel
    empty.wait()


def decode_kernel(
    items_ref, got_ref, conv_ref, u_ref, cw_ref, extra_ref, rank_ref, select_ref, prompt_low_ref,
    prompt_sel_ref, pay_ref, x_ref, pass_ref, pool_scr, pay_scr, scr, x_scr,
):
    groups = got_ref.shape[0]
    reqs, steps, channels = u_ref.shape
    table = groups * ROWS0
    marks = jnp.zeros((8, channels), F32)
    for s in range(groups):
        block = got_ref[s].astype(F32)
        pool_scr[s * ROWS0 : (s + 1) * ROWS0, :] = block
        marks = marks + block[8:16]
    for r in range(reqs):
        put_lanes(scr, 8 * r, u_ref[r].astype(F32))
    pool = pool_scr[...].astype(BF16)
    ids = marks[4:5, :table]
    place = lax.rem(iota((1, table), 1), ROWS0)
    moves = groups * MIG
    square = (moves, LANES)
    wanted = jnp.sum(
        jnp.where(
            iota(square, 0) == iota(square, 1), jnp.broadcast_to(marks[5:6, :LANES], square), 0.0
        ),
        axis=1,
        keepdims=True,
    )
    passed = (wanted == ids) & (place >= STATE_ROW) & (place < STATE_ROW + MIG)
    relay = jnp.dot(jnp.where(passed, 1.0, 0.0).astype(BF16), pool, preferred_element_type=F32)
    for d in range(groups):
        pass_ref[d] = relay[d * MIG : (d + 1) * MIG].astype(BF16)
    moved = items_ref[reqs : 2 * reqs, :] > 0.0
    moved_wide = jnp.concatenate([items_ref[reqs : 2 * reqs, :]] * (channels // LANES), axis=1) > 0.0
    needs = items_ref[:reqs, :]
    found = jnp.concatenate(
        [
            jnp.where(moved & (ids[:, at : at + LANES] == needs), 1.0, 0.0)
            for at in range(0, table, LANES)
        ],
        axis=1,
    )
    hist = []
    for j in range(3):
        hit = jnp.where((place >= 4 * j) & (place < 4 * j + 4), found, 0.0).astype(BF16)
        taken = jnp.dot(hit, pool, preferred_element_type=F32)
        hist.append(jnp.where(moved_wide, taken, conv_ref[j].astype(F32)))
    for l in range(channels // LANES):
        cols = slice(l * LANES, (l + 1) * LANES)
        taps = [cw_ref[k : k + 1, cols] for k in range(4)]
        bias = extra_ref[2:3, cols]
        window = [hist[j][:, cols] for j in range(3)]
        for t in range(steps):
            window.append(scr[l, pl.ds(t, reqs, stride=8), :])
            acc = bias
            for k in range(4):
                acc = acc + taps[k] * window[t + k]
            x_scr[t * reqs : (t + 1) * reqs, cols] = silu(acc)
    x = x_scr[...].astype(BF16)
    x_ref[...] = x
    low, sel = project(x, rank_ref, select_ref)
    prompt_groups = prompt_low_ref.shape[0] // 8
    pay_scr[...] = jnp.zeros(pay_scr.shape, F32)
    put_tiles(pay_scr, 0, prompt_low_ref[...], prompt_sel_ref[...])
    put_tiles(pay_scr, prompt_groups, low, sel)
    peers, blocks, four, _ = pay_ref.shape
    for j in range(peers):
        for a in range(blocks):
            pay_ref[j, a] = pay_scr[j, four * a : four * (a + 1), :].astype(BF16)


def sum_kernel(got_ref, out_ref):
    total = got_ref[0].astype(F32)
    for j in range(1, got_ref.shape[0]):
        total = total + got_ref[j].astype(F32)
    own_rows = total.astype(BF16)
    for j in range(out_ref.shape[0]):
        out_ref[j] = own_rows


def steps_of(low_scr, step_w_ref, step_b):
    low = low_scr[...]
    scale = lax.rsqrt(jnp.mean(low * low, axis=-1, keepdims=True) + EPS)
    raw = jnp.dot(low.astype(BF16), step_w_ref[...], preferred_element_type=F32)
    return softplus(raw * scale + step_b)


def scan(t, items, live, x, gate, sel, step, decay, skip, h_scr, y_scr, y_stride):
    states = decay.shape[1] // 8
    for g in range(items // 8):
        rows = slice(t * items + 8 * g, t * items + 8 * g + 8)
        alive = None if live is None else live[8 * g : 8 * g + 8]
        pair = sel[rows, :]
        lanes = range(h_scr.shape[0])
        steps, drive, y = [], [], []
        for l in lanes:
            cols = slice(l * LANES, (l + 1) * LANES)
            step_l = step[rows, cols]
            if alive is not None:
                step_l = jnp.where(alive, step_l, 0.0)
            x_l = x[rows, cols]
            steps.append(step_l)
            drive.append(step_l * x_l)
            y.append(skip[:, cols] * x_l)
        for n in range(states):
            b = jnp.broadcast_to(pair[:, n : n + 1], (8, LANES))
            c = jnp.broadcast_to(pair[:, states + n : states + n + 1], (8, LANES))
            at = slice(n * items + 8 * g, n * items + 8 * g + 8)
            for l in lanes:
                keep = jnp.exp2(steps[l] * decay[l, 8 * n : 8 * n + 8, :])
                h = keep * h_scr[l, at, :] + drive[l] * b
                h_scr[l, at, :] = h
                y[l] = y[l] + c * h
        for l in lanes:
            cols = slice(l * LANES, (l + 1) * LANES)
            out = y[l] * gate[rows, cols]
            if alive is not None:
                out = jnp.where(alive, out, 0.0)
            y_scr[l, pl.ds(8 * g * y_stride + t, 8, stride=y_stride), :] = out


def prefill_kernel(
    plan_ref, rows_ref, x_ref, step_w_ref, decay_ref, extra_ref, relay_ref, items_ref, _empty,
    sum_ref, pay_ref, low_scr, sel_scr, step_scr, x_scr, sum_scr, h_scr, final_scr, plan_scr, sems,
):
    prompts = final_scr.shape[0]
    total_rows, channels = sum_scr.shape
    steps = total_rows // prompts
    states = decay_ref.shape[1] // 8
    reqs = plan_ref.shape[0] - 2 * prompts
    groups, blocks, four, _ = pay_ref.shape
    parts = states // four
    plan_copy = pltpu.make_async_copy(plan_ref, plan_scr, sems.at[0])
    plan_copy.start()
    passed = pltpu.make_async_copy(relay_ref, pay_ref.at[:, blocks - 1], sems.at[1])
    passed.start()
    take_tiles(rows_ref, 0, low_scr, sel_scr)
    step_scr[...] = steps_of(low_scr, step_w_ref, extra_ref[0:1, :])
    x_scr[...] = x_ref[...].astype(F32)
    lengths = items_ref[2 * reqs :, :]
    skip = extra_ref[1:2, :]
    lanes = range(channels // LANES)
    for t in range(steps):
        rows = slice(t * prompts, (t + 1) * prompts)
        for l in lanes:
            cols = slice(l * LANES, (l + 1) * LANES)
            x_l = x_scr[rows, cols]
            step_l = jnp.where(t < lengths, step_scr[rows, cols], 0.0)
            step_scr[rows, cols] = step_l
            sum_scr[rows, cols] = skip[:, cols] * x_l
            x_scr[rows, cols] = step_l * x_l
    for first in range(0, states, 4):
        names = range(first, first + 4)
        decay = [[decay_ref[l, prompts * n : prompts * (n + 1), :] for l in lanes] for n in names]
        held = [[None for _ in lanes] for _ in names]
        for t in range(steps):
            rows = slice(t * prompts, (t + 1) * prompts)
            pair = sel_scr[rows, :]
            shape = (prompts, LANES)
            bs = [jnp.broadcast_to(pair[:, n : n + 1], shape) for n in names]
            cs = [jnp.broadcast_to(pair[:, states + n : states + n + 1], shape) for n in names]
            for l in lanes:
                cols = slice(l * LANES, (l + 1) * LANES)
                step_l, drive = step_scr[rows, cols], x_scr[rows, cols]
                y = sum_scr[rows, cols]
                for n in range(4):
                    h = drive * bs[n]
                    if t:
                        h = h + jnp.exp2(step_l * decay[n][l]) * held[n][l]
                    held[n][l] = h
                    y = y + cs[n] * h
                sum_scr[rows, cols] = y
        for n in range(4):
            for l in lanes:
                at = (first + n) * prompts
                h_scr[l, at : at + prompts, :] = held[n][l]
    copies = [pltpu.make_async_copy(sum_scr, sum_ref, sems.at[2 + prompts])]
    copies[0].start()
    plan_copy.wait()
    dests, ranks = slots_of(plan_scr, prompts, reqs)
    passed.wait()
    for i in range(prompts):
        for l in range(channels // LANES):
            cols = slice(l * LANES, (l + 1) * LANES)
            for p in range(parts):
                final_scr[i, p, :, cols] = h_scr[
                    l, pl.ds(i + p * four * prompts, four, stride=prompts), :
                ].astype(BF16)
        place = pay_ref.at[dests[i], pl.ds(ranks[i] * parts, parts)]
        copies.append(pltpu.make_async_copy(final_scr.at[i], place, sems.at[2 + i]))
        copies[-1].start()
    for copy in copies:
        copy.wait()


def decode_scan_kernel(
    plan_ref, rows_ref, x_ref, u_ref, gate_ref, state_ref, step_w_ref, decay_ref, extra_ref,
    got_ref, sum_ref, prompt_gate_ref, items_ref, out_ref, final_ref, base_ref, held_ref, weight_ref,
    keep_ref, pick_ref, final_conv_ref, prompt_conv_ref, prefill_ref, prefill_scr, low_scr, sel_scr, step_scr, x_scr, gate_scr, scr, h_scr, y_scr,
    conv_scr,
):
    reqs, steps, channels = gate_ref.shape
    states = state_ref.shape[1]
    lanes = channels // LANES
    own, picks = picks_of(plan_ref, reqs)
    take_tiles(rows_ref, PROMPT_GROUPS, low_scr, sel_scr)
    step_scr[...] = steps_of(low_scr, step_w_ref, extra_ref[0:1, :])
    x_scr[...] = x_ref[...].astype(F32)
    for r in range(reqs):
        put_lanes(scr, 8 * r, silu(gate_ref[r].astype(F32)))
        kept = plan_ref[r] == own * reqs + r
        for l in range(lanes):
            cols = slice(l * LANES, (l + 1) * LANES)
            h_scr[l, pl.ds(r, states, stride=reqs), :] = jnp.where(
                kept, state_ref[r, :, cols], 0.0
            )
    for l in range(lanes):
        cols = slice(l * LANES, (l + 1) * LANES)
        for t in range(steps):
            gate_scr[t * reqs : (t + 1) * reqs, cols] = scr[l, pl.ds(t, reqs, stride=8), :]
    skip = extra_ref[1:2, :]
    for t in range(steps):
        scan(t, reqs, None, x_scr, gate_scr, sel_scr, step_scr, decay_ref, skip, h_scr, y_scr, 8)
    for r in range(reqs):
        final_conv_ref[:, r : r + 1, :] = u_ref[r].astype(F32)[1:4].reshape(3, 1, channels)
        for l in range(lanes):
            cols = slice(l * LANES, (l + 1) * LANES)
            final_ref[r, :, cols] = h_scr[l, pl.ds(r, states, stride=reqs), :]
            out_ref[r, :, cols] = y_scr[l, 8 * r : 8 * r + steps, :].astype(BF16)
    outward = jnp.transpose(sel_scr[...])[states : 2 * states]
    column = iota(outward.shape, 1)
    for k in range(MIG):
        pick_ref[k : k + 1, :] = jnp.broadcast_to(picks[k], (1, LANES)).astype(F32)
        held_ref[k] = final_ref[picks[k]]
        total = jnp.zeros((1, channels), F32)
        for t in range(steps):
            row = t * reqs + picks[k]
            total = total + step_scr[pl.ds(row, 1), :]
            gate = gate_scr[pl.ds(row, 1), :]
            c = jnp.sum(jnp.where(column == row, outward, 0.0), axis=1, keepdims=True)
            for l in range(lanes):
                cols = slice(l * LANES, (l + 1) * LANES)
                keep = jnp.exp2(total[:, cols] * decay_ref[l, pl.ds(0, states, stride=8), :])
                weight_ref[k * steps + t, :, cols] = keep * c * gate[:, cols]
                base_ref[k * steps + t : k * steps + t + 1, cols] = y_scr[
                    l, pl.ds(8 * picks[k] + t, 1), :
                ]
                if t == steps - 1:
                    keep_ref[k, :, cols] = keep
    pick_ref[MIG:, :] = jnp.zeros((pick_ref.shape[0] - MIG, LANES), F32)
    for s in range(got_ref.shape[0]):
        block = got_ref[s].astype(F32)
        for q in range(PAIR):
            for j in range(3):
                at = TAIL_ROW + 3 * q + j
                conv_scr[j, s * PAIR + q : s * PAIR + q + 1, :] = block[at : at + 1]
    prompt_conv_ref[...] = conv_scr[...].astype(BF16)
    prompts, length, _ = prefill_ref.shape
    lengths = items_ref[2 * reqs :, :]
    for l in range(lanes):
        cols = slice(l * LANES, (l + 1) * LANES)
        for t in range(length):
            rows = slice(t * prompts, (t + 1) * prompts)
            out = jnp.where(t < lengths, sum_ref[rows, cols] * prompt_gate_ref[rows, cols], 0.0)
            prefill_scr[l, pl.ds(t, prompts, stride=length), :] = out
        for i in range(prompts):
            prefill_ref[i, :, cols] = prefill_scr[l, i * length : (i + 1) * length, :].astype(BF16)


def finish_kernel(
    got_ref, base_ref, held_ref, weight_ref, keep_ref, pick_ref, _out, _final, out_ref, final_ref,
    prompt_state_ref, state_scr, moved_scr, out_scr, final_scr, sems,
):
    groups, blocks, four, channels = got_ref.shape
    slots, states, _ = state_scr.shape
    steps = base_ref.shape[0] // MIG
    lanes = channels // LANES
    parts = states // four
    copies = []
    for s in range(groups):
        for q in range(PAIR):
            for p in range(parts):
                state_scr[s * PAIR + q, p * four : (p + 1) * four, :] = got_ref[
                    s, q * parts + p
                ].astype(F32)
        if s % 4 == 3:
            here = pl.ds((s - 3) * PAIR, 4 * PAIR)
            copies.append(
                pltpu.make_async_copy(state_scr.at[here], prompt_state_ref.at[here], sems.at[s])
            )
            copies[-1].start()
    for n in range(states):
        put_lanes(moved_scr, n * MIG, got_ref[n, blocks - 1].astype(F32))
    for k in range(MIG):
        pick = jnp.max(pick_ref[k : k + 1, :]).astype(jnp.int32)
        for l in range(lanes):
            cols = slice(l * LANES, (l + 1) * LANES)
            start = moved_scr[l, pl.ds(k, states, stride=MIG), :]
            final_scr[k, :, cols] = held_ref[k, :, cols] + keep_ref[k, :, cols] * start
            rows = []
            for t in range(steps):
                at = k * steps + t
                more = jnp.sum(weight_ref[at, :, cols] * start, axis=0, keepdims=True)
                rows.append(base_ref[at : at + 1, cols] + more)
            out_scr[k, :, cols] = jnp.concatenate(rows, axis=0).astype(BF16)
        copies.append(
            pltpu.make_async_copy(final_scr.at[k], final_ref.at[pick], sems.at[groups + k])
        )
        copies.append(
            pltpu.make_async_copy(out_scr.at[k], out_ref.at[pick], sems.at[groups + MIG + k])
        )
        copies[-2].start()
        copies[-1].start()
    for copy in copies:
        copy.wait()


def exchange(value, axis):
    return lax.all_to_all(value, axis, split_axis=0, concat_axis=0, tiled=True)


def on_device(
    resident_state,
    resident_conv,
    migrate_from,
    decode_inputs,
    decode_gates,
    prompt_inputs,
    prompt_gates,
    prompt_length,
    prompt_dest,
    conv_weight,
    conv_bias,
    rank_weight,
    select_weight,
    step_weight,
    step_bias,
    decay_log,
    skip_gain,
):
    groups = lax.axis_size("group")
    peers = lax.axis_size("mp")
    reqs, states, channels = resident_state.shape
    prompts, steps, _ = prompt_inputs.shape
    decode_steps = decode_inputs.shape[1]
    tiles = channels // LANES
    rank = rank_weight.shape[1]
    selects = select_weight.shape[1]
    prompt_rows = prompts * steps
    decode_rows = reqs * decode_steps
    bias_row = conv_bias.reshape(1, channels)
    step_bias_row = step_bias.reshape(1, channels)
    skip_row = skip_gain.reshape(1, channels)

    def struct(shape, dtype):
        return jax.ShapeDtypeStruct(shape, dtype)

    def scratch(shape):
        return pltpu.VMEM(shape, F32)

    def cost(flops, size):
        return pl.CostEstimate(flops=flops, bytes_accessed=size, transcendentals=0)

    anywhere = pl.BlockSpec(memory_space=pl.ANY)
    send_shape = (groups, PAIR * states // MIG + 1, MIG, channels)
    dest = prompt_dest.reshape(prompts)
    conv_rows = jnp.transpose(resident_conv, (1, 0, 2))
    select_rows = jnp.transpose(select_weight)

    send_first = pl.pallas_call(
        pack_kernel,
        out_shape=struct((groups, ROWS0, channels), BF16),
        in_specs=[SMEM] * 3 + [VMEM] * 3,
        out_specs=anywhere,
        scratch_shapes=[
            scratch((groups + 1, ROWS0, channels)),
            scratch((3 * reqs, channels)),
            scratch((prompts * (steps + 8), channels)),
            pltpu.VMEM((groups, ROWS0, channels), BF16),
            pltpu.SemaphoreType.DMA((groups // 4,)),
        ],
        compiler_params=ALL_VMEM,
        name="pack",
    )(migrate_from, dest, prompt_length, conv_rows, resident_state, prompt_inputs)
    got_first = exchange(send_first, "group")

    prompt_low, prompt_sel, prompt_x, gate_rows, decay, extra, plan, items, empty = pl.pallas_call(
        prompt_kernel,
        out_shape=(
            struct((prompt_rows, rank), F32),
            struct((prompt_rows, selects), F32),
            struct((prompt_rows, channels), BF16),
            struct((prompt_rows, channels), F32),
            struct((tiles, 8 * states, LANES), F32),
            struct((8, channels), F32),
            struct((reqs + 2 * prompts,), jnp.int32),
            struct((2 * reqs + prompts, LANES), F32),
            struct(send_shape, BF16),
        ),
        in_specs=[SMEM] * 3 + [VMEM] * 9,
        out_specs=(VMEM,) * 6 + (SMEM, VMEM, anywhere),
        scratch_shapes=[
            scratch((tiles, prompt_rows, LANES)),
            scratch((prompt_rows, channels)),
            pltpu.VMEM(send_shape, BF16),
            pltpu.SemaphoreType.DMA,
        ],
        compiler_params=PARAMS,
        cost_estimate=cost(10**9, 2 * 10**6),
        name="prompt_features",
    )(
        migrate_from, dest, prompt_length, prompt_inputs, prompt_gates, conv_weight, bias_row,
        rank_weight, select_rows, decay_log, step_bias_row, skip_row,
    )

    pay, decode_x, relay = pl.pallas_call(
        decode_kernel,
        out_shape=(
            struct((peers, 7, 4, LANES), BF16),
            struct((decode_rows, channels), BF16),
            struct((groups, MIG, channels), BF16),
        ),
        in_specs=[VMEM] * 10,
        out_specs=(VMEM,) * 3,
        scratch_shapes=[
            scratch((groups * ROWS0, channels)),
            scratch((peers, 32, LANES)),
            scratch((tiles, reqs * 8, LANES)),
            scratch((decode_rows, channels)),
        ],
        compiler_params=PARAMS,
        name="decode_features",
    )(
        items, got_first, conv_rows, decode_inputs, conv_weight, extra, rank_weight, select_rows,
        prompt_low, prompt_sel,
    )

    parts = exchange(pay, "mp")
    shares = pl.pallas_call(
        sum_kernel,
        out_shape=struct(parts.shape, BF16),
        in_specs=[VMEM],
        out_specs=VMEM,
        compiler_params=PARAMS,
        name="sum_parts",
    )(parts)
    rows = exchange(shares, "mp")

    prompt_sum, send_final = pl.pallas_call(
        prefill_kernel,
        out_shape=(struct((prompt_rows, channels), F32), struct(send_shape, BF16)),
        in_specs=[anywhere] + [VMEM] * 7 + [anywhere],
        out_specs=(anywhere, anywhere),
        scratch_shapes=[
            scratch((prompt_rows, rank)),
            scratch((prompt_rows, LANES)),
            scratch((prompt_rows, channels)),
            scratch((prompt_rows, channels)),
            scratch((prompt_rows, channels)),
            scratch((tiles, prompts * states, LANES)),
            pltpu.VMEM((prompts, states // MIG, MIG, channels), BF16),
            pltpu.SMEM((reqs + 2 * prompts,), jnp.int32),
            pltpu.SemaphoreType.DMA((prompts + 3,)),
        ],
        input_output_aliases={8: 1},
        compiler_params=PARAMS,
        name="prefill_scan",
    )(plan, rows, prompt_x, step_weight, decay, extra, relay, items, empty)
    got_final = exchange(send_final, "group")

    (
        early_out, early_final, base, held, weight, keep, pick, final_conv, prompt_conv, prefill_out,
    ) = pl.pallas_call(
        decode_scan_kernel,
        out_shape=(
            struct(decode_inputs.shape, BF16),
            struct(resident_state.shape, F32),
            struct((MIG * decode_steps, channels), F32),
            struct((MIG, states, channels), F32),
            struct((MIG * decode_steps, states, channels), F32),
            struct((MIG, states, channels), F32),
            struct((8, LANES), F32),
            struct((3, reqs, channels), F32),
            struct((3, groups * PAIR, channels), BF16),
            struct(prompt_inputs.shape, BF16),
        ),
        in_specs=[SMEM] + [VMEM] * 12,
        out_specs=(VMEM,) * 10,
        scratch_shapes=[
            scratch((tiles, prompt_rows, LANES)),
            scratch((decode_rows, rank)),
            scratch((decode_rows, LANES)),
            scratch((decode_rows, channels)),
            scratch((decode_rows, channels)),
            scratch((decode_rows, channels)),
            scratch((tiles, reqs * 8, LANES)),
            scratch((tiles, reqs * states, LANES)),
            scratch((tiles, reqs * 8, LANES)),
            scratch((3, groups * PAIR, channels)),
        ],
        compiler_params=PARAMS,
        cost_estimate=cost(6 * 10**9, 8 * 10**6),
        name="decode_scan",
    )(
        plan, rows, decode_x, decode_inputs, decode_gates, resident_state, step_weight, decay,
        extra, got_first, prompt_sum, gate_rows, items,
    )

    decode_out, final_state, prompt_state = pl.pallas_call(
        finish_kernel,
        out_shape=(
            struct(decode_inputs.shape, BF16),
            struct(resident_state.shape, F32),
            struct((groups * PAIR, states, channels), F32),
        ),
        in_specs=[VMEM] * 6 + [anywhere] * 2,
        out_specs=(anywhere,) * 3,
        scratch_shapes=[
            scratch((groups * PAIR, states, channels)),
            scratch((tiles, states * MIG, LANES)),
            pltpu.VMEM((MIG, decode_steps, channels), BF16),
            scratch((MIG, states, channels)),
            pltpu.SemaphoreType.DMA((groups + 2 * MIG,)),
        ],
        input_output_aliases={6: 0, 7: 1},
        compiler_params=PARAMS,
        name="finish",
    )(got_final, base, held, weight, keep, pick, early_out, early_final)
    final_conv = jnp.transpose(final_conv, (1, 0, 2)).astype(BF16)
    prompt_conv = jnp.transpose(prompt_conv, (1, 0, 2))
    return (decode_out, final_state, final_conv, prefill_out, prompt_state, prompt_conv)


def solution(mesh):
    whole = P("group", None, "mp")
    return jax.shard_map(
        on_device,
        mesh=mesh,
        in_specs=(
            whole,
            whole,
            P("group"),
            whole,
            whole,
            whole,
            whole,
            P("group"),
            P("group", None),
            P(None, "mp"),
            P("mp"),
            P("mp", None),
            P("mp", None),
            P(None, "mp"),
            P("mp"),
            P(None, "mp"),
            P("mp"),
        ),
        out_specs=(whole,) * 6,
        check_vma=False,
    )
```

```python
import jax
import jax.numpy as jnp
from jax import lax
from jax.experimental import pallas as pl
from jax.experimental.pallas import tpu as pltpu
from jax.sharding import PartitionSpec as P

MIG = 4
PAIR = 2
EPS = 1e-06
LANES = 128
ROWS0 = 24
PROMPT_GROUPS = 16
STATE_ROW = 14
TAIL_ROW = 18
LOG2E = 1.4426950408889634

F32 = jnp.float32
BF16 = jnp.bfloat16
VMEM = pl.BlockSpec(memory_space=pltpu.VMEM)
SMEM = pl.BlockSpec(memory_space=pltpu.SMEM)
PARAMS = pltpu.CompilerParams(vmem_limit_bytes=40 * 1024 * 1024)
ALL_VMEM = pltpu.CompilerParams(vmem_limit_bytes=60 * 1024 * 1024)


def silu(x):
    return x / (1.0 + jnp.exp(-x))


def softplus(x):
    return jnp.maximum(x, 0.0) + jnp.log1p(jnp.exp(-jnp.abs(x)))


def iota(shape, dim):
    return lax.broadcasted_iota(jnp.int32, shape, dim)


def from_scalars(ref, count, shape, first=0):
    rows = iota(shape, 0)
    out = jnp.zeros(shape, jnp.int32)
    for i in range(count):
        out = jnp.where(rows == i, ref[first + i], out)
    return out


def slots_of(dest_ref, count, first=0):
    dests = [dest_ref[first + i] for i in range(count)]
    ranks = []
    for i in range(count):
        rank = jnp.int32(0)
        for j in range(i):
            rank = rank + (dests[j] == dests[i]).astype(jnp.int32)
        ranks.append(rank)
    return dests, ranks


def picks_of(mig_ref, reqs):
    own = lax.axis_index("group")
    count = jnp.int32(0)
    picks = [jnp.int32(0) for _ in range(MIG)]
    for r in range(reqs):
        moved = mig_ref[r] != own * reqs + r
        for k in range(MIG):
            picks[k] = jnp.where(moved & (count == k), r, picks[k])
        count = count + moved.astype(jnp.int32)
    return own, picks


def pack_kernel(
    mig_ref, dest_ref, len_ref, conv_ref, state_ref, u_ref, pay_ref, scr, conv_scr, u_scr
):
    groups = pay_ref.shape[0]
    _, reqs, channels = conv_ref.shape
    prompts, steps, _ = u_ref.shape
    states = state_ref.shape[1]
    own, picks = picks_of(mig_ref, reqs)
    base = scr.at[groups]
    base[...] = jnp.zeros(base.shape, F32)
    lane = iota((1, channels), 1)
    ids = jnp.zeros((1, channels), jnp.int32)
    wanted = jnp.zeros((1, channels), jnp.int32)
    for j in range(3):
        conv_scr[j * reqs : (j + 1) * reqs, :] = conv_ref[j].astype(F32)
    for k in range(MIG):
        for at in (k, 4 + k, 8 + k, STATE_ROW + k):
            ids = jnp.where(lane == own * ROWS0 + at, own * reqs + picks[k], ids)
        wanted = jnp.where(lane == own * MIG + k, mig_ref[picks[k]], wanted)
        for j in range(3):
            at = 4 * j + k
            base[at : at + 1, :] = conv_scr[pl.ds(j * reqs + picks[k], 1), :]
    base[12:13, :] = ids.astype(F32)
    base[13:14, :] = wanted.astype(F32)
    for d in range(groups):
        scr[d] = base[...]
    dests, ranks = slots_of(dest_ref, prompts)
    pad = u_scr.shape[0] // prompts
    for i in range(prompts):
        u_scr[i * pad : i * pad + 8, :] = jnp.zeros((8, channels), F32)
        u_scr[i * pad + 8 : i * pad + 8 + steps, :] = u_ref[i].astype(F32)
    for i in range(prompts):
        tails = [u_scr[pl.ds(i * pad + 5 + j + len_ref[i], 1), :] for j in range(3)]
        for q in range(PAIR):

            @pl.when(ranks[i] == q)
            def _():
                for j in range(3):
                    at = TAIL_ROW + 3 * q + j
                    scr[dests[i], at : at + 1, :] = tails[j]

    for k in range(MIG):
        state = state_ref[picks[k]]
        for n in range(states):
            scr[n, STATE_ROW + k : STATE_ROW + k + 1, :] = state[n : n + 1, :]
    for d in range(groups):
        pay_ref[d] = scr[d].astype(BF16)


def put_lanes(ref, start, value):
    for l in range(ref.shape[0]):
        ref[l, start : start + value.shape[0], :] = value[:, l * LANES : (l + 1) * LANES]


def project(x, rank_ref, select_ref):
    low = jnp.dot(x, rank_ref[...], preferred_element_type=F32)
    sel = lax.dot_general(
        x, select_ref[...], (((1,), (1,)), ((), ())), preferred_element_type=F32
    )
    return low, sel


def put_tiles(scr, first, low, sel):
    tiles = low.shape[1] // LANES
    width = sel.shape[1]
    share = LANES // width
    for g in range(low.shape[0] // 8):
        rows = slice(8 * g, 8 * g + 8)
        for l in range(tiles):
            owner, place = divmod((first + g) * tiles + l, 3)
            scr[owner, 8 * place : 8 * place + 8, :] = low[rows, l * LANES : (l + 1) * LANES]
        pair, place = divmod(first + g, share)
        cols = slice(place * width, (place + 1) * width)
        scr[2 * pair, 24:28, cols] = sel[8 * g : 8 * g + 4]
        scr[2 * pair + 1, 24:28, cols] = sel[8 * g + 4 : 8 * g + 8]


def take_tiles(rows_ref, first, low_scr, sel_scr):
    count, channels = low_scr.shape
    tiles = channels // LANES
    for g in range(count // 8):
        upper, lower = slice(8 * g, 8 * g + 4), slice(8 * g + 4, 8 * g + 8)
        for l in range(tiles):
            cols = slice(l * LANES, (l + 1) * LANES)
            owner, place = divmod((first + g) * tiles + l, 3)
            low_scr[upper, cols] = rows_ref[owner, 2 * place].astype(F32)
            low_scr[lower, cols] = rows_ref[owner, 2 * place + 1].astype(F32)
        pair, place = divmod(first + g, 4)
        sel_scr[upper, :] = rows_ref[2 * pair, 6].astype(F32)
        sel_scr[lower, :] = rows_ref[2 * pair + 1, 6].astype(F32)
    for g in range(count // 8):
        place = (first + g) % 4
        if place:
            rows = slice(8 * g, 8 * g + 8)
            sel_scr[rows, :] = pltpu.roll(sel_scr[rows, :], LANES - 32 * place, 1)


def prompt_kernel(
    mig_ref, dest_ref, len_ref, u_ref, gate_ref, cw_ref, cb_ref, rank_ref, select_ref, decay_ref,
    step_b_ref, skip_ref, low_ref, sel_ref, x_ref, gate_out_ref, decay_out_ref, extra_ref,
    plan_ref, items_ref, empty_ref, scr, x_scr, empty_scr, sem,
):
    prompts, steps, channels = u_ref.shape
    reqs = mig_ref.shape[0]
    empty_scr[...] = jnp.zeros(empty_scr.shape, BF16)
    empty = pltpu.make_async_copy(empty_scr, empty_ref, sem)
    empty.start()
    for i in range(reqs):
        plan_ref[i] = mig_ref[i]
    for i in range(prompts):
        plan_ref[reqs + i] = dest_ref[i]
        plan_ref[reqs + prompts + i] = len_ref[i]
    own = lax.axis_index("group")
    wanted = from_scalars(mig_ref, reqs, (reqs, LANES))
    moved = wanted != own * reqs + iota(wanted.shape, 0)
    items_ref[:reqs, :] = wanted.astype(F32)
    items_ref[reqs : 2 * reqs, :] = jnp.where(moved, 1.0, 0.0)
    items_ref[2 * reqs :, :] = from_scalars(len_ref, prompts, (prompts, LANES)).astype(F32)
    extra_ref[0:1, :] = step_b_ref[...]
    extra_ref[1:2, :] = skip_ref[...]
    extra_ref[2:3, :] = cb_ref[...]
    extra_ref[3:8, :] = jnp.zeros((5, channels), F32)
    decay = jnp.exp(decay_ref[...]) * -LOG2E
    for n in range(decay.shape[0]):
        put_lanes(decay_out_ref, 8 * n, jnp.broadcast_to(decay[n : n + 1], (8, channels)))
    for i in range(prompts):
        put_lanes(scr, i * steps, silu(gate_ref[i].astype(F32)))
    for l in range(channels // LANES):
        cols = slice(l * LANES, (l + 1) * LANES)
        for t in range(steps):
            gate_out_ref[t * prompts : (t + 1) * prompts, cols] = scr[
                l, pl.ds(t, prompts, stride=steps), :
            ]
    for i in range(prompts):
        put_lanes(scr, i * steps, u_ref[i].astype(F32))
    for l in range(channels // LANES):
        cols = slice(l * LANES, (l + 1) * LANES)
        taps = [cw_ref[k : k + 1, cols] for k in range(4)]
        bias = cb_ref[:, cols]
        window = [jnp.zeros((prompts, LANES), F32) for _ in range(3)]
        for t in range(steps):
            window.append(scr[l, pl.ds(t, prompts, stride=steps), :])
            acc = bias
            for k in range(4):
                acc = acc + taps[k] * window[t + k]
            x_scr[t * prompts : (t + 1) * prompts, cols] = silu(acc)
    x = x_scr[...].astype(BF16)
    x_ref[...] = x
    low, sel = project(x, rank_ref, select_ref)
    low_ref[...] = low
    sel_ref[...] = sel
    empty.wait()


def decode_kernel(
    items_ref, got_ref, conv_ref, u_ref, cw_ref, extra_ref, rank_ref, select_ref, prompt_low_ref,
    prompt_sel_ref, pay_ref, x_ref, pass_ref, pool_scr, pay_scr, scr, x_scr,
):
    groups = got_ref.shape[0]
    reqs, steps, channels = u_ref.shape
    table = groups * ROWS0
    marks = jnp.zeros((8, channels), F32)
    for s in range(groups):
        block = got_ref[s].astype(F32)
        pool_scr[s * ROWS0 : (s + 1) * ROWS0, :] = block
        marks = marks + block[8:16]
    for r in range(reqs):
        put_lanes(scr, 8 * r, u_ref[r].astype(F32))
    pool = pool_scr[...].astype(BF16)
    ids = marks[4:5, :table]
    place = lax.rem(iota((1, table), 1), ROWS0)
    moves = groups * MIG
    square = (moves, LANES)
    wanted = jnp.sum(
        jnp.where(
            iota(square, 0) == iota(square, 1), jnp.broadcast_to(marks[5:6, :LANES], square), 0.0
        ),
        axis=1,
        keepdims=True,
    )
    passed = (wanted == ids) & (place >= STATE_ROW) & (place < STATE_ROW + MIG)
    relay = jnp.dot(jnp.where(passed, 1.0, 0.0).astype(BF16), pool, preferred_element_type=F32)
    for d in range(groups):
        pass_ref[d] = relay[d * MIG : (d + 1) * MIG].astype(BF16)
    moved = items_ref[reqs : 2 * reqs, :] > 0.0
    moved_wide = jnp.concatenate([items_ref[reqs : 2 * reqs, :]] * (channels // LANES), axis=1) > 0.0
    needs = items_ref[:reqs, :]
    found = jnp.concatenate(
        [
            jnp.where(moved & (ids[:, at : at + LANES] == needs), 1.0, 0.0)
            for at in range(0, table, LANES)
        ],
        axis=1,
    )
    hist = []
    for j in range(3):
        hit = jnp.where((place >= 4 * j) & (place < 4 * j + 4), found, 0.0).astype(BF16)
        taken = jnp.dot(hit, pool, preferred_element_type=F32)
        hist.append(jnp.where(moved_wide, taken, conv_ref[j].astype(F32)))
    for l in range(channels // LANES):
        cols = slice(l * LANES, (l + 1) * LANES)
        taps = [cw_ref[k : k + 1, cols] for k in range(4)]
        bias = extra_ref[2:3, cols]
        window = [hist[j][:, cols] for j in range(3)]
        for t in range(steps):
            window.append(scr[l, pl.ds(t, reqs, stride=8), :])
            acc = bias
            for k in range(4):
                acc = acc + taps[k] * window[t + k]
            x_scr[t * reqs : (t + 1) * reqs, cols] = silu(acc)
    x = x_scr[...].astype(BF16)
    x_ref[...] = x
    low, sel = project(x, rank_ref, select_ref)
    prompt_groups = prompt_low_ref.shape[0] // 8
    pay_scr[...] = jnp.zeros(pay_scr.shape, F32)
    put_tiles(pay_scr, 0, prompt_low_ref[...], prompt_sel_ref[...])
    put_tiles(pay_scr, prompt_groups, low, sel)
    peers, blocks, four, _ = pay_ref.shape
    for j in range(peers):
        for a in range(blocks):
            pay_ref[j, a] = pay_scr[j, four * a : four * (a + 1), :].astype(BF16)


def sum_kernel(got_ref, out_ref):
    total = got_ref[0].astype(F32)
    for j in range(1, got_ref.shape[0]):
        total = total + got_ref[j].astype(F32)
    own_rows = total.astype(BF16)
    for j in range(out_ref.shape[0]):
        out_ref[j] = own_rows


def steps_of(low_scr, step_w_ref, step_b):
    low = low_scr[...]
    scale = lax.rsqrt(jnp.mean(low * low, axis=-1, keepdims=True) + EPS)
    raw = jnp.dot(low.astype(BF16), step_w_ref[...], preferred_element_type=F32)
    return softplus(raw * scale + step_b)


def scan(t, items, live, x, gate, sel, step, decay, skip, h_scr, y_scr, y_stride):
    states = decay.shape[1] // 8
    for g in range(items // 8):
        rows = slice(t * items + 8 * g, t * items + 8 * g + 8)
        alive = None if live is None else live[8 * g : 8 * g + 8]
        pair = sel[rows, :]
        lanes = range(h_scr.shape[0])
        steps, drive, y = [], [], []
        for l in lanes:
            cols = slice(l * LANES, (l + 1) * LANES)
            step_l = step[rows, cols]
            if alive is not None:
                step_l = jnp.where(alive, step_l, 0.0)
            x_l = x[rows, cols]
            steps.append(step_l)
            drive.append(step_l * x_l)
            y.append(skip[:, cols] * x_l)
        for n in range(states):
            b = jnp.broadcast_to(pair[:, n : n + 1], (8, LANES))
            c = jnp.broadcast_to(pair[:, states + n : states + n + 1], (8, LANES))
            at = slice(n * items + 8 * g, n * items + 8 * g + 8)
            for l in lanes:
                keep = jnp.exp2(steps[l] * decay[l, 8 * n : 8 * n + 8, :])
                h = keep * h_scr[l, at, :] + drive[l] * b
                h_scr[l, at, :] = h
                y[l] = y[l] + c * h
        for l in lanes:
            cols = slice(l * LANES, (l + 1) * LANES)
            out = y[l] * gate[rows, cols]
            if alive is not None:
                out = jnp.where(alive, out, 0.0)
            y_scr[l, pl.ds(8 * g * y_stride + t, 8, stride=y_stride), :] = out


def prefill_kernel(
    plan_ref, rows_ref, x_ref, gate_ref, step_w_ref, decay_ref, extra_ref, relay_ref,
    items_ref, _empty, out_ref, pay_ref, low_scr, sel_scr, step_scr, x_scr, sum_scr, h_scr, y_scr,
    final_scr, out_scr, plan_scr, sems,
):
    prompts, steps, channels = out_ref.shape
    states = decay_ref.shape[1] // 8
    reqs = plan_ref.shape[0] - 2 * prompts
    groups, blocks, four, _ = pay_ref.shape
    parts = states // four
    plan_copy = pltpu.make_async_copy(plan_ref, plan_scr, sems.at[0])
    plan_copy.start()
    passed = pltpu.make_async_copy(relay_ref, pay_ref.at[:, blocks - 1], sems.at[1])
    passed.start()
    take_tiles(rows_ref, 0, low_scr, sel_scr)
    step_scr[...] = steps_of(low_scr, step_w_ref, extra_ref[0:1, :])
    x_scr[...] = x_ref[...].astype(F32)
    lengths = items_ref[2 * reqs :, :]
    skip = extra_ref[1:2, :]
    lanes = range(channels // LANES)
    for t in range(steps):
        rows = slice(t * prompts, (t + 1) * prompts)
        for l in lanes:
            cols = slice(l * LANES, (l + 1) * LANES)
            x_l = x_scr[rows, cols]
            step_l = jnp.where(t < lengths, step_scr[rows, cols], 0.0)
            step_scr[rows, cols] = step_l
            sum_scr[rows, cols] = skip[:, cols] * x_l
            x_scr[rows, cols] = step_l * x_l
    for first in range(0, states, 4):
        names = range(first, first + 4)
        decay = [[decay_ref[l, prompts * n : prompts * (n + 1), :] for l in lanes] for n in names]
        held = [[None for _ in lanes] for _ in names]
        for t in range(steps):
            rows = slice(t * prompts, (t + 1) * prompts)
            pair = sel_scr[rows, :]
            shape = (prompts, LANES)
            bs = [jnp.broadcast_to(pair[:, n : n + 1], shape) for n in names]
            cs = [jnp.broadcast_to(pair[:, states + n : states + n + 1], shape) for n in names]
            for l in lanes:
                cols = slice(l * LANES, (l + 1) * LANES)
                step_l, drive = step_scr[rows, cols], x_scr[rows, cols]
                y = sum_scr[rows, cols]
                for n in range(4):
                    h = drive * bs[n]
                    if t:
                        h = h + jnp.exp2(step_l * decay[n][l]) * held[n][l]
                    held[n][l] = h
                    y = y + cs[n] * h
                sum_scr[rows, cols] = y
        for n in range(4):
            for l in lanes:
                at = (first + n) * prompts
                h_scr[l, at : at + prompts, :] = held[n][l]
    for t in range(steps):
        rows = slice(t * prompts, (t + 1) * prompts)
        for l in lanes:
            cols = slice(l * LANES, (l + 1) * LANES)
            out = jnp.where(t < lengths, sum_scr[rows, cols] * gate_ref[rows, cols], 0.0)
            y_scr[l, pl.ds(t, prompts, stride=steps), :] = out
    plan_copy.wait()
    dests, ranks = slots_of(plan_scr, prompts, reqs)
    passed.wait()
    copies = []
    for i in range(prompts):
        for l in range(channels // LANES):
            cols = slice(l * LANES, (l + 1) * LANES)
            for p in range(parts):
                final_scr[i, p, :, cols] = h_scr[
                    l, pl.ds(i + p * four * prompts, four, stride=prompts), :
                ].astype(BF16)
        place = pay_ref.at[dests[i], pl.ds(ranks[i] * parts, parts)]
        copies.append(pltpu.make_async_copy(final_scr.at[i], place, sems.at[2 + i]))
        copies[-1].start()
    for i in range(prompts):
        for l in range(channels // LANES):
            cols = slice(l * LANES, (l + 1) * LANES)
            out_scr[i, :, cols] = y_scr[l, i * steps : (i + 1) * steps, :].astype(BF16)
    copies.append(pltpu.make_async_copy(out_scr, out_ref, sems.at[2 + prompts]))
    copies[-1].start()
    for copy in copies:
        copy.wait()


def decode_scan_kernel(
    plan_ref, rows_ref, x_ref, u_ref, gate_ref, state_ref, step_w_ref, decay_ref, extra_ref,
    got_ref, out_ref, final_ref, base_ref, held_ref, weight_ref, keep_ref, pick_ref,
    final_conv_ref, prompt_conv_ref, low_scr, sel_scr, step_scr, x_scr, gate_scr, scr, h_scr, y_scr,
    conv_scr,
):
    reqs, steps, channels = gate_ref.shape
    states = state_ref.shape[1]
    lanes = channels // LANES
    own, picks = picks_of(plan_ref, reqs)
    take_tiles(rows_ref, PROMPT_GROUPS, low_scr, sel_scr)
    step_scr[...] = steps_of(low_scr, step_w_ref, extra_ref[0:1, :])
    x_scr[...] = x_ref[...].astype(F32)
    for r in range(reqs):
        put_lanes(scr, 8 * r, silu(gate_ref[r].astype(F32)))
        kept = plan_ref[r] == own * reqs + r
        for l in range(lanes):
            cols = slice(l * LANES, (l + 1) * LANES)
            h_scr[l, pl.ds(r, states, stride=reqs), :] = jnp.where(
                kept, state_ref[r, :, cols], 0.0
            )
    for l in range(lanes):
        cols = slice(l * LANES, (l + 1) * LANES)
        for t in range(steps):
            gate_scr[t * reqs : (t + 1) * reqs, cols] = scr[l, pl.ds(t, reqs, stride=8), :]
    skip = extra_ref[1:2, :]
    for t in range(steps):
        scan(t, reqs, None, x_scr, gate_scr, sel_scr, step_scr, decay_ref, skip, h_scr, y_scr, 8)
    for r in range(reqs):
        final_conv_ref[:, r : r + 1, :] = u_ref[r].astype(F32)[1:4].reshape(3, 1, channels)
        for l in range(lanes):
            cols = slice(l * LANES, (l + 1) * LANES)
            final_ref[r, :, cols] = h_scr[l, pl.ds(r, states, stride=reqs), :]
            out_ref[r, :, cols] = y_scr[l, 8 * r : 8 * r + steps, :].astype(BF16)
    outward = jnp.transpose(sel_scr[...])[states : 2 * states]
    column = iota(outward.shape, 1)
    for k in range(MIG):
        pick_ref[k : k + 1, :] = jnp.broadcast_to(picks[k], (1, LANES)).astype(F32)
        held_ref[k] = final_ref[picks[k]]
        total = jnp.zeros((1, channels), F32)
        for t in range(steps):
            row = t * reqs + picks[k]
            total = total + step_scr[pl.ds(row, 1), :]
            gate = gate_scr[pl.ds(row, 1), :]
            c = jnp.sum(jnp.where(column == row, outward, 0.0), axis=1, keepdims=True)
            for l in range(lanes):
                cols = slice(l * LANES, (l + 1) * LANES)
                keep = jnp.exp2(total[:, cols] * decay_ref[l, pl.ds(0, states, stride=8), :])
                weight_ref[k * steps + t, :, cols] = keep * c * gate[:, cols]
                base_ref[k * steps + t : k * steps + t + 1, cols] = y_scr[
                    l, pl.ds(8 * picks[k] + t, 1), :
                ]
                if t == steps - 1:
                    keep_ref[k, :, cols] = keep
    pick_ref[MIG:, :] = jnp.zeros((pick_ref.shape[0] - MIG, LANES), F32)
    for s in range(got_ref.shape[0]):
        block = got_ref[s].astype(F32)
        for q in range(PAIR):
            for j in range(3):
                at = TAIL_ROW + 3 * q + j
                conv_scr[j, s * PAIR + q : s * PAIR + q + 1, :] = block[at : at + 1]
    prompt_conv_ref[...] = conv_scr[...].astype(BF16)


def finish_kernel(
    got_ref, base_ref, held_ref, weight_ref, keep_ref, pick_ref, _out, _final, out_ref, final_ref,
    prompt_state_ref, state_scr, moved_scr, out_scr, final_scr, sems,
):
    groups, blocks, four, channels = got_ref.shape
    slots, states, _ = state_scr.shape
    steps = base_ref.shape[0] // MIG
    lanes = channels // LANES
    parts = states // four
    copies = []
    for s in range(groups):
        for q in range(PAIR):
            for p in range(parts):
                state_scr[s * PAIR + q, p * four : (p + 1) * four, :] = got_ref[
                    s, q * parts + p
                ].astype(F32)
        if s % 4 == 3:
            here = pl.ds((s - 3) * PAIR, 4 * PAIR)
            copies.append(
                pltpu.make_async_copy(state_scr.at[here], prompt_state_ref.at[here], sems.at[s])
            )
            copies[-1].start()
    for n in range(states):
        put_lanes(moved_scr, n * MIG, got_ref[n, blocks - 1].astype(F32))
    for k in range(MIG):
        pick = jnp.max(pick_ref[k : k + 1, :]).astype(jnp.int32)
        for l in range(lanes):
            cols = slice(l * LANES, (l + 1) * LANES)
            start = moved_scr[l, pl.ds(k, states, stride=MIG), :]
            final_scr[k, :, cols] = held_ref[k, :, cols] + keep_ref[k, :, cols] * start
            rows = []
            for t in range(steps):
                at = k * steps + t
                more = jnp.sum(weight_ref[at, :, cols] * start, axis=0, keepdims=True)
                rows.append(base_ref[at : at + 1, cols] + more)
            out_scr[k, :, cols] = jnp.concatenate(rows, axis=0).astype(BF16)
        copies.append(
            pltpu.make_async_copy(final_scr.at[k], final_ref.at[pick], sems.at[groups + k])
        )
        copies.append(
            pltpu.make_async_copy(out_scr.at[k], out_ref.at[pick], sems.at[groups + MIG + k])
        )
        copies[-2].start()
        copies[-1].start()
    for copy in copies:
        copy.wait()


def exchange(value, axis):
    return lax.all_to_all(value, axis, split_axis=0, concat_axis=0, tiled=True)


def on_device(
    resident_state,
    resident_conv,
    migrate_from,
    decode_inputs,
    decode_gates,
    prompt_inputs,
    prompt_gates,
    prompt_length,
    prompt_dest,
    conv_weight,
    conv_bias,
    rank_weight,
    select_weight,
    step_weight,
    step_bias,
    decay_log,
    skip_gain,
):
    groups = lax.axis_size("group")
    peers = lax.axis_size("mp")
    reqs, states, channels = resident_state.shape
    prompts, steps, _ = prompt_inputs.shape
    decode_steps = decode_inputs.shape[1]
    tiles = channels // LANES
    rank = rank_weight.shape[1]
    selects = select_weight.shape[1]
    prompt_rows = prompts * steps
    decode_rows = reqs * decode_steps
    bias_row = conv_bias.reshape(1, channels)
    step_bias_row = step_bias.reshape(1, channels)
    skip_row = skip_gain.reshape(1, channels)

    def struct(shape, dtype):
        return jax.ShapeDtypeStruct(shape, dtype)

    def scratch(shape):
        return pltpu.VMEM(shape, F32)

    def cost(flops, size):
        return pl.CostEstimate(flops=flops, bytes_accessed=size, transcendentals=0)

    anywhere = pl.BlockSpec(memory_space=pl.ANY)
    send_shape = (groups, PAIR * states // MIG + 1, MIG, channels)
    dest = prompt_dest.reshape(prompts)
    conv_rows = jnp.transpose(resident_conv, (1, 0, 2))
    select_rows = jnp.transpose(select_weight)

    send_first = pl.pallas_call(
        pack_kernel,
        out_shape=struct((groups, ROWS0, channels), BF16),
        in_specs=[SMEM] * 3 + [VMEM] * 3,
        out_specs=VMEM,
        scratch_shapes=[
            scratch((groups + 1, ROWS0, channels)),
            scratch((3 * reqs, channels)),
            scratch((prompts * (steps + 8), channels)),
        ],
        compiler_params=ALL_VMEM,
        name="pack",
    )(migrate_from, dest, prompt_length, conv_rows, resident_state, prompt_inputs)
    got_first = exchange(send_first, "group")

    prompt_low, prompt_sel, prompt_x, gate_rows, decay, extra, plan, items, empty = pl.pallas_call(
        prompt_kernel,
        out_shape=(
            struct((prompt_rows, rank), F32),
            struct((prompt_rows, selects), F32),
            struct((prompt_rows, channels), BF16),
            struct((prompt_rows, channels), F32),
            struct((tiles, 8 * states, LANES), F32),
            struct((8, channels), F32),
            struct((reqs + 2 * prompts,), jnp.int32),
            struct((2 * reqs + prompts, LANES), F32),
            struct(send_shape, BF16),
        ),
        in_specs=[SMEM] * 3 + [VMEM] * 9,
        out_specs=(VMEM,) * 6 + (SMEM, VMEM, anywhere),
        scratch_shapes=[
            scratch((tiles, prompt_rows, LANES)),
            scratch((prompt_rows, channels)),
            pltpu.VMEM(send_shape, BF16),
            pltpu.SemaphoreType.DMA,
        ],
        compiler_params=PARAMS,
        cost_estimate=cost(10**9, 2 * 10**6),
        name="prompt_features",
    )(
        migrate_from, dest, prompt_length, prompt_inputs, prompt_gates, conv_weight, bias_row,
        rank_weight, select_rows, decay_log, step_bias_row, skip_row,
    )

    pay, decode_x, relay = pl.pallas_call(
        decode_kernel,
        out_shape=(
            struct((peers, 7, 4, LANES), BF16),
            struct((decode_rows, channels), BF16),
            struct((groups, MIG, channels), BF16),
        ),
        in_specs=[VMEM] * 10,
        out_specs=(VMEM,) * 3,
        scratch_shapes=[
            scratch((groups * ROWS0, channels)),
            scratch((peers, 32, LANES)),
            scratch((tiles, reqs * 8, LANES)),
            scratch((decode_rows, channels)),
        ],
        compiler_params=PARAMS,
        name="decode_features",
    )(
        items, got_first, conv_rows, decode_inputs, conv_weight, extra, rank_weight, select_rows,
        prompt_low, prompt_sel,
    )

    parts = exchange(pay, "mp")
    shares = pl.pallas_call(
        sum_kernel,
        out_shape=struct(parts.shape, BF16),
        in_specs=[VMEM],
        out_specs=VMEM,
        compiler_params=PARAMS,
        name="sum_parts",
    )(parts)
    rows = exchange(shares, "mp")

    prefill_out, send_final = pl.pallas_call(
        prefill_kernel,
        out_shape=(
            struct(prompt_inputs.shape, BF16),
            struct(send_shape, BF16),
        ),
        in_specs=[anywhere] + [VMEM] * 8 + [anywhere],
        out_specs=(anywhere,) * 2,
        scratch_shapes=[
            scratch((prompt_rows, rank)),
            scratch((prompt_rows, LANES)),
            scratch((prompt_rows, channels)),
            scratch((prompt_rows, channels)),
            scratch((prompt_rows, channels)),
            scratch((tiles, prompts * states, LANES)),
            scratch((tiles, prompt_rows, LANES)),
            pltpu.VMEM((prompts, states // MIG, MIG, channels), BF16),
            pltpu.VMEM(prompt_inputs.shape, BF16),
            pltpu.SMEM((reqs + 2 * prompts,), jnp.int32),
            pltpu.SemaphoreType.DMA((prompts + 3,)),
        ],
        input_output_aliases={9: 1},
        compiler_params=PARAMS,
        name="prefill_scan",
    )(plan, rows, prompt_x, gate_rows, step_weight, decay, extra, relay, items, empty)
    got_final = exchange(send_final, "group")

    early_out, early_final, base, held, weight, keep, pick, final_conv, prompt_conv = pl.pallas_call(
        decode_scan_kernel,
        out_shape=(
            struct(decode_inputs.shape, BF16),
            struct(resident_state.shape, F32),
            struct((MIG * decode_steps, channels), F32),
            struct((MIG, states, channels), F32),
            struct((MIG * decode_steps, states, channels), F32),
            struct((MIG, states, channels), F32),
            struct((8, LANES), F32),
            struct((3, reqs, channels), F32),
            struct((3, groups * PAIR, channels), BF16),
        ),
        in_specs=[SMEM] + [VMEM] * 9,
        out_specs=(VMEM,) * 9,
        scratch_shapes=[
            scratch((decode_rows, rank)),
            scratch((decode_rows, LANES)),
            scratch((decode_rows, channels)),
            scratch((decode_rows, channels)),
            scratch((decode_rows, channels)),
            scratch((tiles, reqs * 8, LANES)),
            scratch((tiles, reqs * states, LANES)),
            scratch((tiles, reqs * 8, LANES)),
            scratch((3, groups * PAIR, channels)),
        ],
        compiler_params=PARAMS,
        cost_estimate=cost(6 * 10**9, 8 * 10**6),
        name="decode_scan",
    )(
        plan, rows, decode_x, decode_inputs, decode_gates, resident_state, step_weight, decay,
        extra, got_first,
    )

    decode_out, final_state, prompt_state = pl.pallas_call(
        finish_kernel,
        out_shape=(
            struct(decode_inputs.shape, BF16),
            struct(resident_state.shape, F32),
            struct((groups * PAIR, states, channels), F32),
        ),
        in_specs=[VMEM] * 6 + [anywhere] * 2,
        out_specs=(anywhere,) * 3,
        scratch_shapes=[
            scratch((groups * PAIR, states, channels)),
            scratch((tiles, states * MIG, LANES)),
            pltpu.VMEM((MIG, decode_steps, channels), BF16),
            scratch((MIG, states, channels)),
            pltpu.SemaphoreType.DMA((groups + 2 * MIG,)),
        ],
        input_output_aliases={6: 0, 7: 1},
        compiler_params=PARAMS,
        name="finish",
    )(got_final, base, held, weight, keep, pick, early_out, early_final)
    final_conv = jnp.transpose(final_conv, (1, 0, 2)).astype(BF16)
    prompt_conv = jnp.transpose(prompt_conv, (1, 0, 2))
    return (decode_out, final_state, final_conv, prefill_out, prompt_state, prompt_conv)


def solution(mesh):
    whole = P("group", None, "mp")
    return jax.shard_map(
        on_device,
        mesh=mesh,
        in_specs=(
            whole,
            whole,
            P("group"),
            whole,
            whole,
            whole,
            whole,
            P("group"),
            P("group", None),
            P(None, "mp"),
            P("mp"),
            P("mp", None),
            P("mp", None),
            P(None, "mp"),
            P("mp"),
            P(None, "mp"),
            P("mp"),
        ),
        out_specs=(whole,) * 6,
        check_vma=False,
    )
```
